128 devices in a mesh: dp: 8 (over z_hi, y), grp: 16 (over x, z_lo, core).
Axes of the slice: x: 4, y: 4, z: 4 (z_hi: 2, z_lo: 2; z = z_hi * 2 + z_lo), core: 2. Of those that a mesh axis runs over, the one named last changes fastest.
Arguments:
- query_latent: bfloat16 [4, 64, 1536], P(None, 'dp'), may hold values from -6 to 6
- q_up: bfloat16 [1536, 24576], P(('dp', 'grp')), may hold values from -0.15625 to 0.15625
- kv_up: bfloat16 [512, 32768], P(('dp', 'grp')), may hold values from -0.25 to 0.25
- latent_cache: bfloat16 [64, 8192, 576], P('dp', 'grp')
- new_latent: bfloat16 [4, 64, 576], P(None, 'dp'), may hold values from -6 to 6
- lengths: int32 [64], P('dp'), may hold values from 1 to 8192, as said below
Outputs:
- attn_out: bfloat16 [4, 64, 16384], P(None, 'dp', 'grp')
The draws below stay inside these ranges and needn't reach their ends.
Inputs may be any that keep to these rules, and one draw needn't show every extreme that they name: The cache positions 0 to lengths - 1 of a request are live; some request has all 8192 positions live.
All inputs are finite; a program needn't handle non-finite values.
Results may differ from the reference program's by a relative error of at most 0.02.
Values may be sent and summed in bfloat16 or wider, within the bound.
A program may use at most 128 MiB of HBM per device.

```python
import jax
import jax.numpy as jnp
from jax import lax

H = 128
QL = 1536
KVL = 512
NOPE = 128
ROPE = 64
VDIM = 128
STEPS = 4
REQS = 64
CTX = 8192


def draw_lengths(key, part):
    key = jax.random.fold_in(key, 11)
    first, second, third = jax.random.split(key, 3)
    top = CTX.bit_length() - 1
    exponent = jax.random.randint(first, (REQS,), 0, top + 1)
    upper = jnp.left_shift(jnp.ones((REQS,), jnp.int32), exponent) + 1
    drawn = jax.random.randint(second, (REQS,), 1, upper)
    drawn = jnp.minimum(drawn, CTX)
    where_full = jax.random.randint(third, (), 0, REQS)
    return drawn.at[where_full].set(CTX).astype(jnp.int32)


def draw_latent_cache(key, part):
    key = jax.random.fold_in(key, 23)
    first = jax.random.fold_in(key, 0)
    base = jnp.clip(jax.random.normal(first, (REQS, CTX, KVL + ROPE), jnp.float32), -6.0, 6.0)
    return base.astype(jnp.bfloat16)


def block_scale(key, dims, cuts, low, high):
    def one(axis_at, blocks):
        heights = jax.random.uniform(jax.random.fold_in(jax.random.fold_in(key, 6), axis_at), (blocks,), jnp.float32, low / len(cuts), high / len(cuts))
        return jnp.repeat(jnp.exp(heights), dims[axis_at] // blocks).reshape((-1,) + (1,) * (len(dims) - axis_at - 1))

    loudness = one(*cuts[0])
    for cut in cuts[1:]:
        loudness = loudness * one(*cut)
    return loudness


def bell_draw(stream_key, shape, scale, limit, pieces=(), kind=jnp.bfloat16):
    array = jax.random.normal(stream_key, shape, jnp.float32) * scale
    if len(pieces) > 0:
        array = block_scale(stream_key, shape, pieces, -0.22, 0.18) * array
    return jnp.clip(array, min=-limit, max=limit).astype(kind)


def setup_inputs(seed: int = 0) -> dict:
    arg_keys = jax.random.split(jax.random.key(seed), 7)
    query_latent = bell_draw(arg_keys[0], (STEPS, REQS, QL), 1.0, 6.0, ((1, 8),))
    q_up = bell_draw(arg_keys[1], (QL, H * (NOPE + ROPE)), QL ** -0.5, 0.15625, ((0, 128),))
    kv_up = bell_draw(arg_keys[2], (KVL, H * (NOPE + VDIM)), KVL ** -0.5, 0.25, ((0, 128),))
    latent_cache = draw_latent_cache(jax.random.fold_in(arg_keys[6], 71), 0)
    new_latent = bell_draw(arg_keys[4], (STEPS, REQS, KVL + ROPE), 1.0, 6.0, ((1, 8),))
    lengths = draw_lengths(jax.random.fold_in(arg_keys[6], 71), 0)
    return {"query_latent": query_latent, "q_up": q_up, "kv_up": kv_up, "latent_cache": latent_cache, "new_latent": new_latent, "lengths": lengths}


def rotate(pairs_in, position):
    half = pairs_in.shape[-1] // 2
    pairs = pairs_in.reshape(pairs_in.shape[:-1] + (half, 2))
    freq = 10000.0 ** (-(2.0 * jnp.arange(half, dtype=jnp.float32)) / pairs_in.shape[-1])
    angle = position[..., None] * freq
    first = pairs[..., 0]
    second = pairs[..., 1]
    rotated = jnp.stack([first * jnp.cos(angle) - second * jnp.sin(angle), first * jnp.sin(angle) + second * jnp.cos(angle)], -1)
    return rotated.reshape(pairs_in.shape)


def reference(query_latent, q_up, kv_up, latent_cache, new_latent, lengths):
    scale = float(NOPE + ROPE) ** -0.5
    q = jnp.dot(query_latent.reshape(STEPS * REQS, QL), q_up, preferred_element_type=jnp.float32)
    q = q.astype(jnp.bfloat16).reshape(STEPS, REQS, H, NOPE + ROPE)
    blocks = kv_up.reshape(KVL, H, NOPE + VDIM).astype(jnp.float32)
    w_k = blocks[:, :, :NOPE]
    w_v = blocks[:, :, NOPE:]
    q_abs = jnp.einsum('srhd,chd->srhc', q[..., :NOPE].astype(jnp.float32), w_k)
    position = (lengths[None, :] + jnp.arange(STEPS, dtype=jnp.int32)[:, None]).astype(jnp.float32)
    q_rot = rotate(q[..., NOPE:].astype(jnp.float32), position[:, :, None])
    q_cat = jnp.concatenate([q_abs, q_rot], -1).astype(jnp.bfloat16)
    step_ids = jnp.arange(STEPS, dtype=jnp.int32)

    def one_request(items):
        query, cache, fresh, length = items
        keys = jnp.concatenate([cache, fresh], 0).astype(jnp.float32)
        score = jnp.einsum('shc,kc->shk', query.astype(jnp.float32), keys) * scale
        index = jnp.arange(CTX + STEPS, dtype=jnp.int32)
        live = jnp.where(index[None, :] < CTX, index[None, :] < length, (index[None, :] - CTX) <= step_ids[:, None])
        score = jnp.where(live[:, None, :], score, -1e30)
        peak = jnp.max(score, -1)
        prob = jnp.where(live[:, None, :], jnp.exp(score - peak[..., None]), 0.0)
        denom = jnp.sum(prob, -1)
        numer = jnp.einsum('shk,kc->shc', prob.astype(jnp.bfloat16).astype(jnp.float32), keys[:, :KVL])
        return (numer / denom[..., None]).astype(jnp.bfloat16)

    latent_out = lax.map(one_request, (q_cat.transpose(1, 0, 2, 3), latent_cache, new_latent.transpose(1, 0, 2), lengths))
    result = jnp.einsum('rshc,chv->srhv', latent_out.astype(jnp.float32), w_v)
    return result.astype(jnp.bfloat16).reshape(STEPS, REQS, H * VDIM)
```

```python
import jax
import jax.numpy as jnp
from jax import lax
from jax.experimental import pallas as pl
from jax.experimental.pallas import tpu as pltpu
from jax.sharding import PartitionSpec as P

MESH = pl.DeviceIdType.MESH

H = 128
QL = 1536
KVL = 512
NOPE = 128
ROPE = 64
VDIM = 128
STEPS = 4
WIDTH = KVL + ROPE
LOG2E = 1.4426950408889634


def rotate(pairs_in, position):
    half = pairs_in.shape[-1] // 2
    pairs = pairs_in.reshape(pairs_in.shape[:-1] + (half, 2))
    freq = 10000.0 ** (-(2.0 * jnp.arange(half, dtype=jnp.float32)) / pairs_in.shape[-1])
    angle = position[..., None] * freq
    first = pairs[..., 0]
    second = pairs[..., 1]
    rotated = jnp.stack(
        [
            first * jnp.cos(angle) - second * jnp.sin(angle),
            first * jnp.sin(angle) + second * jnp.cos(angle),
        ],
        -1,
    )
    return rotated.reshape(pairs_in.shape)


class Copies:
    def __init__(self, send_sem, recv_sem):
        self.send_sem, self.recv_sem, self.sent = send_sem, recv_sem, []

    def send(self, src, dst, peer):
        k = len(self.sent)
        copy = pltpu.make_async_remote_copy(
            src_ref=src,
            dst_ref=dst,
            send_sem=self.send_sem.at[k],
            recv_sem=self.recv_sem.at[k],
            device_id={"grp": peer},
            device_id_type=MESH,
        )
        copy.start()
        self.sent.append(copy)
        return copy

    def finish(self):
        for copy in self.sent:
            copy.wait_send()


def merge(a, b):
    peak = jnp.maximum(a[0], b[0])
    return peak, a[1] * jnp.exp2(a[0] - peak) + b[1] * jnp.exp2(b[0] - peak)


def attend_kernel(
    own_ref, cache_ref, new_ref, len_ref, wv_ref, out_ref,
    G, K, O, NB, RD, T, RF, RL, RR, RL1, RR1, RZ0, RZ1, U0, V1, M, L, ml_send, ml_recv, SC, SCT, F,
    send_sem, recv_sem, cache_sem,
):
    gi = lax.axis_index("grp")
    x, zl, c = gi // 4, (gi // 2) % 2, gi % 2
    xp, xm, x2 = (x + 1) % 4, (x + 3) % 4, (x + 2) % 4
    zo, co = 1 - zl, 1 - c

    def at(xx, zz, cc):
        return xx * 4 + zz * 2 + cc

    p_xp, p_xm, p_x2 = at(xp, zl, c), at(xm, zl, c), at(x2, zl, c)
    p_z, p_c = at(x, zo, c), at(x, zl, co)

    load = pltpu.make_async_copy(cache_ref, K, cache_sem)
    load.start()
    barrier = pltpu.get_barrier_semaphore()
    for peer in (p_xp, p_xm, p_x2, p_z, p_c):
        pl.semaphore_signal(barrier, inc=1, device_id={"grp": peer}, device_id_type=MESH)
    G[:, pl.ds(gi, 1)] = own_ref[...][:, None]
    pl.semaphore_wait(barrier, 5)

    net = Copies(send_sem, recv_sem)

    def pass_on(first, count, slot, peer):
        block = G.at[pl.ds(first, count), slot]
        return net.send(block, block, peer)

    s_l, s_r, s_z = p_xm, p_xp, p_z
    s_lz, s_rz, s_f, s_fz = at(xm, zo, c), at(xp, zo, c), p_x2, at(x2, zo, c)
    mate = []
    z0 = pass_on(0, 4, gi, p_z)
    l0 = pass_on(0, 4, gi, p_xp)
    r0 = pass_on(0, 4, gi, p_xm)
    l1 = pass_on(4, 4, gi, p_xp)
    r1 = pass_on(4, 4, gi, p_xm)
    mate.append(pass_on(0, 8, gi, p_c))
    z1 = pass_on(4, 4, gi, p_z)
    z0.wait_recv()
    lz0 = pass_on(0, 4, s_z, p_xp)
    rz0 = pass_on(0, 4, s_z, p_xm)
    mate.append(pass_on(0, 4, s_z, p_c))
    l0.wait_recv()
    fa0 = pass_on(0, 2, s_l, p_xp)
    mate.append(pass_on(0, 4, s_l, p_c))
    r0.wait_recv()
    fb0 = pass_on(2, 2, s_r, p_xm)
    mate.append(pass_on(0, 4, s_r, p_c))
    l1.wait_recv()
    fa1 = pass_on(4, 2, s_l, p_xp)
    lz1 = pass_on(4, 4, s_l, p_z)
    mate.append(pass_on(4, 4, s_l, p_c))
    r1.wait_recv()
    fb1 = pass_on(6, 2, s_r, p_xm)
    rz1 = pass_on(4, 4, s_r, p_z)
    mate.append(pass_on(4, 4, s_r, p_c))
    lz0.wait_recv()
    fza0 = pass_on(0, 2, s_lz, p_xp)
    mate.append(pass_on(0, 4, s_lz, p_c))
    rz0.wait_recv()
    fzb0 = pass_on(2, 2, s_rz, p_xm)
    mate.append(pass_on(0, 4, s_rz, p_c))
    fa0.wait_recv()
    mate.append(pass_on(0, 2, s_f, p_c))
    fb0.wait_recv()
    mate.append(pass_on(2, 2, s_f, p_c))
    fa1.wait_recv()
    fza1 = pass_on(4, 2, s_f, p_z)
    mate.append(pass_on(4, 2, s_f, p_c))
    fb1.wait_recv()
    fzb1 = pass_on(6, 2, s_f, p_z)
    mate.append(pass_on(6, 2, s_f, p_c))
    z1.wait_recv()
    mate.append(pass_on(4, 4, s_z, p_c))
    fza0.wait_recv()
    mate.append(pass_on(0, 2, s_fz, p_c))
    fzb0.wait_recv()
    mate.append(pass_on(2, 2, s_fz, p_c))
    lz1.wait_recv()
    mate.append(pass_on(4, 4, s_lz, p_c))
    rz1.wait_recv()
    mate.append(pass_on(4, 4, s_rz, p_c))
    fza1.wait_recv()
    mate.append(pass_on(4, 2, s_fz, p_c))
    fzb1.wait_recv()
    mate.append(pass_on(6, 2, s_fz, p_c))
    for copy in mate:
        copy.wait_recv()
    load.wait()

    to_log2 = float(NOPE + ROPE) ** -0.5 * LOG2E
    lane = lax.broadcasted_iota(jnp.int32, (512, 128), 1)
    key_at = lax.broadcasted_iota(jnp.int32, (1, 512), 1) + gi * 512
    new_live = lax.broadcasted_iota(jnp.int32, (32, 16), 1) <= (
        lax.broadcasted_iota(jnp.int32, (32, 16), 0) % 4
    )
    nt = (((1,), (1,)), ((), ()))
    rows = pl.ds(gi * 32, 32)

    def one_request(r, carry):
        q = G[r].reshape(512, WIDTH)
        k = K[r]
        kn = new_ref[r]
        s = lax.dot_general(q, k, nt, preferred_element_type=jnp.float32) * to_log2
        s = jnp.where(key_at < len_ref[pl.ds(r, 1), :], s, -1e30)
        sn = lax.dot_general(G[r, gi], kn, nt, preferred_element_type=jnp.float32) * to_log2
        sn = jnp.where(new_live, sn, -1e30)
        M[...] = jnp.broadcast_to(jnp.maximum(jnp.max(s, 1, keepdims=True), -1e29), (512, 128))
        M[rows, :] = jnp.maximum(M[rows, :], jnp.max(sn, 1, keepdims=True))
        p = jnp.exp2(s - M[:, 0:1])
        pn = jnp.exp2(sn - M[rows, 0:1])
        L[...] = jnp.broadcast_to(jnp.sum(p, 1, keepdims=True), (512, 128))
        L[rows, :] = L[rows, :] + jnp.sum(pn, 1, keepdims=True)
        O[r] = jnp.dot(p.astype(jnp.bfloat16), k[:, :KVL], preferred_element_type=jnp.float32)
        O[r, rows, :] = O[r, rows, :] + jnp.dot(
            pn.astype(jnp.bfloat16), kn[:, :KVL], preferred_element_type=jnp.float32
        )
        both = jnp.transpose(jnp.where(lane == 0, M[...], L[...]))
        ml_send[0, 0, pl.ds(r, 1), :] = both[0:1]
        ml_send[0, 1, pl.ds(r, 1), :] = both[1:2]
        return carry

    lax.fori_loop(0, 8, one_request, 0)

    mine = (ml_send[0, 0], ml_send[0, 1])
    total = mine
    for stage, peer in ((0, p_c), (1, p_z)):
        copy = net.send(ml_send.at[stage], ml_recv.at[stage], peer)
        copy.wait_recv()
        total = merge(total, (ml_recv[stage, 0], ml_recv[stage, 1]))
        ml_send[stage + 1, 0] = total[0]
        ml_send[stage + 1, 1] = total[1]
    last = [net.send(ml_send.at[2], ml_recv.at[2 + j], p) for j, p in enumerate((p_xp, p_xm, p_x2))]
    for j, copy in enumerate(last):
        copy.wait_recv()
        total = merge(total, (ml_recv[2 + j, 0], ml_recv[2 + j, 1]))
    SC[...] = jnp.zeros_like(SC)
    SC[0:8, :] = jnp.exp2(mine[0] - total[0]) / total[1]
    SCT[...] = jnp.transpose(SC[...])

    halves = []
    for r in range(8):
        part = (O[r] * SCT[:, r : r + 1]).astype(jnp.bfloat16)
        NB[r] = part.reshape(4, 2, 2, 32, KVL)
        if r % 4 == 3:
            span = pl.ds(r - 3, 4)
            halves.append(net.send(NB.at[span, :, :, co], RD.at[span], p_c))

    def add(a, b):
        return (a.astype(jnp.float32) + b.astype(jnp.float32)).astype(jnp.bfloat16)

    for h in range(2):
        halves[h].wait_recv()
        for r in range(4 * h, 4 * h + 4):
            T[r] = add(NB[r, :, :, c], RD[r])
        if h == 0:
            fa = net.send(T.at[0:2, x2], RF.at[0], p_xp)
            fb = net.send(T.at[2:4, x2], RF.at[1], p_xm)
    zr = net.send(T.at[4:8, :, zo], RZ1, p_z)
    fa.wait_recv()
    T[0:2, xp] = add(T[0:2, xp], RF[0])
    to_r = net.send(T.at[0:4, xp], RL, p_xp)
    fb.wait_recv()
    T[2:4, xm] = add(T[2:4, xm], RF[1])
    to_l = net.send(T.at[0:4, xm], RR, p_xm)
    zr.wait_recv()
    for r in range(4):
        V1[r] = add(T[4 + r, :, zl], RZ1[r])
    ga = net.send(V1.at[0:2, x2], RF.at[2, :, 0], p_xp)
    gb = net.send(V1.at[2:4, x2], RF.at[2, :, 1], p_xm)
    to_r.wait_recv()
    to_l.wait_recv()
    U0[...] = (
        T[0:4, x].astype(jnp.float32) + RL[...].astype(jnp.float32) + RR[...].astype(jnp.float32)
    ).astype(jnp.bfloat16)
    zz = net.send(U0.at[:, zo], RZ0, p_z)
    ga.wait_recv()
    V1[0:2, xp] = add(V1[0:2, xp], RF[2, :, 0])
    to_r1 = net.send(V1.at[:, xp], RL1, p_xp)
    gb.wait_recv()
    V1[2:4, xm] = add(V1[2:4, xm], RF[2, :, 1])
    to_l1 = net.send(V1.at[:, xm], RR1, p_xm)
    zz.wait_recv()
    F[0:4] = add(U0[:, zl], RZ0[...])
    to_r1.wait_recv()
    to_l1.wait_recv()
    F[4:8] = (
        V1[:, x].astype(jnp.float32) + RL1[...].astype(jnp.float32) + RR1[...].astype(jnp.float32)
    ).astype(jnp.bfloat16)

    to = lax.broadcasted_iota(jnp.int32, (256, 256), 0)
    was = lax.broadcasted_iota(jnp.int32, (256, 256), 1)
    move = (was == (to % 8) * 32 + to // 8).astype(jnp.bfloat16)
    latent = jnp.dot(
        move, F[...].reshape(256, KVL), preferred_element_type=jnp.float32
    ).astype(jnp.bfloat16)
    for i in range(8):
        out_ref[:, i * VDIM : (i + 1) * VDIM] = jnp.dot(
            latent[i * 32 : (i + 1) * 32], wv_ref[i], preferred_element_type=jnp.float32
        ).astype(jnp.bfloat16)
    net.finish()


def attend(own, cache, new_latent, lengths, w_value):
    fresh = jnp.pad(new_latent.transpose(1, 0, 2), ((0, 0), (0, 16 - STEPS), (0, 0)))
    limit = jnp.broadcast_to(lengths[:, None], (8, 512))
    vmem = pl.BlockSpec(memory_space=pltpu.VMEM)
    bf, f32 = jnp.bfloat16, jnp.float32
    copies = 64
    return pl.pallas_call(
        attend_kernel,
        out_shape=jax.ShapeDtypeStruct((32, 8 * VDIM), bf),
        in_specs=[vmem, pl.BlockSpec(memory_space=pl.ANY), vmem, vmem, vmem],
        out_specs=vmem,
        scratch_shapes=[
            pltpu.VMEM((8, 16, 32, WIDTH), bf),
            pltpu.VMEM((8, 512, WIDTH), bf),
            pltpu.VMEM((8, 512, KVL), f32),
            pltpu.VMEM((8, 4, 2, 2, 32, KVL), bf),
            pltpu.VMEM((8, 4, 2, 32, KVL), bf),
            pltpu.VMEM((8, 4, 2, 32, KVL), bf),
            pltpu.VMEM((3, 2, 2, 32, KVL), bf),
            pltpu.VMEM((4, 2, 32, KVL), bf),
            pltpu.VMEM((4, 2, 32, KVL), bf),
            pltpu.VMEM((4, 32, KVL), bf),
            pltpu.VMEM((4, 32, KVL), bf),
            pltpu.VMEM((4, 32, KVL), bf),
            pltpu.VMEM((4, 4, 32, KVL), bf),
            pltpu.VMEM((4, 2, 32, KVL), bf),
            pltpu.VMEM((4, 4, 32, KVL), bf),
            pltpu.VMEM((512, 128), f32),
            pltpu.VMEM((512, 128), f32),
            pltpu.VMEM((3, 2, 8, 512), f32),
            pltpu.VMEM((5, 2, 8, 512), f32),
            pltpu.VMEM((128, 512), f32),
            pltpu.VMEM((512, 128), f32),
            pltpu.VMEM((8, 32, KVL), bf),
            pltpu.SemaphoreType.DMA((copies,)),
            pltpu.SemaphoreType.DMA((copies,)),
            pltpu.SemaphoreType.DMA,
        ],
        compiler_params=pltpu.CompilerParams(
            collective_id=1, has_side_effects=True, vmem_limit_bytes=56 * 1024 * 1024
        ),
    )(own, cache, fresh, limit, w_value)


def per_device(query_latent, q_up, kv_up, latent_cache, new_latent, lengths):
    groups = lax.axis_size("grp")
    replicas = lax.axis_size("dp")
    heads = H // groups
    q_rows, kv_rows = (
        lax.all_gather(q_up, "dp", axis=0, tiled=True),
        lax.all_gather(kv_up, "dp", axis=0, tiled=True),
    )
    q_mixed, kv_mixed = (
        lax.all_to_all(q_rows, "grp", split_axis=1, concat_axis=0, tiled=True),
        lax.all_to_all(kv_rows, "grp", split_axis=1, concat_axis=0, tiled=True),
    )
    q_owned = (
        q_mixed.reshape(groups, replicas, q_up.shape[0], q_mixed.shape[1])
        .transpose(1, 0, 2, 3)
        .reshape(QL, q_mixed.shape[1])
    )
    kv_owned = (
        kv_mixed.reshape(groups, replicas, kv_up.shape[0], kv_mixed.shape[1])
        .transpose(1, 0, 2, 3)
        .reshape(KVL, kv_mixed.shape[1])
    )
    requests = query_latent.shape[1]
    q = jnp.dot(
        query_latent.reshape(STEPS * requests, QL), q_owned, preferred_element_type=jnp.float32
    )
    q = q.astype(jnp.bfloat16).reshape(STEPS, requests, heads, NOPE + ROPE)
    blocks = kv_owned.reshape(KVL, heads, NOPE + VDIM)
    w_key = blocks[:, :, :NOPE]
    w_value = blocks[:, :, NOPE:]
    q_abs = jnp.einsum("srhd,chd->srhc", q[..., :NOPE], w_key, preferred_element_type=jnp.float32)
    step_ids = lax.broadcasted_iota(jnp.int32, (STEPS, 1), 0)
    position = (lengths[None, :] + step_ids).astype(jnp.float32)
    q_rot = rotate(q[..., NOPE:].astype(jnp.float32), position[:, :, None])
    q_cat = jnp.concatenate([q_abs, q_rot], -1).astype(jnp.bfloat16)
    own = q_cat.transpose(1, 2, 0, 3).reshape(requests, heads * STEPS, WIDTH)
    out = attend(own, latent_cache, new_latent, lengths, w_value.transpose(1, 0, 2))
    return out.reshape(STEPS, requests, heads * VDIM)


def solution(mesh):
    return jax.shard_map(
        per_device,
        mesh=mesh,
        in_specs=(
            P(None, "dp", None),
            P(("dp", "grp"), None),
            P(("dp", "grp"), None),
            P("dp", "grp", None),
            P(None, "dp", None),
            P("dp"),
        ),
        out_specs=P(None, "dp", "grp"),
        check_vma=False,
    )
```

```python
import jax
import jax.numpy as jnp
import numpy as np
from jax import lax
from jax.experimental import pallas as pl
from jax.experimental.pallas import tpu as pltpu
from jax.sharding import PartitionSpec as P

MESH = pl.DeviceIdType.MESH

H = 128
QL = 1536
KVL = 512
NOPE = 128
ROPE = 64
VDIM = 128
STEPS = 4
WIDTH = KVL + ROPE
WIDE = KVL + 128
LOG2E = 1.4426950408889634


class Copies:
    def __init__(self, send_sem, recv_sem):
        self.send_sem, self.recv_sem, self.sent = send_sem, recv_sem, []

    def send(self, src, dst, peer, axis="grp"):
        k = len(self.sent)
        copy = pltpu.make_async_remote_copy(
            src_ref=src,
            dst_ref=dst,
            send_sem=self.send_sem.at[k],
            recv_sem=self.recv_sem.at[k],
            device_id={axis: peer},
            device_id_type=MESH,
        )
        copy.start()
        self.sent.append(copy)
        return copy

    def finish(self):
        for copy in self.sent:
            copy.wait_send()


def merge(a, b):
    peak = jnp.maximum(a[0], b[0])
    return peak, a[1] * jnp.exp2(a[0] - peak) + b[1] * jnp.exp2(b[0] - peak)


def kernel(
    ql_ref, q_ref, kv_ref, cache_ref, new_ref, len_ref, cos_ref, sin_ref, move_ref, out_ref,
    X, LAND, QLS, W, KC, E, QR, WV,
    G, K, O, NB, RD, T, RF, RL, RR, RL1, RR1, RZ0, RZ1, U0, V1, M, L, ml_send, ml_recv, SC, SCT, F,
    send_sem, recv_sem, cache_sem, all_send, all_recv,
):
    di, gi = lax.axis_index("dp"), lax.axis_index("grp")
    me = di * 16 + gi
    x, zl, c = gi // 4, (gi // 2) % 2, gi % 2
    xp, xm, x2 = (x + 1) % 4, (x + 3) % 4, (x + 2) % 4
    zo, co = 1 - zl, 1 - c

    def at(xx, zz, cc):
        return xx * 4 + zz * 2 + cc

    p_xp, p_xm, p_x2 = at(xp, zl, c), at(xm, zl, c), at(x2, zl, c)
    p_z, p_c = at(x, zo, c), at(x, zl, co)

    load = pltpu.make_async_copy(cache_ref, K, cache_sem)
    load.start()
    barrier = pltpu.get_barrier_semaphore()

    def there(j):
        d = (me + 37 * j) % 128
        return d // 16, d % 16

    def greet(j, carry):
        dd, gg = there(j)
        pl.semaphore_signal(
            barrier, inc=1, device_id={"dp": dd, "grp": gg}, device_id_type=MESH
        )
        return carry

    lax.fori_loop(1, 128, greet, 0)

    def pack(p, carry):
        def tile(ref, n):
            return ref[:, pl.ds(pl.multiple_of(n * 128, 128), 128)]

        first, middle, last = tile(q_ref, 3 * p), tile(q_ref, 3 * p + 1), tile(q_ref, 3 * p + 2)
        X[2 * p, 0:16] = first + tile(kv_ref, 4 * p)
        X[2 * p, 16:32] = middle + tile(kv_ref, 4 * p + 1)
        X[2 * p + 1, 0:16] = middle + tile(kv_ref, 4 * p + 2)
        X[2 * p + 1, 16:32] = last + tile(kv_ref, 4 * p + 3)
        return carry

    lax.fori_loop(0, 64, pack, 0)
    QLS[di, c] = ql_ref[c]
    LAND[me] = X[8 * gi + di]
    pl.semaphore_wait(barrier, 127)

    net = Copies(send_sem, recv_sem)
    latents = [net.send(QLS.at[di, c], QLS.at[di, c], (di + j) % 8, "dp") for j in range(1, 8)]

    def deal(j, carry):
        dd, gg = there(j)
        pltpu.make_async_remote_copy(
            src_ref=X.at[8 * gg + dd],
            dst_ref=LAND.at[me],
            send_sem=all_send,
            recv_sem=all_recv,
            device_id={"dp": dd, "grp": gg},
            device_id_type=MESH,
        ).start()
        return carry

    lax.fori_loop(1, 128, deal, 0)
    for copy in latents:
        copy.wait_recv()
    net.send(QLS.at[:, c], QLS.at[:, c], p_c).wait_recv()
    pltpu.make_async_copy(LAND.at[0:127], LAND.at[0:127], all_recv).wait()

    bf, f32 = jnp.bfloat16, jnp.float32
    for b in range(16):
        block = jnp.dot(
            move_ref[0], LAND[8 * b : 8 * b + 8].reshape(256, 128), preferred_element_type=f32
        ).astype(bf)
        W[0, 96 * b : 96 * b + 96] = block[0:96]
        W[1, 96 * b : 96 * b + 96] = block[96:192]
        KC[32 * b : 32 * b + 32] = block[192:224]
        WV[di, 32 * b : 32 * b + 32] = block[224:256]
    latent_in = QLS[...].reshape(256, QL)
    qa = jnp.dot(latent_in, W[0], preferred_element_type=f32)
    qb = jnp.dot(latent_in, W[1], preferred_element_type=f32)
    ra, rb = pltpu.roll(qa, 64, 1), pltpu.roll(qb, 64, 1)
    lane = lax.broadcasted_iota(jnp.int32, (256, 128), 1)
    odd = di % 2 == 1
    plain = jnp.where(odd, jnp.where(lane < 64, ra, rb), qa).astype(bf)
    rotary = jnp.where(lane < 64, jnp.where(odd, rb, qb), 0.0).astype(bf)
    nt = (((1,), (1,)), ((), ()))
    absorbed = lax.dot_general(plain, KC[...], nt, preferred_element_type=f32).astype(bf)
    E[:, :, 0:KVL] = absorbed.reshape(8, 32, KVL)
    E[:, :, KVL:WIDE] = rotary.reshape(8, 32, 128)
    heads = []
    for j in range(1, 8):
        dd = (di + j) % 8
        heads.append(net.send(E.at[dd], QR.at[di], dd, "dp"))
    QR[di] = E[di]
    for copy in heads:
        copy.wait_recv()
    values = [net.send(WV.at[di], WV.at[di], (di + j) % 8, "dp") for j in range(1, 8)]

    turned = jnp.dot(move_ref[1], QR[...].reshape(256, WIDE), preferred_element_type=f32)
    rotary = turned[:, KVL:]
    other = jnp.where(lane % 2 == 0, pltpu.roll(rotary, 127, 1), pltpu.roll(rotary, 1, 1))
    rotary = rotary * cos_ref[...] + other * sin_ref[...]
    G[:, pl.ds(gi, 1), :, 0:KVL] = turned[:, :KVL].astype(bf).reshape(8, 1, 32, KVL)
    G[:, pl.ds(gi, 1), :, KVL:WIDTH] = rotary[:, :ROPE].astype(bf).reshape(8, 1, 32, ROPE)

    def pass_on(first, count, slot, peer):
        block = G.at[pl.ds(first, count), slot]
        return net.send(block, block, peer)

    s_l, s_r, s_z = p_xm, p_xp, p_z
    s_lz, s_rz, s_f, s_fz = at(xm, zo, c), at(xp, zo, c), p_x2, at(x2, zo, c)
    mate = []
    z0 = pass_on(0, 4, gi, p_z)
    l0 = pass_on(0, 4, gi, p_xp)
    r0 = pass_on(0, 4, gi, p_xm)
    l1 = pass_on(4, 4, gi, p_xp)
    r1 = pass_on(4, 4, gi, p_xm)
    mate.append(pass_on(0, 8, gi, p_c))
    z1 = pass_on(4, 4, gi, p_z)
    z0.wait_recv()
    lz0 = pass_on(0, 4, s_z, p_xp)
    rz0 = pass_on(0, 4, s_z, p_xm)
    mate.append(pass_on(0, 4, s_z, p_c))
    l0.wait_recv()
    fa0 = pass_on(0, 2, s_l, p_xp)
    mate.append(pass_on(0, 4, s_l, p_c))
    r0.wait_recv()
    fb0 = pass_on(2, 2, s_r, p_xm)
    mate.append(pass_on(0, 4, s_r, p_c))
    l1.wait_recv()
    fa1 = pass_on(4, 2, s_l, p_xp)
    lz1 = pass_on(4, 4, s_l, p_z)
    mate.append(pass_on(4, 4, s_l, p_c))
    r1.wait_recv()
    fb1 = pass_on(6, 2, s_r, p_xm)
    rz1 = pass_on(4, 4, s_r, p_z)
    mate.append(pass_on(4, 4, s_r, p_c))
    lz0.wait_recv()
    fza0 = pass_on(0, 2, s_lz, p_xp)
    mate.append(pass_on(0, 4, s_lz, p_c))
    rz0.wait_recv()
    fzb0 = pass_on(2, 2, s_rz, p_xm)
    mate.append(pass_on(0, 4, s_rz, p_c))
    fa0.wait_recv()
    mate.append(pass_on(0, 2, s_f, p_c))
    fb0.wait_recv()
    mate.append(pass_on(2, 2, s_f, p_c))
    fa1.wait_recv()
    fza1 = pass_on(4, 2, s_f, p_z)
    mate.append(pass_on(4, 2, s_f, p_c))
    fb1.wait_recv()
    fzb1 = pass_on(6, 2, s_f, p_z)
    mate.append(pass_on(6, 2, s_f, p_c))
    z1.wait_recv()
    mate.append(pass_on(4, 4, s_z, p_c))
    fza0.wait_recv()
    mate.append(pass_on(0, 2, s_fz, p_c))
    fzb0.wait_recv()
    mate.append(pass_on(2, 2, s_fz, p_c))
    lz1.wait_recv()
    mate.append(pass_on(4, 4, s_lz, p_c))
    rz1.wait_recv()
    mate.append(pass_on(4, 4, s_rz, p_c))
    fza1.wait_recv()
    mate.append(pass_on(4, 2, s_fz, p_c))
    fzb1.wait_recv()
    mate.append(pass_on(6, 2, s_fz, p_c))
    for copy in mate:
        copy.wait_recv()
    load.wait()

    to_log2 = float(NOPE + ROPE) ** -0.5 * LOG2E
    lane = lax.broadcasted_iota(jnp.int32, (512, 128), 1)
    key_at = lax.broadcasted_iota(jnp.int32, (1, 512), 1) + gi * 512
    new_live = lax.broadcasted_iota(jnp.int32, (32, 16), 1) <= (
        lax.broadcasted_iota(jnp.int32, (32, 16), 0) % 4
    )
    rows = pl.ds(gi * 32, 32)

    def one_request(r, carry):
        q = G[r].reshape(512, WIDTH)
        k = K[r]
        kn = new_ref[r]
        s = jnp.dot(q, k, preferred_element_type=jnp.float32) * to_log2
        s = jnp.where(key_at < len_ref[pl.ds(r, 1), :], s, -1e30)
        sn = lax.dot_general(G[r, gi], kn, nt, preferred_element_type=jnp.float32) * to_log2
        sn = jnp.where(new_live, sn, -1e30)
        M[...] = jnp.broadcast_to(jnp.maximum(jnp.max(s, 1, keepdims=True), -1e29), (512, 128))
        M[rows, :] = jnp.maximum(M[rows, :], jnp.max(sn, 1, keepdims=True))
        p = jnp.exp2(s - M[:, 0:1])
        pn = jnp.exp2(sn - M[rows, 0:1])
        L[...] = jnp.broadcast_to(jnp.sum(p, 1, keepdims=True), (512, 128))
        L[rows, :] = L[rows, :] + jnp.sum(pn, 1, keepdims=True)
        O[r] = lax.dot_general(
            p.astype(jnp.bfloat16), k[:KVL], nt, preferred_element_type=jnp.float32
        )
        O[r, rows, :] = O[r, rows, :] + jnp.dot(
            pn.astype(jnp.bfloat16), kn[:, :KVL], preferred_element_type=jnp.float32
        )
        both = jnp.transpose(jnp.where(lane == 0, M[...], L[...]))
        ml_send[0, 0, pl.ds(r, 1), :] = both[0:1]
        ml_send[0, 1, pl.ds(r, 1), :] = both[1:2]
        return carry

    lax.fori_loop(0, 8, one_request, 0)

    mine = (ml_send[0, 0], ml_send[0, 1])
    total = mine
    for stage, peer in ((0, p_c), (1, p_z)):
        copy = net.send(ml_send.at[stage], ml_recv.at[stage], peer)
        copy.wait_recv()
        total = merge(total, (ml_recv[stage, 0], ml_recv[stage, 1]))
        ml_send[stage + 1, 0] = total[0]
        ml_send[stage + 1, 1] = total[1]
    last = [net.send(ml_send.at[2], ml_recv.at[2 + j], p) for j, p in enumerate((p_xp, p_xm, p_x2))]
    for j, copy in enumerate(last):
        copy.wait_recv()
        total = merge(total, (ml_recv[2 + j, 0], ml_recv[2 + j, 1]))
    SC[...] = jnp.zeros_like(SC)
    SC[0:8, :] = jnp.exp2(mine[0] - total[0]) / total[1]
    SCT[...] = jnp.transpose(SC[...])

    halves = []
    for r in range(8):
        part = (O[r] * SCT[:, r : r + 1]).astype(jnp.bfloat16)
        NB[r] = part.reshape(4, 2, 2, 32, KVL)
        if r % 4 == 3:
            span = pl.ds(r - 3, 4)
            halves.append(net.send(NB.at[span, :, :, co], RD.at[span], p_c))

    def add(a, b):
        return (a.astype(jnp.float32) + b.astype(jnp.float32)).astype(jnp.bfloat16)

    for h in range(2):
        halves[h].wait_recv()
        for r in range(4 * h, 4 * h + 4):
            T[r] = add(NB[r, :, :, c], RD[r])
        if h == 0:
            fa = net.send(T.at[0:2, x2], RF.at[0], p_xp)
            fb = net.send(T.at[2:4, x2], RF.at[1], p_xm)
    zr = net.send(T.at[4:8, :, zo], RZ1, p_z)
    fa.wait_recv()
    T[0:2, xp] = add(T[0:2, xp], RF[0])
    to_r = net.send(T.at[0:4, xp], RL, p_xp)
    fb.wait_recv()
    T[2:4, xm] = add(T[2:4, xm], RF[1])
    to_l = net.send(T.at[0:4, xm], RR, p_xm)
    zr.wait_recv()
    for r in range(4):
        V1[r] = add(T[4 + r, :, zl], RZ1[r])
    ga = net.send(V1.at[0:2, x2], RF.at[2, :, 0], p_xp)
    gb = net.send(V1.at[2:4, x2], RF.at[2, :, 1], p_xm)
    to_r.wait_recv()
    to_l.wait_recv()
    U0[...] = (
        T[0:4, x].astype(jnp.float32) + RL[...].astype(jnp.float32) + RR[...].astype(jnp.float32)
    ).astype(jnp.bfloat16)
    zz = net.send(U0.at[:, zo], RZ0, p_z)
    ga.wait_recv()
    V1[0:2, xp] = add(V1[0:2, xp], RF[2, :, 0])
    to_r1 = net.send(V1.at[:, xp], RL1, p_xp)
    gb.wait_recv()
    V1[2:4, xm] = add(V1[2:4, xm], RF[2, :, 1])
    to_l1 = net.send(V1.at[:, xm], RR1, p_xm)
    zz.wait_recv()
    F[0:4] = add(U0[:, zl], RZ0[...])
    to_r1.wait_recv()
    to_l1.wait_recv()
    F[4:8] = (
        V1[:, x].astype(jnp.float32) + RL1[...].astype(jnp.float32) + RR1[...].astype(jnp.float32)
    ).astype(jnp.bfloat16)

    latent = jnp.dot(
        move_ref[2], F[...].reshape(256, KVL), preferred_element_type=jnp.float32
    ).astype(jnp.bfloat16)
    for copy in values:
        copy.wait_recv()
    for i in range(8):
        out_ref[:, i * VDIM : (i + 1) * VDIM] = jnp.dot(
            latent[i * 32 : (i + 1) * 32], WV[i], preferred_element_type=jnp.float32
        ).astype(jnp.bfloat16)
    net.finish()
    pltpu.make_async_copy(X.at[0:127], X.at[0:127], all_send).wait()


def moves():
    sources = np.arange(256).reshape(8, 32)
    deal = np.concatenate(
        [sources[:, a:b].reshape(-1) for a, b in ((0, 12), (16, 28), (12, 16), (28, 32))]
    )
    turn = np.arange(256).reshape(8, 4, 8).transpose(2, 0, 1).reshape(-1)
    back = np.arange(256).reshape(8, 8, 4).transpose(1, 2, 0).reshape(-1)
    return np.stack([np.eye(256)[order] for order in (deal, turn, back)])


def rotation(lengths):
    freq = 10000.0 ** (-(2.0 * jnp.arange(ROPE // 2, dtype=jnp.float32)) / ROPE)
    position = (lengths[:, None] + jnp.arange(STEPS, dtype=jnp.int32)).astype(jnp.float32)
    angle = position[..., None] * jnp.repeat(freq, 2)
    sign = jnp.where(jnp.arange(ROPE) % 2 == 0, -1.0, 1.0)

    def rows(table):
        table = jnp.pad(table, ((0, 0), (0, 0), (0, 128 - ROPE)))
        return jnp.broadcast_to(table[:, None], (8, 8, STEPS, 128)).reshape(256, 128)

    return rows(jnp.cos(angle)), rows(jnp.sin(angle) * sign)


def per_device(query_latent, q_up, kv_up, latent_cache, new_latent, lengths):
    bf, f32 = jnp.bfloat16, jnp.float32
    latent_in = query_latent.reshape(2, 16, QL)
    q_rows = jnp.pad(q_up, ((0, 4), (0, 0)))
    kv_rows = jnp.pad(kv_up, ((12, 0), (0, 0)))
    fresh = jnp.pad(new_latent.transpose(1, 0, 2), ((0, 0), (0, 16 - STEPS), (0, 0)))
    limit = jnp.broadcast_to(lengths[:, None], (8, 512))
    cosines, sines = rotation(lengths)
    vmem = pl.BlockSpec(memory_space=pltpu.VMEM)
    copies = 96
    out = pl.pallas_call(
        kernel,
        out_shape=jax.ShapeDtypeStruct((32, 8 * VDIM), bf),
        in_specs=[vmem] * 3 + [pl.BlockSpec(memory_space=pl.ANY)] + [vmem] * 5,
        out_specs=vmem,
        scratch_shapes=[
            pltpu.VMEM((128, 32, 128), bf),
            pltpu.VMEM((128, 32, 128), bf),
            pltpu.VMEM((8, 2, 16, QL), bf),
            pltpu.VMEM((2, QL, 128), bf),
            pltpu.VMEM((KVL, NOPE), bf),
            pltpu.VMEM((8, 32, WIDE), bf),
            pltpu.VMEM((8, 32, WIDE), bf),
            pltpu.VMEM((8, KVL, VDIM), bf),
            pltpu.VMEM((8, 16, 32, WIDTH), bf),
            pltpu.VMEM((8, WIDTH, 512), bf),
            pltpu.VMEM((8, 512, KVL), f32),
            pltpu.VMEM((8, 4, 2, 2, 32, KVL), bf),
            pltpu.VMEM((8, 4, 2, 32, KVL), bf),
            pltpu.VMEM((8, 4, 2, 32, KVL), bf),
            pltpu.VMEM((3, 2, 2, 32, KVL), bf),
            pltpu.VMEM((4, 2, 32, KVL), bf),
            pltpu.VMEM((4, 2, 32, KVL), bf),
            pltpu.VMEM((4, 32, KVL), bf),
            pltpu.VMEM((4, 32, KVL), bf),
            pltpu.VMEM((4, 32, KVL), bf),
            pltpu.VMEM((4, 4, 32, KVL), bf),
            pltpu.VMEM((4, 2, 32, KVL), bf),
            pltpu.VMEM((4, 4, 32, KVL), bf),
            pltpu.VMEM((512, 128), f32),
            pltpu.VMEM((512, 128), f32),
            pltpu.VMEM((3, 2, 8, 512), f32),
            pltpu.VMEM((5, 2, 8, 512), f32),
            pltpu.VMEM((128, 512), f32),
            pltpu.VMEM((512, 128), f32),
            pltpu.VMEM((8, 32, KVL), bf),
            pltpu.SemaphoreType.DMA((copies,)),
            pltpu.SemaphoreType.DMA((copies,)),
            pltpu.SemaphoreType.DMA,
            pltpu.SemaphoreType.DMA,
            pltpu.SemaphoreType.DMA,
        ],
        compiler_params=pltpu.CompilerParams(
            collective_id=1, has_side_effects=True, vmem_limit_bytes=60 * 1024 * 1024
        ),
    )(
        latent_in, q_rows, kv_rows, latent_cache.transpose(0, 2, 1), fresh, limit, cosines, sines,
        jnp.asarray(moves(), bf),
    )
    return out.reshape(STEPS, 8, 8 * VDIM)


def solution(mesh):
    return jax.shard_map(
        per_device,
        mesh=mesh,
        in_specs=(
            P(None, "dp", None),
            P(("dp", "grp"), None),
            P(("dp", "grp"), None),
            P("dp", "grp", None),
            P(None, "dp", None),
            P("dp"),
        ),
        out_specs=P(None, "dp", "grp"),
        check_vma=False,
    )
```

```python
import jax
import jax.numpy as jnp
import numpy as np
from jax import lax
from jax.experimental import pallas as pl
from jax.experimental.pallas import tpu as pltpu
from jax.sharding import PartitionSpec as P

MESH = pl.DeviceIdType.MESH

H = 128
QL = 1536
KVL = 512
NOPE = 128
ROPE = 64
VDIM = 128
STEPS = 4
WIDTH = KVL + ROPE
WIDE = KVL + 128
LOG2E = 1.4426950408889634


class Copies:
    def __init__(self, send_sem, recv_sem):
        self.send_sem, self.recv_sem, self.sent = send_sem, recv_sem, []

    def send(self, src, dst, peer, axis="grp"):
        k = len(self.sent)
        copy = pltpu.make_async_remote_copy(
            src_ref=src,
            dst_ref=dst,
            send_sem=self.send_sem.at[k],
            recv_sem=self.recv_sem.at[k],
            device_id={axis: peer},
            device_id_type=MESH,
        )
        copy.start()
        self.sent.append(copy)
        return copy

    def finish(self):
        for copy in self.sent:
            copy.wait_send()


def merge(a, b):
    peak = jnp.maximum(a[0], b[0])
    return peak, a[1] * jnp.exp2(a[0] - peak) + b[1] * jnp.exp2(b[0] - peak)


def kernel(
    len_ref, freq_ref, ql_ref, q_ref, kv_ref, cache_ref, new_ref, out_ref,
    QIN, KVIN, NEW, MOVE, SN, X, LAND, QLS, W, KC, E, QR, WV,
    G, K, O, NB, RD, T, RF, RL, RR, RL1, RR1, RZ0, RZ1, U0, V1, M, L, ml_send, ml_recv, SC, SCT, F,
    send_sem, recv_sem, load_sem, all_send, all_recv,
):
    di, gi = lax.axis_index("dp"), lax.axis_index("grp")
    me = di * 16 + gi
    x, zl, c = gi // 4, (gi // 2) % 2, gi % 2
    xp, xm, x2 = (x + 1) % 4, (x + 3) % 4, (x + 2) % 4
    zo, co = 1 - zl, 1 - c

    def at(xx, zz, cc):
        return xx * 4 + zz * 2 + cc

    p_xp, p_xm, p_x2 = at(xp, zl, c), at(xm, zl, c), at(x2, zl, c)
    p_z, p_c = at(x, zo, c), at(x, zl, co)

    loads = [
        pltpu.make_async_copy(src, dst, load_sem.at[n])
        for n, (src, dst) in enumerate(
            ((q_ref, QIN), (kv_ref, KVIN), (ql_ref.at[c], QLS.at[di, c]), (new_ref, NEW), (cache_ref, K))
        )
    ]
    barrier = pltpu.get_barrier_semaphore()

    def there(j):
        d = (me + 37 * j) % 128
        return d // 16, d % 16

    def greet(j, carry):
        dd, gg = there(j)
        pl.semaphore_signal(
            barrier, inc=1, device_id={"dp": dd, "grp": gg}, device_id_type=MESH
        )
        return carry

    lax.fori_loop(1, 128, greet, 0)

    for load in loads:
        load.start()
    bf, f32 = jnp.bfloat16, jnp.float32
    nt = (((1,), (1,)), ((), ()))

    to = lax.broadcasted_iota(jnp.int32, (256, 256), 0)
    was = lax.broadcasted_iota(jnp.int32, (256, 256), 1)
    within = jnp.where(to < 96, to, to - 96)
    twelve = jnp.where(to < 96, to, to - 80)
    for n in range(1, 8):
        twelve = twelve + jnp.where(within >= 12 * n, 20, 0)
    four = 32 * ((to % 32) // 4) + to % 4 + jnp.where(to < 224, 12, 28)
    MOVE[0] = (was == jnp.where(to < 192, twelve, four)).astype(f32).astype(bf)
    MOVE[1] = (was == ((to // 4) % 8) * 32 + (to % 4) * 8 + to // 32).astype(f32).astype(bf)
    MOVE[2] = (was == (to % 8) * 32 + to // 8).astype(f32).astype(bf)

    loads[0].wait()
    loads[1].wait()

    def pack(p, carry):
        def tiles(upper, lower):
            a = QIN[:, pl.ds(pl.multiple_of(upper * 128, 128), 128)]
            b = KVIN[:, pl.ds(pl.multiple_of(lower * 128, 128), 128)]
            return jnp.concatenate([a, b], 0)

        X[2 * p, 0:16] = tiles(3 * p, 4 * p)
        X[2 * p, 16:32] = tiles(3 * p + 1, 4 * p + 1)
        X[2 * p + 1, 0:16] = tiles(3 * p + 1, 4 * p + 2)
        X[2 * p + 1, 16:32] = tiles(3 * p + 2, 4 * p + 3)
        return carry

    lax.fori_loop(0, 64, pack, 0)
    LAND[me] = X[8 * gi + di]
    loads[2].wait()
    pl.semaphore_wait(barrier, 127)

    net = Copies(send_sem, recv_sem)
    latents = [net.send(QLS.at[di, c], QLS.at[di, c], (di + j) % 8, "dp") for j in range(1, 8)]

    def deal(j, carry):
        dd, gg = there(j)
        pltpu.make_async_remote_copy(
            src_ref=X.at[8 * gg + dd],
            dst_ref=LAND.at[me],
            send_sem=all_send,
            recv_sem=all_recv,
            device_id={"dp": dd, "grp": gg},
            device_id_type=MESH,
        ).start()
        return carry

    lax.fori_loop(1, 128, deal, 0)

    row = lax.broadcasted_iota(jnp.int32, (32, 128), 0)
    lane32 = lax.broadcasted_iota(jnp.int32, (32, 128), 1)
    position = row // 8
    for r in range(8):
        position = position + jnp.where(row % 8 == r, len_ref[r], 0)
    angle = position.astype(f32) * freq_ref[...]
    cosine = jnp.cos(angle)
    sine = jnp.where(lane32 % 2 == 0, -1.0, 1.0) * jnp.sin(angle)
    for copy in latents:
        copy.wait_recv()
    net.send(QLS.at[:, c], QLS.at[:, c], p_c).wait_recv()
    pltpu.make_async_copy(LAND.at[0:127], LAND.at[0:127], all_recv).wait()

    for b in range(16):
        block = jnp.dot(
            MOVE[0], LAND[8 * b : 8 * b + 8].reshape(256, 128), preferred_element_type=f32
        ).astype(bf)
        W[0, 96 * b : 96 * b + 96] = block[0:96]
        W[1, 96 * b : 96 * b + 96] = block[96:192]
        KC[32 * b : 32 * b + 32] = block[192:224]
        WV[di, 32 * b : 32 * b + 32] = block[224:256]
    latent_in = QLS[...].reshape(256, QL)
    qa = jnp.dot(latent_in, W[0], preferred_element_type=f32)
    qb = jnp.dot(latent_in, W[1], preferred_element_type=f32)
    ra, rb = pltpu.roll(qa, 64, 1), pltpu.roll(qb, 64, 1)
    lane = lax.broadcasted_iota(jnp.int32, (256, 128), 1)
    odd = di % 2 == 1
    plain = jnp.where(odd, jnp.where(lane < 64, ra, rb), qa).astype(bf)
    rotary = jnp.where(lane < 64, jnp.where(odd, rb, qb), 0.0).astype(bf)
    absorbed = lax.dot_general(plain, KC[...], nt, preferred_element_type=f32).astype(bf)
    E[:, :, 0:KVL] = absorbed.reshape(8, 32, KVL)
    E[:, :, KVL:WIDE] = rotary.reshape(8, 32, 128)
    heads = []
    for j in range(1, 8):
        dd = (di + j) % 8
        heads.append(net.send(E.at[dd], QR.at[di], dd, "dp"))
    QR[di] = E[di]
    for copy in heads:
        copy.wait_recv()
    values = [net.send(WV.at[di], WV.at[di], (di + j) % 8, "dp") for j in range(1, 8)]

    rotary = QR[:, :, KVL:WIDE].reshape(256, 128).astype(f32)
    other = jnp.where(lane % 2 == 0, pltpu.roll(rotary, 127, 1), pltpu.roll(rotary, 1, 1))
    rotary = (
        rotary.reshape(8, 32, 128) * cosine[None] + other.reshape(8, 32, 128) * sine[None]
    ).reshape(256, 128)
    absorbed = jnp.dot(MOVE[1], QR[:, :, 0:KVL].reshape(256, KVL), preferred_element_type=f32)
    rotary = jnp.dot(MOVE[1], rotary.astype(bf), preferred_element_type=f32)
    G[:, pl.ds(gi, 1), :, 0:KVL] = absorbed.astype(bf).reshape(8, 1, 32, KVL)
    G[:, pl.ds(gi, 1), :, KVL:WIDTH] = rotary[:, :ROPE].astype(bf).reshape(8, 1, 32, ROPE)

    def pass_on(first, count, slot, peer):
        block = G.at[pl.ds(first, count), slot]
        return net.send(block, block, peer)

    s_l, s_r, s_z = p_xm, p_xp, p_z
    s_lz, s_rz, s_f, s_fz = at(xm, zo, c), at(xp, zo, c), p_x2, at(x2, zo, c)
    mate = []
    z0 = pass_on(0, 4, gi, p_z)
    l0 = pass_on(0, 4, gi, p_xp)
    r0 = pass_on(0, 4, gi, p_xm)
    l1 = pass_on(4, 4, gi, p_xp)
    r1 = pass_on(4, 4, gi, p_xm)
    mate.append(pass_on(0, 8, gi, p_c))
    z1 = pass_on(4, 4, gi, p_z)
    z0.wait_recv()
    lz0 = pass_on(0, 4, s_z, p_xp)
    rz0 = pass_on(0, 4, s_z, p_xm)
    mate.append(pass_on(0, 4, s_z, p_c))
    l0.wait_recv()
    fa0 = pass_on(0, 2, s_l, p_xp)
    mate.append(pass_on(0, 4, s_l, p_c))
    r0.wait_recv()
    fb0 = pass_on(2, 2, s_r, p_xm)
    mate.append(pass_on(0, 4, s_r, p_c))
    l1.wait_recv()
    fa1 = pass_on(4, 2, s_l, p_xp)
    lz1 = pass_on(4, 4, s_l, p_z)
    mate.append(pass_on(4, 4, s_l, p_c))
    r1.wait_recv()
    fb1 = pass_on(6, 2, s_r, p_xm)
    rz1 = pass_on(4, 4, s_r, p_z)
    mate.append(pass_on(4, 4, s_r, p_c))
    lz0.wait_recv()
    fza0 = pass_on(0, 2, s_lz, p_xp)
    mate.append(pass_on(0, 4, s_lz, p_c))
    rz0.wait_recv()
    fzb0 = pass_on(2, 2, s_rz, p_xm)
    mate.append(pass_on(0, 4, s_rz, p_c))
    fa0.wait_recv()
    mate.append(pass_on(0, 2, s_f, p_c))
    fb0.wait_recv()
    mate.append(pass_on(2, 2, s_f, p_c))
    fa1.wait_recv()
    fza1 = pass_on(4, 2, s_f, p_z)
    mate.append(pass_on(4, 2, s_f, p_c))
    fb1.wait_recv()
    fzb1 = pass_on(6, 2, s_f, p_z)
    mate.append(pass_on(6, 2, s_f, p_c))
    z1.wait_recv()
    mate.append(pass_on(4, 4, s_z, p_c))
    fza0.wait_recv()
    mate.append(pass_on(0, 2, s_fz, p_c))
    fzb0.wait_recv()
    mate.append(pass_on(2, 2, s_fz, p_c))
    lz1.wait_recv()
    mate.append(pass_on(4, 4, s_lz, p_c))
    rz1.wait_recv()
    mate.append(pass_on(4, 4, s_rz, p_c))
    fza1.wait_recv()
    mate.append(pass_on(4, 2, s_fz, p_c))
    fzb1.wait_recv()
    mate.append(pass_on(6, 2, s_fz, p_c))
    for copy in mate:
        copy.wait_recv()
    loads[4].wait()

    to_log2 = float(NOPE + ROPE) ** -0.5 * LOG2E
    lane = lax.broadcasted_iota(jnp.int32, (512, 128), 1)
    key_at = lax.broadcasted_iota(jnp.int32, (1, 512), 1) + gi * 512
    loads[3].wait()
    query = lax.broadcasted_iota(jnp.int32, (256, 32), 0)
    key = lax.broadcasted_iota(jnp.int32, (256, 32), 1)
    new_live = (key % 8 == query // 32) & (key // 8 <= query % 4)
    new_score = lax.dot_general(
        G[:, pl.ds(gi, 1)].reshape(256, WIDTH), NEW[...], nt, preferred_element_type=f32
    )
    SN[...] = jnp.where(new_live, new_score * to_log2, -1e30)
    rows = pl.ds(gi * 32, 32)

    def one_request(r, carry):
        q = G[r].reshape(512, WIDTH)
        k = K[r]
        s = jnp.dot(q, k, preferred_element_type=jnp.float32) * to_log2
        s = jnp.where(key_at < len_ref[r], s, -1e30)
        sn = SN[pl.ds(r * 32, 32), :]
        M[...] = jnp.broadcast_to(jnp.maximum(jnp.max(s, 1, keepdims=True), -1e29), (512, 128))
        M[rows, :] = jnp.maximum(M[rows, :], jnp.max(sn, 1, keepdims=True))
        p = jnp.exp2(s - M[:, 0:1])
        pn = jnp.exp2(sn - M[rows, 0:1])
        L[...] = jnp.broadcast_to(jnp.sum(p, 1, keepdims=True), (512, 128))
        L[rows, :] = L[rows, :] + jnp.sum(pn, 1, keepdims=True)
        O[r] = lax.dot_general(
            p.astype(jnp.bfloat16), k[:KVL], nt, preferred_element_type=jnp.float32
        )
        O[r, rows, :] = O[r, rows, :] + jnp.dot(
            pn.astype(jnp.bfloat16), NEW[:, :KVL], preferred_element_type=jnp.float32
        )
        both = jnp.transpose(jnp.where(lane == 0, M[...], L[...]))
        ml_send[0, 0, pl.ds(r, 1), :] = both[0:1]
        ml_send[0, 1, pl.ds(r, 1), :] = both[1:2]
        return carry

    lax.fori_loop(0, 8, one_request, 0)

    mine = (ml_send[0, 0], ml_send[0, 1])
    total = mine
    for stage, peer in ((0, p_c), (1, p_z)):
        copy = net.send(ml_send.at[stage], ml_recv.at[stage], peer)
        copy.wait_recv()
        total = merge(total, (ml_recv[stage, 0], ml_recv[stage, 1]))
        ml_send[stage + 1, 0] = total[0]
        ml_send[stage + 1, 1] = total[1]
    last = [net.send(ml_send.at[2], ml_recv.at[2 + j], p) for j, p in enumerate((p_xp, p_xm, p_x2))]
    for j, copy in enumerate(last):
        copy.wait_recv()
        total = merge(total, (ml_recv[2 + j, 0], ml_recv[2 + j, 1]))
    SC[...] = jnp.zeros_like(SC)
    SC[0:8, :] = jnp.exp2(mine[0] - total[0]) / total[1]
    SCT[...] = jnp.transpose(SC[...])

    halves = []
    for r in range(8):
        part = (O[r] * SCT[:, r : r + 1]).astype(jnp.bfloat16)
        NB[r] = part.reshape(4, 2, 2, 32, KVL)
        if r % 4 == 3:
            span = pl.ds(r - 3, 4)
            halves.append(net.send(NB.at[span, :, :, co], RD.at[span], p_c))

    def add(a, b):
        return (a.astype(jnp.float32) + b.astype(jnp.float32)).astype(jnp.bfloat16)

    for h in range(2):
        halves[h].wait_recv()
        for r in range(4 * h, 4 * h + 4):
            T[r] = add(NB[r, :, :, c], RD[r])
        if h == 0:
            fa = net.send(T.at[0:2, x2], RF.at[0], p_xp)
            fb = net.send(T.at[2:4, x2], RF.at[1], p_xm)
    zr = net.send(T.at[4:8, :, zo], RZ1, p_z)
    fa.wait_recv()
    T[0:2, xp] = add(T[0:2, xp], RF[0])
    to_r = net.send(T.at[0:4, xp], RL, p_xp)
    fb.wait_recv()
    T[2:4, xm] = add(T[2:4, xm], RF[1])
    to_l = net.send(T.at[0:4, xm], RR, p_xm)
    zr.wait_recv()
    for r in range(4):
        V1[r] = add(T[4 + r, :, zl], RZ1[r])
    ga = net.send(V1.at[0:2, x2], RF.at[2, :, 0], p_xp)
    gb = net.send(V1.at[2:4, x2], RF.at[2, :, 1], p_xm)
    to_r.wait_recv()
    to_l.wait_recv()
    U0[...] = (
        T[0:4, x].astype(jnp.float32) + RL[...].astype(jnp.float32) + RR[...].astype(jnp.float32)
    ).astype(jnp.bfloat16)
    zz = net.send(U0.at[:, zo], RZ0, p_z)
    ga.wait_recv()
    V1[0:2, xp] = add(V1[0:2, xp], RF[2, :, 0])
    to_r1 = net.send(V1.at[:, xp], RL1, p_xp)
    gb.wait_recv()
    V1[2:4, xm] = add(V1[2:4, xm], RF[2, :, 1])
    to_l1 = net.send(V1.at[:, xm], RR1, p_xm)
    zz.wait_recv()
    F[0:4] = add(U0[:, zl], RZ0[...])
    to_r1.wait_recv()
    to_l1.wait_recv()
    F[4:8] = (
        V1[:, x].astype(jnp.float32) + RL1[...].astype(jnp.float32) + RR1[...].astype(jnp.float32)
    ).astype(jnp.bfloat16)

    latent = jnp.dot(
        MOVE[2], F[...].reshape(256, KVL), preferred_element_type=jnp.float32
    ).astype(jnp.bfloat16)
    for copy in values:
        copy.wait_recv()
    for i in range(8):
        out_ref[:, i * VDIM : (i + 1) * VDIM] = jnp.dot(
            latent[i * 32 : (i + 1) * 32], WV[i], preferred_element_type=jnp.float32
        ).astype(jnp.bfloat16)
    net.finish()
    pltpu.make_async_copy(X.at[0:127], X.at[0:127], all_send).wait()


def per_device(query_latent, q_up, kv_up, latent_cache, new_latent, lengths):
    bf, f32 = jnp.bfloat16, jnp.float32
    pair = np.arange(128) // 2
    freq = np.where(pair < ROPE // 2, 10000.0 ** (-(2.0 * pair) / ROPE), 0.0).astype(np.float32)
    vmem = pl.BlockSpec(memory_space=pltpu.VMEM)
    copies = 96
    out = pl.pallas_call(
        kernel,
        out_shape=jax.ShapeDtypeStruct((32, 8 * VDIM), bf),
        in_specs=[pl.BlockSpec(memory_space=pltpu.SMEM), vmem] + [pl.BlockSpec(memory_space=pl.ANY)] * 5,
        out_specs=vmem,
        scratch_shapes=[
            pltpu.VMEM((12, H * (NOPE + ROPE)), bf),
            pltpu.VMEM((4, H * (NOPE + VDIM)), bf),
            pltpu.VMEM((32, WIDTH), bf),
            pltpu.VMEM((3, 256, 256), bf),
            pltpu.VMEM((256, 32), f32),
            pltpu.VMEM((128, 32, 128), bf),
            pltpu.VMEM((128, 32, 128), bf),
            pltpu.VMEM((8, 2, 16, QL), bf),
            pltpu.VMEM((2, QL, 128), bf),
            pltpu.VMEM((KVL, NOPE), bf),
            pltpu.VMEM((8, 32, WIDE), bf),
            pltpu.VMEM((8, 32, WIDE), bf),
            pltpu.VMEM((8, KVL, VDIM), bf),
            pltpu.VMEM((8, 16, 32, WIDTH), bf),
            pltpu.VMEM((8, WIDTH, 512), bf),
            pltpu.VMEM((8, 512, KVL), f32),
            pltpu.VMEM((8, 4, 2, 2, 32, KVL), bf),
            pltpu.VMEM((8, 4, 2, 32, KVL), bf),
            pltpu.VMEM((8, 4, 2, 32, KVL), bf),
            pltpu.VMEM((3, 2, 2, 32, KVL), bf),
            pltpu.VMEM((4, 2, 32, KVL), bf),
            pltpu.VMEM((4, 2, 32, KVL), bf),
            pltpu.VMEM((4, 32, KVL), bf),
            pltpu.VMEM((4, 32, KVL), bf),
            pltpu.VMEM((4, 32, KVL), bf),
            pltpu.VMEM((4, 4, 32, KVL), bf),
            pltpu.VMEM((4, 2, 32, KVL), bf),
            pltpu.VMEM((4, 4, 32, KVL), bf),
            pltpu.VMEM((512, 128), f32),
            pltpu.VMEM((512, 128), f32),
            pltpu.VMEM((3, 2, 8, 512), f32),
            pltpu.VMEM((5, 2, 8, 512), f32),
            pltpu.VMEM((128, 512), f32),
            pltpu.VMEM((512, 128), f32),
            pltpu.VMEM((8, 32, KVL), bf),
            pltpu.SemaphoreType.DMA((copies,)),
            pltpu.SemaphoreType.DMA((copies,)),
            pltpu.SemaphoreType.DMA((5,)),
            pltpu.SemaphoreType.DMA,
            pltpu.SemaphoreType.DMA,
        ],
        compiler_params=pltpu.CompilerParams(
            collective_id=1, has_side_effects=True, vmem_limit_bytes=60 * 1024 * 1024
        ),
    )(
        lengths, jnp.asarray(freq)[None], query_latent.reshape(2, 16, QL), q_up, kv_up,
        latent_cache.transpose(0, 2, 1), new_latent.reshape(32, WIDTH),
    )
    return out.reshape(STEPS, 8, 8 * VDIM)


def solution(mesh):
    return jax.shard_map(
        per_device,
        mesh=mesh,
        in_specs=(
            P(None, "dp", None),
            P(("dp", "grp"), None),
            P(("dp", "grp"), None),
            P("dp", "grp", None),
            P(None, "dp", None),
            P("dp"),
        ),
        out_specs=P(None, "dp", "grp"),
        check_vma=False,
    )
```

```python
import jax
import jax.numpy as jnp
import numpy as np
from jax import lax
from jax.experimental import pallas as pl
from jax.experimental.pallas import tpu as pltpu
from jax.sharding import PartitionSpec as P

MESH = pl.DeviceIdType.MESH

H = 128
QL = 1536
KVL = 512
NOPE = 128
ROPE = 64
VDIM = 128
STEPS = 4
WIDTH = KVL + ROPE
WIDE = KVL + 128
LOG2E = 1.4426950408889634


class Copies:
    def __init__(self, send_sem, recv_sem):
        self.send_sem, self.recv_sem, self.sent = send_sem, recv_sem, []

    def send(self, src, dst, peer, axis="grp"):
        k = len(self.sent)
        copy = pltpu.make_async_remote_copy(
            src_ref=src,
            dst_ref=dst,
            send_sem=self.send_sem.at[k],
            recv_sem=self.recv_sem.at[k],
            device_id={axis: peer},
            device_id_type=MESH,
        )
        copy.start()
        self.sent.append(copy)
        return copy

    def finish(self):
        for copy in self.sent:
            copy.wait_send()


def merge(a, b):
    peak = jnp.maximum(a[0], b[0])
    return peak, a[1] * jnp.exp2(a[0] - peak) + b[1] * jnp.exp2(b[0] - peak)


def kernel(
    len_ref, freq_ref, ql_ref, q_ref, kv_ref, cache_ref, new_ref, out_ref,
    QIN, KVIN, NEW, MOVE, SN, X, LAND, QLS, W, KC, E, QR, WV,
    G, K, O, NB, RD, T, V, U, RFA, RLA, RRA, RZA, RFB, RLB, RRB, RZB, M, L, ml_send, ml_recv, SC, SCT, F,
    send_sem, recv_sem, load_sem, all_send, all_recv,
):
    di, gi = lax.axis_index("dp"), lax.axis_index("grp")
    me = di * 16 + gi
    x, zl, c = gi // 4, (gi // 2) % 2, gi % 2
    xp, xm, x2 = (x + 1) % 4, (x + 3) % 4, (x + 2) % 4
    zo, co = 1 - zl, 1 - c

    def at(xx, zz, cc):
        return xx * 4 + zz * 2 + cc

    p_xp, p_xm, p_x2 = at(xp, zl, c), at(xm, zl, c), at(x2, zl, c)
    p_z, p_c = at(x, zo, c), at(x, zl, co)

    loads = [
        pltpu.make_async_copy(src, dst, load_sem.at[n])
        for n, (src, dst) in enumerate(
            ((q_ref, QIN), (kv_ref, KVIN), (ql_ref, QLS.at[0]), (new_ref, NEW), (cache_ref, K))
        )
    ]
    for load in loads:
        load.start()
    barrier = pltpu.get_barrier_semaphore()

    def there(j):
        d = (me + 37 * j) % 128
        return d // 16, d % 16

    def greet(j, carry):
        dd, gg = there(j)
        pl.semaphore_signal(
            barrier, inc=1, device_id={"dp": dd, "grp": gg}, device_id_type=MESH
        )
        return carry

    lax.fori_loop(1, 128, greet, 0)
    bf, f32 = jnp.bfloat16, jnp.float32
    nt = (((1,), (1,)), ((), ()))

    loads[0].wait()
    loads[1].wait()

    def pack(p, carry):
        def tiles(upper, lower):
            a = QIN[:, pl.ds(pl.multiple_of(upper * 128, 128), 128)]
            b = KVIN[:, pl.ds(pl.multiple_of(lower * 128, 128), 128)]
            return jnp.concatenate([a, b], 0)

        X[2 * p, 0:16] = tiles(3 * p, 4 * p)
        X[2 * p, 16:32] = tiles(3 * p + 1, 4 * p + 1)
        X[2 * p + 1, 0:16] = tiles(3 * p + 1, 4 * p + 2)
        X[2 * p + 1, 16:32] = tiles(3 * p + 2, 4 * p + 3)
        return carry

    lax.fori_loop(0, 64, pack, 0)
    LAND[me] = X[8 * gi + di]
    loads[2].wait()
    pl.semaphore_wait(barrier, 127)

    net = Copies(send_sem, recv_sem)
    rows = pl.ds(pl.multiple_of(c * 16, 16), 16)
    columns = pl.ds(pl.multiple_of(x * 384, 128), 384)
    latents = [
        net.send(QLS.at[0, rows, columns], QLS.at[8 - j, rows, columns], (di + j) % 8, "dp")
        for j in range(1, 8)
    ]

    def deal(j, carry):
        dd, gg = there(j)
        pltpu.make_async_remote_copy(
            src_ref=X.at[8 * gg + dd],
            dst_ref=LAND.at[me],
            send_sem=all_send,
            recv_sem=all_recv,
            device_id={"dp": dd, "grp": gg},
            device_id_type=MESH,
        ).start()
        return carry

    lax.fori_loop(1, 128, deal, 0)
    for copy in latents:
        copy.wait_recv()
    piece = QLS.at[1:8, rows, columns]
    latents = [net.send(piece, piece, p) for p in (p_xp, p_xm, p_x2)]

    to = lax.broadcasted_iota(jnp.int32, (256, 256), 0)
    was = lax.broadcasted_iota(jnp.int32, (256, 256), 1)
    within = jnp.where(to < 96, to, to - 96)
    twelve = jnp.where(to < 96, to, to - 80)
    for n in range(1, 8):
        twelve = twelve + jnp.where(within >= 12 * n, 20, 0)
    four = 32 * ((to % 32) // 4) + to % 4 + jnp.where(to < 224, 12, 28)
    half = to - to % 32 + ((to % 16) // 4) * 8 + ((to % 32) // 16) * 4 + to % 4
    MOVE[0] = (was == jnp.where(to < 192, twelve, four)).astype(f32).astype(bf)
    MOVE[1] = (was == half).astype(f32).astype(bf)
    MOVE[2] = (was == ((to // 4) % 8) * 16 + (to % 4) * 4 + to // 32).astype(f32).astype(bf)
    MOVE[3] = (was == (to % 8) * 32 + to // 8).astype(f32).astype(bf)
    SC[...] = jnp.zeros_like(SC)

    row = lax.broadcasted_iota(jnp.int32, (16, 128), 0)
    sign = jnp.where(lax.broadcasted_iota(jnp.int32, (16, 128), 1) % 2 == 0, -1.0, 1.0)
    turns = []
    for h in range(2):
        position = row // 4
        for r in range(4):
            position = position + jnp.where(row % 4 == r, len_ref[4 * h + r], 0)
        angle = position.astype(f32) * freq_ref[...]
        turns.append((jnp.cos(angle), sign * jnp.sin(angle)))

    for copy in latents:
        copy.wait_recv()
    net.send(QLS.at[1:8, rows], QLS.at[1:8, rows], p_c).wait_recv()
    pltpu.make_async_copy(LAND.at[0:127], LAND.at[0:127], all_recv).wait()

    for b in range(16):
        block = jnp.dot(
            MOVE[0], LAND[8 * b : 8 * b + 8].reshape(256, 128), preferred_element_type=f32
        ).astype(bf)
        W[0, 96 * b : 96 * b + 96] = block[0:96]
        W[1, 96 * b : 96 * b + 96] = block[96:192]
        KC[32 * b : 32 * b + 32] = block[192:224]
        WV[di, 32 * b : 32 * b + 32] = block[224:256]
    latent_in = QLS[...].reshape(256, QL)
    qa = jnp.dot(latent_in, W[0], preferred_element_type=f32).astype(bf)
    qb = jnp.dot(latent_in, W[1], preferred_element_type=f32).astype(bf)
    qa = jnp.dot(MOVE[1], qa, preferred_element_type=f32)
    qb = jnp.dot(MOVE[1], qb, preferred_element_type=f32)
    ra, rb = pltpu.roll(qa, 64, 1), pltpu.roll(qb, 64, 1)
    lane = lax.broadcasted_iota(jnp.int32, (256, 128), 1)
    odd = di % 2 == 1
    plain = jnp.where(odd, jnp.where(lane < 64, ra, rb), qa).astype(bf)
    rotary = jnp.where(lane < 64, jnp.where(odd, rb, qb), 0.0).astype(bf)
    absorbed = lax.dot_general(plain, KC[...], nt, preferred_element_type=f32).astype(bf)
    E[:, :, 0:KVL] = absorbed.reshape(8, 32, KVL)
    E[:, :, KVL:WIDE] = rotary.reshape(8, 32, 128)
    heads = []
    for h in range(2):
        span = pl.ds(16 * h, 16)
        heads.append(
            [net.send(E.at[j, span], QR.at[h, di], (di + j) % 8, "dp") for j in range(1, 8)]
        )
        QR[h, di] = E[0, span]
    loads[3].wait()
    to_log2 = float(NOPE + ROPE) ** -0.5 * LOG2E

    def place(h):
        for copy in heads[h]:
            copy.wait_recv()
        span = pl.ds(4 * h, 4)
        rotary = QR[h, :, :, KVL:WIDE].reshape(128, 128).astype(f32)
        even = lax.broadcasted_iota(jnp.int32, (128, 128), 1) % 2 == 0
        other = jnp.where(even, pltpu.roll(rotary, 127, 1), pltpu.roll(rotary, 1, 1))
        cosine, sine = turns[h]
        rotary = rotary.reshape(8, 16, 128) * cosine[None] + other.reshape(8, 16, 128) * sine[None]
        move = MOVE[2, 0:128, 0:128]
        absorbed = jnp.dot(move, QR[h, :, :, 0:KVL].reshape(128, KVL), preferred_element_type=f32)
        rotary = jnp.dot(move, rotary.reshape(128, 128).astype(bf), preferred_element_type=f32)
        G[span, pl.ds(gi, 1), :, 0:KVL] = absorbed.astype(bf).reshape(4, 1, 32, KVL)
        G[span, pl.ds(gi, 1), :, KVL:WIDTH] = rotary[:, :ROPE].astype(bf).reshape(4, 1, 32, ROPE)

    def new_scores(h):
        query = lax.broadcasted_iota(jnp.int32, (128, 32), 0)
        key = lax.broadcasted_iota(jnp.int32, (128, 32), 1)
        live = (key % 8 == 4 * h + query // 32) & (key // 8 <= query % 4)
        score = lax.dot_general(
            G[pl.ds(4 * h, 4), pl.ds(gi, 1)].reshape(128, WIDTH), NEW[...], nt,
            preferred_element_type=f32,
        )
        SN[pl.ds(128 * h, 128)] = jnp.where(live, score * to_log2, -1e30)

    def gather(h):
        b = 4 * h
        A, B = (b, 2), (b + 2, 2)
        s_l, s_r, s_z = p_xm, p_xp, p_z
        s_lz, s_rz, s_f, s_fz = at(xm, zo, c), at(xp, zo, c), p_x2, at(x2, zo, c)

        def go(span, slot, peer):
            block = G.at[pl.ds(span[0], span[1]), slot]
            return net.send(block, block, peer)

        mate = []

        def share(span, slot):
            mate.append(go(span, slot, p_c))

        z_a = go(A, gi, p_z)
        l_b, r_b = go(B, gi, p_xp), go(B, gi, p_xm)
        l_a, r_a = go(A, gi, p_xp), go(A, gi, p_xm)
        share((b, 4), gi)
        z_b = go(B, gi, p_z)
        yield
        z_a.wait_recv()
        lz_a, rz_a = go(A, s_z, p_xp), go(A, s_z, p_xm)
        share(A, s_z)
        l_b.wait_recv()
        f0_b, lz_b = go((b + 2, 1), s_l, p_xp), go(B, s_l, p_z)
        share(B, s_l)
        r_b.wait_recv()
        f1_b, rz_b = go((b + 3, 1), s_r, p_xm), go(B, s_r, p_z)
        share(B, s_r)
        l_a.wait_recv()
        f0_a = go((b, 1), s_l, p_xp)
        share(A, s_l)
        r_a.wait_recv()
        f1_a = go((b + 1, 1), s_r, p_xm)
        share(A, s_r)
        yield
        lz_a.wait_recv()
        fz0_a = go((b, 1), s_lz, p_xp)
        share(A, s_lz)
        rz_a.wait_recv()
        fz1_a = go((b + 1, 1), s_rz, p_xm)
        share(A, s_rz)
        f0_b.wait_recv()
        fz0_b = go((b + 2, 1), s_f, p_z)
        f1_b.wait_recv()
        fz1_b = go((b + 3, 1), s_f, p_z)
        share(B, s_f)
        f0_a.wait_recv()
        f1_a.wait_recv()
        share(A, s_f)
        yield
        z_b.wait_recv()
        share(B, s_z)
        lz_b.wait_recv()
        share(B, s_lz)
        rz_b.wait_recv()
        share(B, s_rz)
        fz0_a.wait_recv()
        fz1_a.wait_recv()
        share(A, s_fz)
        fz0_b.wait_recv()
        fz1_b.wait_recv()
        share(B, s_fz)
        yield
        for copy in mate:
            copy.wait_recv()
        yield

    lanes = lax.broadcasted_iota(jnp.int32, (512, 128), 1)
    key_at = lax.broadcasted_iota(jnp.int32, (1, 512), 1) + gi * 512
    own_rows = pl.ds(gi * 32, 32)

    def one_request(r, carry):
        h = r // 4
        q = G[r].reshape(512, WIDTH)
        k = K[r]
        s = jnp.dot(q, k, preferred_element_type=f32) * to_log2
        s = jnp.where(key_at < len_ref[r], s, -1e30)
        sn = SN[pl.ds(r * 32, 32), :]
        M[...] = jnp.broadcast_to(jnp.maximum(jnp.max(s, 1, keepdims=True), -1e29), (512, 128))
        M[own_rows, :] = jnp.maximum(M[own_rows, :], jnp.max(sn, 1, keepdims=True))
        p = jnp.exp2(s - M[:, 0:1])
        pn = jnp.exp2(sn - M[own_rows, 0:1])
        L[...] = jnp.broadcast_to(jnp.sum(p, 1, keepdims=True), (512, 128))
        L[own_rows, :] = L[own_rows, :] + jnp.sum(pn, 1, keepdims=True)
        O[r] = lax.dot_general(p.astype(bf), k[:KVL], nt, preferred_element_type=f32)
        O[r, own_rows, :] = O[r, own_rows, :] + jnp.dot(
            pn.astype(bf), NEW[:, :KVL], preferred_element_type=f32
        )
        both = jnp.transpose(jnp.where(lanes == 0, M[...], L[...]))
        ml_send[h, 0, pl.ds(r % 4, 1), :] = both[0:1]
        ml_send[h, 0, pl.ds(4 + r % 4, 1), :] = both[1:2]
        return carry

    def work(r):
        lax.fori_loop(r, r + 1, one_request, 0)

    def peaks(h):
        def pair(ref):
            return ref[0:4], ref[4:8]

        mine = pair(ml_send[h, 0])
        total = mine
        for stage, peer in ((0, p_c), (1, p_z)):
            copy = net.send(ml_send.at[h, stage], ml_recv.at[h, stage], peer)
            yield
            copy.wait_recv()
            total = merge(total, pair(ml_recv[h, stage]))
            ml_send[h, stage + 1, 0:4] = total[0]
            ml_send[h, stage + 1, 4:8] = total[1]
        last = [
            net.send(ml_send.at[h, 2], ml_recv.at[h, 2 + j], p)
            for j, p in enumerate((p_xp, p_xm, p_x2))
        ]
        yield
        for j, copy in enumerate(last):
            copy.wait_recv()
            total = merge(total, pair(ml_recv[h, 2 + j]))
        SC[0:4] = jnp.exp2(mine[0] - total[0]) / total[1]
        SCT[h] = jnp.transpose(SC[...])
        yield

    def add(*terms):
        total = terms[0].astype(f32)
        for term in terms[1:]:
            total = total + term.astype(f32)
        return total.astype(bf)

    def reduce(h):
        b = 4 * h
        two = pl.ds(b, 2), pl.ds(b + 2, 2)
        mate = []
        for n in range(2):
            for r in (b + 2 * n, b + 2 * n + 1):
                part = (O[r] * SCT[h, :, r - b : r - b + 1]).astype(bf)
                NB[r] = part.reshape(4, 2, 2, 32, KVL)
            mate.append(net.send(NB.at[two[n], :, :, co], RD.at[two[n]], p_c))
        yield
        mate[0].wait_recv()
        for r in (b, b + 1):
            T[r] = add(NB[r, :, :, c], RD[r])
        f0 = net.send(T.at[b, x2], RFA.at[h, 0], p_xp)
        f1 = net.send(T.at[b + 1, x2], RFA.at[h, 1], p_xm)
        l1 = net.send(T.at[b + 1, xp], RLA.at[h, 1], p_xp)
        r0 = net.send(T.at[b, xm], RRA.at[h, 0], p_xm)
        mate[1].wait_recv()
        for r in (b + 2, b + 3):
            T[r] = add(NB[r, :, :, c], RD[r])
        z_b = net.send(T.at[two[1], :, zo], RZB.at[h], p_z)
        yield
        f0.wait_recv()
        T[b, xp] = add(T[b, xp], RFA[h, 0])
        l0 = net.send(T.at[b, xp], RLA.at[h, 0], p_xp)
        f1.wait_recv()
        T[b + 1, xm] = add(T[b + 1, xm], RFA[h, 1])
        r1 = net.send(T.at[b + 1, xm], RRA.at[h, 1], p_xm)
        z_b.wait_recv()
        for n in range(2):
            V[h, n] = add(T[b + 2 + n, :, zl], RZB[h, n])
        g0 = net.send(V.at[h, 0, x2], RFB.at[h, 0], p_xp)
        g1 = net.send(V.at[h, 1, x2], RFB.at[h, 1], p_xm)
        k1 = net.send(V.at[h, 1, xp], RLB.at[h, 1], p_xp)
        q0 = net.send(V.at[h, 0, xm], RRB.at[h, 0], p_xm)
        yield
        for copy in (l1, r0, l0, r1):
            copy.wait_recv()
        for n in range(2):
            U[h, n] = add(T[b + n, x], RLA[h, n], RRA[h, n])
        z_a = net.send(U.at[h, :, zo], RZA.at[h], p_z)
        g0.wait_recv()
        V[h, 0, xp] = add(V[h, 0, xp], RFB[h, 0])
        k0 = net.send(V.at[h, 0, xp], RLB.at[h, 0], p_xp)
        g1.wait_recv()
        V[h, 1, xm] = add(V[h, 1, xm], RFB[h, 1])
        q1 = net.send(V.at[h, 1, xm], RRB.at[h, 1], p_xm)
        yield
        z_a.wait_recv()
        F[two[0]] = add(U[h, :, zl], RZA[h])
        for copy in (k1, q0, k0, q1):
            copy.wait_recv()
        F[two[1]] = add(V[h, :, x], RLB[h], RRB[h])
        yield

    def values():
        partner = (di + 4) % 8
        around = [(di // 4) * 4 + (di + j) % 4 for j in range(1, 4)]
        mine = [net.send(WV.at[di], WV.at[di], p, "dp") for p in around]
        yield
        over = net.send(WV.at[di], WV.at[di], partner, "dp")
        yield
        over.wait_recv()
        mine += [net.send(WV.at[partner], WV.at[partner], p, "dp") for p in around]
        yield
        for copy in mine:
            copy.wait_recv()
        yield

    gather0, gather1 = gather(0), gather(1)
    peaks0, peaks1 = peaks(0), peaks(1)
    reduce0, reduce1 = reduce(0), reduce(1)
    weights = values()
    place(0)
    next(gather0)
    place(1)
    new_scores(0)
    new_scores(1)
    next(weights)
    next(gather0)
    next(gather0)
    next(gather1)
    next(weights)
    next(gather0)
    loads[4].wait()
    next(gather0)
    work(0)
    next(gather1)
    work(1)
    next(gather1)
    work(2)
    next(gather1)
    work(3)
    next(peaks0)
    next(weights)
    next(gather1)
    next(peaks0)
    work(4)
    next(peaks0)
    work(5)
    next(peaks0)
    next(reduce0)
    work(6)
    next(reduce0)
    work(7)
    next(peaks1)
    next(reduce0)
    next(peaks1)
    next(peaks1)
    next(reduce0)
    next(peaks1)
    next(reduce1)
    next(reduce0)
    next(reduce1)
    next(reduce1)
    next(reduce1)
    next(weights)
    next(reduce1)

    latent = jnp.dot(MOVE[3], F[...].reshape(256, KVL), preferred_element_type=f32).astype(bf)
    for i in range(8):
        out_ref[:, i * VDIM : (i + 1) * VDIM] = jnp.dot(
            latent[i * 32 : (i + 1) * 32], WV[i], preferred_element_type=f32
        ).astype(bf)
    net.finish()
    pltpu.make_async_copy(X.at[0:127], X.at[0:127], all_send).wait()


def per_device(query_latent, q_up, kv_up, latent_cache, new_latent, lengths):
    bf, f32 = jnp.bfloat16, jnp.float32
    pair = np.arange(128) // 2
    freq = np.where(pair < ROPE // 2, 10000.0 ** (-(2.0 * pair) / ROPE), 0.0).astype(np.float32)
    vmem = pl.BlockSpec(memory_space=pltpu.VMEM)
    copies = 160
    out = pl.pallas_call(
        kernel,
        out_shape=jax.ShapeDtypeStruct((32, 8 * VDIM), bf),
        in_specs=[pl.BlockSpec(memory_space=pltpu.SMEM), vmem] + [pl.BlockSpec(memory_space=pl.ANY)] * 5,
        out_specs=vmem,
        scratch_shapes=[
            pltpu.VMEM((12, H * (NOPE + ROPE)), bf),
            pltpu.VMEM((4, H * (NOPE + VDIM)), bf),
            pltpu.VMEM((32, WIDTH), bf),
            pltpu.VMEM((4, 256, 256), bf),
            pltpu.VMEM((256, 32), f32),
            pltpu.VMEM((128, 32, 128), bf),
            pltpu.VMEM((128, 32, 128), bf),
            pltpu.VMEM((8, 32, QL), bf),
            pltpu.VMEM((2, QL, 128), bf),
            pltpu.VMEM((KVL, NOPE), bf),
            pltpu.VMEM((8, 32, WIDE), bf),
            pltpu.VMEM((2, 8, 16, WIDE), bf),
            pltpu.VMEM((8, KVL, VDIM), bf),
            pltpu.VMEM((8, 16, 32, WIDTH), bf),
            pltpu.VMEM((8, WIDTH, 512), bf),
            pltpu.VMEM((8, 512, KVL), f32),
            pltpu.VMEM((8, 4, 2, 2, 32, KVL), bf),
            pltpu.VMEM((8, 4, 2, 32, KVL), bf),
            pltpu.VMEM((8, 4, 2, 32, KVL), bf),
            pltpu.VMEM((2, 2, 4, 32, KVL), bf),
            pltpu.VMEM((2, 2, 2, 32, KVL), bf),
            pltpu.VMEM((2, 2, 2, 32, KVL), bf),
            pltpu.VMEM((2, 2, 2, 32, KVL), bf),
            pltpu.VMEM((2, 2, 2, 32, KVL), bf),
            pltpu.VMEM((2, 2, 32, KVL), bf),
            pltpu.VMEM((2, 2, 32, KVL), bf),
            pltpu.VMEM((2, 2, 32, KVL), bf),
            pltpu.VMEM((2, 2, 32, KVL), bf),
            pltpu.VMEM((2, 2, 4, 32, KVL), bf),
            pltpu.VMEM((512, 128), f32),
            pltpu.VMEM((512, 128), f32),
            pltpu.VMEM((2, 3, 8, 512), f32),
            pltpu.VMEM((2, 5, 8, 512), f32),
            pltpu.VMEM((128, 512), f32),
            pltpu.VMEM((2, 512, 128), f32),
            pltpu.VMEM((8, 32, KVL), bf),
            pltpu.SemaphoreType.DMA((copies,)),
            pltpu.SemaphoreType.DMA((copies,)),
            pltpu.SemaphoreType.DMA((5,)),
            pltpu.SemaphoreType.DMA,
            pltpu.SemaphoreType.DMA,
        ],
        compiler_params=pltpu.CompilerParams(
            collective_id=1, has_side_effects=True, vmem_limit_bytes=60 * 1024 * 1024
        ),
    )(
        lengths, jnp.asarray(freq)[None], query_latent.reshape(32, QL), q_up, kv_up,
        latent_cache.transpose(0, 2, 1), new_latent.reshape(32, WIDTH),
    )
    return out.reshape(STEPS, 8, 8 * VDIM)


def solution(mesh):
    return jax.shard_map(
        per_device,
        mesh=mesh,
        in_specs=(
            P(None, "dp", None),
            P(("dp", "grp"), None),
            P(("dp", "grp"), None),
            P("dp", "grp", None),
            P(None, "dp", None),
            P("dp"),
        ),
        out_specs=P(None, "dp", "grp"),
        check_vma=False,
    )
```

```python
import jax
import jax.numpy as jnp
import numpy as np
from jax import lax
from jax.experimental import pallas as pl
from jax.experimental.pallas import tpu as pltpu
from jax.sharding import PartitionSpec as P

MESH = pl.DeviceIdType.MESH

H = 128
QL = 1536
KVL = 512
NOPE = 128
ROPE = 64
VDIM = 128
STEPS = 4
WIDTH = KVL + ROPE
WIDE = KVL + 128
LOG2E = 1.4426950408889634
POOL = 40
GROUPS = 68
SPLIT = 40


class Copies:
    def __init__(self, send_sem, recv_sem):
        self.send_sem, self.recv_sem, self.sent, self.groups = send_sem, recv_sem, [], 0

    def group(self):
        self.groups += 1
        assert self.groups <= GROUPS
        return self.groups - 1

    def send(self, src, dst, peer, axis="grp", group=None):
        k = len(self.sent)
        if k >= POOL:
            self.sent[k - POOL].wait_send()
        copy = pltpu.make_async_remote_copy(
            src_ref=src,
            dst_ref=dst,
            send_sem=self.send_sem.at[k % POOL],
            recv_sem=self.recv_sem.at[self.group() if group is None else group],
            device_id={axis: peer},
            device_id_type=MESH,
        )
        copy.start()
        self.sent.append(copy)
        return copy

    def arrive(self, group, like):
        pltpu.make_async_copy(like, like, self.recv_sem.at[group]).wait()

    def finish(self):
        for copy in self.sent[-POOL:]:
            copy.wait_send()


def kernel(
    len_ref, freq_ref, ql_ref, q_ref, kv_ref, cache_ref, new_ref, out_ref,
    QIN, KVIN, NEW, MOVE, SN, X, LAND, QLS, W, KC, E, QR, WV,
    G, K, O, NB, RD, T, V, U, RFA, RLA, RRA, RZA, RFB, RLB, RRB, RZB, S, M, L, sums, ml_send, ml_recv, SC, SCT, F,
    send_sem, recv_sem, load_sem, all_send, all_recv,
):
    di, gi = lax.axis_index("dp"), lax.axis_index("grp")
    me = di * 16 + gi
    x, zl, c = gi // 4, (gi // 2) % 2, gi % 2
    xp, xm, x2 = (x + 1) % 4, (x + 3) % 4, (x + 2) % 4
    zo, co = 1 - zl, 1 - c

    def at(xx, zz, cc):
        return xx * 4 + zz * 2 + cc

    p_xp, p_xm, p_x2 = at(xp, zl, c), at(xm, zl, c), at(x2, zl, c)
    p_z, p_c = at(x, zo, c), at(x, zl, co)

    loads = [
        pltpu.make_async_copy(src, dst, load_sem.at[n])
        for n, (src, dst) in enumerate(
            ((q_ref, QIN), (kv_ref, KVIN), (ql_ref, QLS.at[0]), (new_ref, NEW), (cache_ref, K))
        )
    ]
    for load in loads:
        load.start()
    barrier = pltpu.get_barrier_semaphore()

    def there(j):
        d = (me + 37 * j) % 128
        return d // 16, d % 16

    def greet(j, carry):
        dd, gg = there(j)
        pl.semaphore_signal(
            barrier, inc=1, device_id={"dp": dd, "grp": gg}, device_id_type=MESH
        )
        return carry

    lax.fori_loop(1, 128, greet, 0)
    bf, f32 = jnp.bfloat16, jnp.float32
    nt = (((1,), (1,)), ((), ()))

    loads[0].wait()
    loads[1].wait()

    def pack(p, carry):
        def tiles(upper, lower):
            a = QIN[:, pl.ds(pl.multiple_of(upper * 128, 128), 128)]
            b = KVIN[:, pl.ds(pl.multiple_of(lower * 128, 128), 128)]
            return jnp.concatenate([a, b], 0)

        X[2 * p, 0:16] = tiles(3 * p, 4 * p)
        X[2 * p, 16:32] = tiles(3 * p + 1, 4 * p + 1)
        X[2 * p + 1, 0:16] = tiles(3 * p + 1, 4 * p + 2)
        X[2 * p + 1, 16:32] = tiles(3 * p + 2, 4 * p + 3)
        return carry

    lax.fori_loop(0, 64, pack, 0)
    LAND[me] = X[8 * gi + di]
    loads[2].wait()
    pl.semaphore_wait(barrier, 127)

    net = Copies(send_sem, recv_sem)
    rows = pl.ds(pl.multiple_of(c * 16, 16), 16)
    columns = pl.ds(pl.multiple_of(x * 384, 128), 384)
    piece = QLS.at[1:8, rows, columns]
    first, second = net.group(), net.group()
    for j in range(1, 8):
        net.send(QLS.at[0, rows, columns], QLS.at[8 - j, rows, columns], (di + j) % 8, "dp", first)

    def deal(j, carry):
        dd, gg = there(j)
        pltpu.make_async_remote_copy(
            src_ref=X.at[8 * gg + dd],
            dst_ref=LAND.at[me],
            send_sem=all_send,
            recv_sem=all_recv,
            device_id={"dp": dd, "grp": gg},
            device_id_type=MESH,
        ).start()
        return carry

    lax.fori_loop(1, SPLIT, deal, 0)
    net.arrive(first, piece)
    for p in (p_xp, p_xm, p_x2):
        net.send(piece, piece, p, group=second)
    lax.fori_loop(SPLIT, 128, deal, 0)

    to = lax.broadcasted_iota(jnp.int32, (256, 256), 0)
    was = lax.broadcasted_iota(jnp.int32, (256, 256), 1)
    within = jnp.where(to < 96, to, to - 96)
    twelve = jnp.where(to < 96, to, to - 80)
    for n in range(1, 8):
        twelve = twelve + jnp.where(within >= 12 * n, 20, 0)
    four = 32 * ((to % 32) // 4) + to % 4 + jnp.where(to < 224, 12, 28)
    half = to - to % 32 + ((to % 16) // 4) * 8 + ((to % 32) // 16) * 4 + to % 4
    MOVE[0] = (was == jnp.where(to < 192, twelve, four)).astype(f32).astype(bf)
    MOVE[1] = (was == half).astype(f32).astype(bf)
    MOVE[2] = (was == ((to // 4) % 8) * 16 + (to % 4) * 4 + to // 32).astype(f32).astype(bf)
    MOVE[3] = (was == (to % 8) * 32 + to // 8).astype(f32).astype(bf)
    SC[...] = jnp.zeros_like(SC)
    ml_send[...] = jnp.zeros_like(ml_send)

    row = lax.broadcasted_iota(jnp.int32, (16, 128), 0)
    sign = jnp.where(lax.broadcasted_iota(jnp.int32, (16, 128), 1) % 2 == 0, -1.0, 1.0)
    turns = []
    for h in range(2):
        position = row // 4
        for r in range(4):
            position = position + jnp.where(row % 4 == r, len_ref[4 * h + r], 0)
        angle = position.astype(f32) * freq_ref[...]
        turns.append((jnp.cos(angle), sign * jnp.sin(angle)))

    net.arrive(second, QLS.at[1:8, rows, 0:1152])
    net.send(QLS.at[1:8, rows], QLS.at[1:8, rows], p_c).wait_recv()
    pltpu.make_async_copy(LAND.at[0:127], LAND.at[0:127], all_recv).wait()

    for b in range(16):
        block = jnp.dot(
            MOVE[0], LAND[8 * b : 8 * b + 8].reshape(256, 128), preferred_element_type=f32
        ).astype(bf)
        W[0, 96 * b : 96 * b + 96] = block[0:96]
        W[1, 96 * b : 96 * b + 96] = block[96:192]
        KC[32 * b : 32 * b + 32] = block[192:224]
        WV[di, 32 * b : 32 * b + 32] = block[224:256]
    latent_in = QLS[...].reshape(256, QL)
    qa = jnp.dot(latent_in, W[0], preferred_element_type=f32).astype(bf)
    qb = jnp.dot(latent_in, W[1], preferred_element_type=f32).astype(bf)
    qa = jnp.dot(MOVE[1], qa, preferred_element_type=f32)
    qb = jnp.dot(MOVE[1], qb, preferred_element_type=f32)
    ra, rb = pltpu.roll(qa, 64, 1), pltpu.roll(qb, 64, 1)
    lane = lax.broadcasted_iota(jnp.int32, (256, 128), 1)
    odd = di % 2 == 1
    plain = jnp.where(odd, jnp.where(lane < 64, ra, rb), qa).astype(bf)
    rotary = jnp.where(lane < 64, jnp.where(odd, rb, qb), 0.0).astype(bf)
    absorbed = lax.dot_general(plain, KC[...], nt, preferred_element_type=f32).astype(bf)
    E[:, :, 0:KVL] = absorbed.reshape(8, 32, KVL)
    E[:, :, KVL:WIDE] = rotary.reshape(8, 32, 128)
    heads = []
    for h in range(2):
        span = pl.ds(16 * h, 16)
        heads.append(net.group())
        for j in range(1, 8):
            net.send(E.at[j, span], QR.at[h, di], (di + j) % 8, "dp", heads[h])
        QR[h, di] = E[0, span]
    loads[3].wait()
    to_log2 = float(NOPE + ROPE) ** -0.5 * LOG2E

    def place(h):
        net.arrive(heads[h], QR.at[h, 0:7])
        span = pl.ds(4 * h, 4)
        rotary = QR[h, :, :, KVL:WIDE].reshape(128, 128).astype(f32)
        even = lax.broadcasted_iota(jnp.int32, (128, 128), 1) % 2 == 0
        other = jnp.where(even, pltpu.roll(rotary, 127, 1), pltpu.roll(rotary, 1, 1))
        cosine, sine = turns[h]
        rotary = rotary.reshape(8, 16, 128) * cosine[None] + other.reshape(8, 16, 128) * sine[None]
        move = MOVE[2, 0:128, 0:128]
        absorbed = jnp.dot(move, QR[h, :, :, 0:KVL].reshape(128, KVL), preferred_element_type=f32)
        rotary = jnp.dot(move, rotary.reshape(128, 128).astype(bf), preferred_element_type=f32)
        G[span, pl.ds(gi, 1), :, 0:KVL] = absorbed.astype(bf).reshape(4, 1, 32, KVL)
        G[span, pl.ds(gi, 1), :, KVL:WIDTH] = rotary[:, :ROPE].astype(bf).reshape(4, 1, 32, ROPE)

    def new_scores(h):
        query = lax.broadcasted_iota(jnp.int32, (128, 32), 0)
        key = lax.broadcasted_iota(jnp.int32, (128, 32), 1)
        live = (key % 8 == 4 * h + query // 32) & (key // 8 <= query % 4)
        score = lax.dot_general(
            G[pl.ds(4 * h, 4), pl.ds(gi, 1)].reshape(128, WIDTH), NEW[...], nt,
            preferred_element_type=f32,
        )
        SN[pl.ds(128 * h, 128)] = jnp.where(live, score * to_log2, -1e30)

    def gather(h):
        b = 4 * h
        A, B = (b, 2), (b + 2, 2)
        s_l, s_r, s_z = p_xm, p_xp, p_z
        s_lz, s_rz, s_f, s_fz = at(xm, zo, c), at(xp, zo, c), p_x2, at(x2, zo, c)

        def go(span, slot, peer, group=None):
            block = G.at[pl.ds(span[0], span[1]), slot]
            return net.send(block, block, peer, group=group)

        mate, far, far_a, far_b = net.group(), net.group(), net.group(), net.group()

        def share(span, slot):
            go(span, slot, p_c, mate)

        z_a = go(A, gi, p_z)
        l_b, r_b = go(B, gi, p_xp), go(B, gi, p_xm)
        l_a, r_a = go(A, gi, p_xp), go(A, gi, p_xm)
        share((b, 4), gi)
        z_b = go(B, gi, p_z)
        yield
        z_a.wait_recv()
        lz_a, rz_a = go(A, s_z, p_xp), go(A, s_z, p_xm)
        share(A, s_z)
        l_b.wait_recv()
        f0_b, lz_b = go((b + 2, 1), s_l, p_xp), go(B, s_l, p_z)
        share(B, s_l)
        r_b.wait_recv()
        f1_b, rz_b = go((b + 3, 1), s_r, p_xm), go(B, s_r, p_z)
        share(B, s_r)
        l_a.wait_recv()
        go((b, 1), s_l, p_xp, far)
        share(A, s_l)
        r_a.wait_recv()
        go((b + 1, 1), s_r, p_xm, far)
        share(A, s_r)
        yield
        lz_a.wait_recv()
        go((b, 1), s_lz, p_xp, far_a)
        share(A, s_lz)
        rz_a.wait_recv()
        go((b + 1, 1), s_rz, p_xm, far_a)
        share(A, s_rz)
        f0_b.wait_recv()
        go((b + 2, 1), s_f, p_z, far_b)
        f1_b.wait_recv()
        go((b + 3, 1), s_f, p_z, far_b)
        share(B, s_f)
        net.arrive(far, G.at[pl.ds(b, 2), 0])
        share(A, s_f)
        yield
        z_b.wait_recv()
        share(B, s_z)
        lz_b.wait_recv()
        share(B, s_lz)
        rz_b.wait_recv()
        share(B, s_rz)
        net.arrive(far_a, G.at[pl.ds(b, 2), 0])
        share(A, s_fz)
        net.arrive(far_b, G.at[pl.ds(b, 2), 0])
        share(B, s_fz)
        yield
        net.arrive(mate, G.at[pl.ds(b, 4), 0:8])
        yield

    lanes = lax.broadcasted_iota(jnp.int32, (512, 128), 1)
    key_at = lax.broadcasted_iota(jnp.int32, (1, 512), 1) + gi * 512
    own_rows = pl.ds(gi * 32, 32)

    def score_one(r, carry):
        s = jnp.dot(G[r].reshape(512, WIDTH), K[r], preferred_element_type=f32) * to_log2
        s = jnp.where(key_at < len_ref[r], s, -1e30)
        S[r % 4] = s
        peak = jnp.maximum(jnp.max(s, 1, keepdims=True), -1e29)
        M[r] = jnp.broadcast_to(peak, (512, 128))
        M[r, own_rows, :] = jnp.maximum(
            M[r, own_rows, :], jnp.max(SN[pl.ds(r * 32, 32), :], 1, keepdims=True)
        )
        ml_send[r // 4, 0, pl.ds(r % 4, 1), :] = jnp.transpose(M[r])[0:1]
        return carry

    def value_one(r, carry):
        p = jnp.exp2(S[r % 4] - M[r, :, 0:1])
        pn = jnp.exp2(SN[pl.ds(r * 32, 32), :] - M[r, own_rows, 0:1])
        L[...] = jnp.broadcast_to(jnp.sum(p, 1, keepdims=True), (512, 128))
        L[own_rows, :] = L[own_rows, :] + jnp.sum(pn, 1, keepdims=True)
        O[r] = lax.dot_general(p.astype(bf), K[r, 0:KVL], nt, preferred_element_type=f32)
        O[r, own_rows, :] = O[r, own_rows, :] + jnp.dot(
            pn.astype(bf), NEW[:, :KVL], preferred_element_type=f32
        )
        sums[pl.ds(r, 1), :] = jnp.transpose(L[...])[0:1]
        return carry

    def score(first, count):
        lax.fori_loop(first, first + count, score_one, 0)

    def value(first, count):
        lax.fori_loop(first, first + count, value_one, 0)

    def butterfly(n, join):
        total = ml_send[n, 0]
        for stage, peer in ((0, p_c), (1, p_z)):
            copy = net.send(ml_send.at[n, stage], ml_recv.at[n, stage], peer)
            yield
            copy.wait_recv()
            total = join(total, ml_recv[n, stage])
            ml_send[n, stage + 1] = total
        last = net.group()
        for j, p in enumerate((p_xp, p_xm, p_x2)):
            net.send(ml_send.at[n, 2], ml_recv.at[n, 2 + j], p, group=last)
        yield
        net.arrive(last, ml_recv.at[n, 2:5])
        for j in range(3):
            total = join(total, ml_recv[n, 2 + j])
        ml_send[n, 3] = total

    def peaks(h):
        yield from butterfly(h, jnp.maximum)
        factor = jnp.exp2(ml_send[h, 0] - ml_send[h, 3])
        sums[4 * h : 4 * h + 4] = sums[4 * h : 4 * h + 4] * factor[0:4]
        SC[0:8] = factor
        SCT[h] = jnp.transpose(SC[...])
        yield

    def totals():
        ml_send[2, 0] = sums[...]
        yield from butterfly(2, jnp.add)
        SC[0:8] = ml_send[2, 3]
        SCT[2] = jnp.transpose(SC[...])
        yield

    def total_of(*terms):
        total = terms[0].astype(f32)
        for term in terms[1:]:
            total = total + term.astype(f32)
        return total

    def add(*terms):
        return total_of(*terms).astype(bf)

    def reduce(h):
        b = 4 * h
        two = pl.ds(b, 2), pl.ds(b + 2, 2)
        mate = []
        for n in range(2):
            for r in (b + 2 * n, b + 2 * n + 1):
                part = (O[r] * SCT[h, :, r - b : r - b + 1]).astype(bf)
                NB[r] = part.reshape(4, 2, 2, 32, KVL)
            mate.append(net.send(NB.at[two[n], :, :, co], RD.at[two[n]], p_c))
        yield
        mate[0].wait_recv()
        for r in (b, b + 1):
            T[r] = add(NB[r, :, :, c], RD[r])
        f0 = net.send(T.at[b, x2], RFA.at[h, 0], p_xp)
        f1 = net.send(T.at[b + 1, x2], RFA.at[h, 1], p_xm)
        near_a, near_b = net.group(), net.group()
        net.send(T.at[b + 1, xp], RLA.at[h, 1], p_xp, group=near_a)
        net.send(T.at[b, xm], RRA.at[h, 0], p_xm, group=near_a)
        mate[1].wait_recv()
        for r in (b + 2, b + 3):
            T[r] = add(NB[r, :, :, c], RD[r])
        z_b = net.send(T.at[two[1], :, zo], RZB.at[h], p_z)
        yield
        f0.wait_recv()
        T[b, xp] = add(T[b, xp], RFA[h, 0])
        net.send(T.at[b, xp], RLA.at[h, 0], p_xp, group=near_a)
        f1.wait_recv()
        T[b + 1, xm] = add(T[b + 1, xm], RFA[h, 1])
        net.send(T.at[b + 1, xm], RRA.at[h, 1], p_xm, group=near_a)
        z_b.wait_recv()
        for n in range(2):
            V[h, n] = add(T[b + 2 + n, :, zl], RZB[h, n])
        g0 = net.send(V.at[h, 0, x2], RFB.at[h, 0], p_xp)
        g1 = net.send(V.at[h, 1, x2], RFB.at[h, 1], p_xm)
        net.send(V.at[h, 1, xp], RLB.at[h, 1], p_xp, group=near_b)
        net.send(V.at[h, 0, xm], RRB.at[h, 0], p_xm, group=near_b)
        yield
        net.arrive(near_a, RLA)
        for n in range(2):
            U[h, n] = add(T[b + n, x], RLA[h, n], RRA[h, n])
        z_a = net.send(U.at[h, :, zo], RZA.at[h], p_z)
        g0.wait_recv()
        V[h, 0, xp] = add(V[h, 0, xp], RFB[h, 0])
        net.send(V.at[h, 0, xp], RLB.at[h, 0], p_xp, group=near_b)
        g1.wait_recv()
        V[h, 1, xm] = add(V[h, 1, xm], RFB[h, 1])
        net.send(V.at[h, 1, xm], RRB.at[h, 1], p_xm, group=near_b)
        yield
        z_a.wait_recv()
        F[two[0]] = total_of(U[h, :, zl], RZA[h])
        net.arrive(near_b, RLB)
        F[two[1]] = total_of(V[h, :, x], RLB[h], RRB[h])
        yield

    def values():
        partner = (di + 4) % 8
        around = [(di // 4) * 4 + (di + j) % 4 for j in range(1, 4)]
        mine = net.group()
        for p in around:
            net.send(WV.at[di], WV.at[di], p, "dp", mine)
        yield
        over = net.send(WV.at[di], WV.at[di], partner, "dp")
        yield
        over.wait_recv()
        for p in around:
            net.send(WV.at[partner], WV.at[partner], p, "dp", mine)
        yield
        net.arrive(mine, WV.at[0:6])
        yield

    gather0, gather1 = gather(0), gather(1)
    peaks0, peaks1 = peaks(0), peaks(1)
    reduce0, reduce1 = reduce(0), reduce(1)
    weights, sum_up = values(), totals()
    place(0)
    next(gather0)
    place(1)
    new_scores(0)
    new_scores(1)
    next(weights)
    next(gather0)
    next(gather0)
    next(gather1)
    next(weights)
    next(gather0)
    loads[4].wait()
    next(gather0)
    score(0, 4)
    next(peaks0)
    next(gather1)
    value(0, 2)
    next(peaks0)
    value(2, 2)
    next(gather1)
    next(peaks0)
    next(weights)
    next(gather1)
    next(peaks0)
    next(reduce0)
    next(gather1)
    score(4, 4)
    next(peaks1)
    next(reduce0)
    value(4, 1)
    next(peaks1)
    value(5, 1)
    next(peaks1)
    value(6, 1)
    next(reduce0)
    value(7, 1)
    next(peaks1)
    next(reduce1)
    next(sum_up)
    next(reduce1)
    next(sum_up)
    next(reduce0)
    next(reduce1)
    next(sum_up)
    next(reduce0)
    next(reduce1)
    next(sum_up)
    next(weights)
    next(reduce1)

    for r in range(8):
        F[r] = F[r] / SCT[2, own_rows, r : r + 1]
    latent = jnp.dot(
        MOVE[3], F[...].astype(bf).reshape(256, KVL), preferred_element_type=f32
    ).astype(bf)
    for i in range(8):
        out_ref[:, i * VDIM : (i + 1) * VDIM] = jnp.dot(
            latent[i * 32 : (i + 1) * 32], WV[i], preferred_element_type=f32
        ).astype(bf)
    net.finish()
    pltpu.make_async_copy(X.at[0:127], X.at[0:127], all_send).wait()


def per_device(query_latent, q_up, kv_up, latent_cache, new_latent, lengths):
    bf, f32 = jnp.bfloat16, jnp.float32
    pair = np.arange(128) // 2
    freq = np.where(pair < ROPE // 2, 10000.0 ** (-(2.0 * pair) / ROPE), 0.0).astype(np.float32)
    vmem = pl.BlockSpec(memory_space=pltpu.VMEM)
    out = pl.pallas_call(
        kernel,
        out_shape=jax.ShapeDtypeStruct((32, 8 * VDIM), bf),
        in_specs=[pl.BlockSpec(memory_space=pltpu.SMEM), vmem] + [pl.BlockSpec(memory_space=pl.ANY)] * 5,
        out_specs=vmem,
        scratch_shapes=[
            pltpu.VMEM((12, H * (NOPE + ROPE)), bf),
            pltpu.VMEM((4, H * (NOPE + VDIM)), bf),
            pltpu.VMEM((32, WIDTH), bf),
            pltpu.VMEM((4, 256, 256), bf),
            pltpu.VMEM((256, 32), f32),
            pltpu.VMEM((128, 32, 128), bf),
            pltpu.VMEM((128, 32, 128), bf),
            pltpu.VMEM((8, 32, QL), bf),
            pltpu.VMEM((2, QL, 128), bf),
            pltpu.VMEM((KVL, NOPE), bf),
            pltpu.VMEM((8, 32, WIDE), bf),
            pltpu.VMEM((2, 8, 16, WIDE), bf),
            pltpu.VMEM((8, KVL, VDIM), bf),
            pltpu.VMEM((8, 16, 32, WIDTH), bf),
            pltpu.VMEM((8, WIDTH, 512), bf),
            pltpu.VMEM((8, 512, KVL), f32),
            pltpu.VMEM((8, 4, 2, 2, 32, KVL), bf),
            pltpu.VMEM((8, 4, 2, 32, KVL), bf),
            pltpu.VMEM((8, 4, 2, 32, KVL), bf),
            pltpu.VMEM((2, 2, 4, 32, KVL), bf),
            pltpu.VMEM((2, 2, 2, 32, KVL), bf),
            pltpu.VMEM((2, 2, 2, 32, KVL), bf),
            pltpu.VMEM((2, 2, 2, 32, KVL), bf),
            pltpu.VMEM((2, 2, 2, 32, KVL), bf),
            pltpu.VMEM((2, 2, 32, KVL), bf),
            pltpu.VMEM((2, 2, 32, KVL), bf),
            pltpu.VMEM((2, 2, 32, KVL), bf),
            pltpu.VMEM((2, 2, 32, KVL), bf),
            pltpu.VMEM((2, 2, 4, 32, KVL), bf),
            pltpu.VMEM((4, 512, 512), f32),
            pltpu.VMEM((8, 512, 128), f32),
            pltpu.VMEM((512, 128), f32),
            pltpu.VMEM((8, 512), f32),
            pltpu.VMEM((3, 4, 8, 512), f32),
            pltpu.VMEM((3, 5, 8, 512), f32),
            pltpu.VMEM((128, 512), f32),
            pltpu.VMEM((3, 512, 128), f32),
            pltpu.VMEM((8, 32, KVL), f32),
            pltpu.SemaphoreType.DMA((POOL,)),
            pltpu.SemaphoreType.DMA((GROUPS,)),
            pltpu.SemaphoreType.DMA((5,)),
            pltpu.SemaphoreType.DMA,
            pltpu.SemaphoreType.DMA,
        ],
        compiler_params=pltpu.CompilerParams(
            collective_id=1, has_side_effects=True, vmem_limit_bytes=60 * 1024 * 1024
        ),
    )(
        lengths, jnp.asarray(freq)[None], query_latent.reshape(32, QL), q_up, kv_up,
        latent_cache.transpose(0, 2, 1), new_latent.reshape(32, WIDTH),
    )
    return out.reshape(STEPS, 8, 8 * VDIM)


def solution(mesh):
    return jax.shard_map(
        per_device,
        mesh=mesh,
        in_specs=(
            P(None, "dp", None),
            P(("dp", "grp"), None),
            P(("dp", "grp"), None),
            P("dp", "grp", None),
            P(None, "dp", None),
            P("dp"),
        ),
        out_specs=P(None, "dp", "grp"),
        check_vma=False,
    )
```

```python
import jax
import jax.numpy as jnp
import numpy as np
from jax import lax
from jax.experimental import pallas as pl
from jax.experimental.pallas import tpu as pltpu
from jax.sharding import PartitionSpec as P

MESH = pl.DeviceIdType.MESH

H = 128
QL = 1536
KVL = 512
NOPE = 128
ROPE = 64
VDIM = 128
STEPS = 4
WIDTH = KVL + ROPE
WIDE = KVL + 128
LOG2E = 1.4426950408889634
POOL = 40
GROUPS = 73


class Copies:
    def __init__(self, send_sem, recv_sem):
        self.send_sem, self.recv_sem, self.sent, self.groups = send_sem, recv_sem, [], 0

    def group(self):
        self.groups += 1
        assert self.groups <= GROUPS
        return self.groups - 1

    def send(self, src, dst, peer, axis="grp", group=None):
        k = len(self.sent)
        if k >= POOL:
            self.sent[k - POOL].wait_send()
        copy = pltpu.make_async_remote_copy(
            src_ref=src,
            dst_ref=dst,
            send_sem=self.send_sem.at[k % POOL],
            recv_sem=self.recv_sem.at[self.group() if group is None else group],
            device_id={axis: peer},
            device_id_type=MESH,
        )
        copy.start()
        self.sent.append(copy)
        return copy

    def arrive(self, group, like):
        pltpu.make_async_copy(like, like, self.recv_sem.at[group]).wait()

    def finish(self):
        for copy in self.sent[-POOL:]:
            copy.wait_send()


def kernel(
    len_ref, freq_ref, ql_ref, q_ref, kv_ref, cache_ref, new_ref, out_ref,
    QIN, KVIN, NEW, MOVE, SN, X, LAND, QLS, W, KC, E, QR, WV,
    G, K, O, NB, RD, T, V, U, RFA, RLA, RRA, RZA, RFB, RLB, RRB, RZB, S, M, L, sums, ml_send, ml_recv, SC, SCT, F,
    send_sem, recv_sem, load_sem, all_send, all_recv,
):
    di, gi = lax.axis_index("dp"), lax.axis_index("grp")
    me = di * 16 + gi
    x, zl, c = gi // 4, (gi // 2) % 2, gi % 2
    xp, xm, x2 = (x + 1) % 4, (x + 3) % 4, (x + 2) % 4
    zo, co = 1 - zl, 1 - c

    def at(xx, zz, cc):
        return xx * 4 + zz * 2 + cc

    p_xp, p_xm, p_x2 = at(xp, zl, c), at(xm, zl, c), at(x2, zl, c)
    p_z, p_c = at(x, zo, c), at(x, zl, co)

    loads = [
        pltpu.make_async_copy(src, dst, load_sem.at[n])
        for n, (src, dst) in enumerate(
            ((q_ref, QIN), (kv_ref, KVIN), (ql_ref, QLS.at[0]), (new_ref, NEW), (cache_ref, K))
        )
    ]
    for load in loads:
        load.start()
    barrier = pltpu.get_barrier_semaphore()

    def there(j):
        d = (me + 37 * j) % 128
        return d // 16, d % 16

    def greet(j, carry):
        dd, gg = there(j)
        pl.semaphore_signal(
            barrier, inc=1, device_id={"dp": dd, "grp": gg}, device_id_type=MESH
        )
        return carry

    lax.fori_loop(1, 128, greet, 0)
    bf, f32 = jnp.bfloat16, jnp.float32
    nt = (((1,), (1,)), ((), ()))

    loads[0].wait()
    loads[1].wait()

    def pack(p, carry):
        def tiles(upper, lower):
            a = QIN[:, pl.ds(pl.multiple_of(upper * 128, 128), 128)]
            b = KVIN[:, pl.ds(pl.multiple_of(lower * 128, 128), 128)]
            return jnp.concatenate([a, b], 0)

        X[2 * p, 0:16] = tiles(3 * p, 4 * p)
        X[2 * p, 16:32] = tiles(3 * p + 1, 4 * p + 1)
        X[2 * p + 1, 0:16] = tiles(3 * p + 1, 4 * p + 2)
        X[2 * p + 1, 16:32] = tiles(3 * p + 2, 4 * p + 3)
        return carry

    lax.fori_loop(0, 64, pack, 0)
    LAND[me] = X[8 * gi + di]
    loads[2].wait()
    pl.semaphore_wait(barrier, 127)

    net = Copies(send_sem, recv_sem)
    rows = pl.ds(pl.multiple_of(c * 16, 16), 16)
    first = net.group()
    for j in range(1, 8):
        net.send(QLS.at[0, rows], QLS.at[8 - j, rows], (di + j) % 8, "dp", first)

    def deal(j, carry):
        dd, gg = there(j)
        pltpu.make_async_remote_copy(
            src_ref=X.at[8 * gg + dd],
            dst_ref=LAND.at[me],
            send_sem=all_send,
            recv_sem=all_recv,
            device_id={"dp": dd, "grp": gg},
            device_id_type=MESH,
        ).start()
        return carry

    lax.fori_loop(1, 128, deal, 0)

    to = lax.broadcasted_iota(jnp.int32, (256, 256), 0)
    was = lax.broadcasted_iota(jnp.int32, (256, 256), 1)
    within = jnp.where(to < 96, to, to - 96)
    twelve = jnp.where(to < 96, to, to - 80)
    for n in range(1, 8):
        twelve = twelve + jnp.where(within >= 12 * n, 20, 0)
    four = 32 * ((to % 32) // 4) + to % 4 + jnp.where(to < 224, 12, 28)
    half = to - to % 32 + ((to % 16) // 4) * 8 + ((to % 32) // 16) * 4 + to % 4
    MOVE[0] = (was == jnp.where(to < 192, twelve, four)).astype(f32).astype(bf)
    MOVE[1] = (was == half).astype(f32).astype(bf)
    MOVE[2] = (was == ((to // 4) % 8) * 16 + (to % 4) * 4 + to // 32).astype(f32).astype(bf)
    MOVE[3] = (was == (to % 8) * 32 + to // 8).astype(f32).astype(bf)
    SC[...] = jnp.zeros_like(SC)
    ml_send[...] = jnp.zeros_like(ml_send)

    row = lax.broadcasted_iota(jnp.int32, (16, 128), 0)
    sign = jnp.where(lax.broadcasted_iota(jnp.int32, (16, 128), 1) % 2 == 0, -1.0, 1.0)
    turns = []
    for h in range(2):
        position = row // 4
        for r in range(4):
            position = position + jnp.where(row % 4 == r, len_ref[4 * h + r], 0)
        angle = position.astype(f32) * freq_ref[...]
        turns.append((jnp.cos(angle), sign * jnp.sin(angle)))

    net.arrive(first, QLS.at[1:8, rows])
    net.send(QLS.at[1:8, rows], QLS.at[1:8, rows], p_c).wait_recv()
    pltpu.make_async_copy(LAND.at[0:127], LAND.at[0:127], all_recv).wait()

    for b in range(16):
        block = jnp.dot(
            MOVE[0], LAND[8 * b : 8 * b + 8].reshape(256, 128), preferred_element_type=f32
        ).astype(bf)
        W[0, 96 * b : 96 * b + 96] = block[0:96]
        W[1, 96 * b : 96 * b + 96] = block[96:192]
        KC[32 * b : 32 * b + 32] = block[192:224]
        WV[di, 32 * b : 32 * b + 32] = block[224:256]
    latent_in = QLS[...].reshape(256, QL)
    qa = jnp.dot(latent_in, W[0], preferred_element_type=f32).astype(bf)
    qb = jnp.dot(latent_in, W[1], preferred_element_type=f32).astype(bf)
    qa = jnp.dot(MOVE[1], qa, preferred_element_type=f32)
    qb = jnp.dot(MOVE[1], qb, preferred_element_type=f32)
    ra, rb = pltpu.roll(qa, 64, 1), pltpu.roll(qb, 64, 1)
    lane = lax.broadcasted_iota(jnp.int32, (256, 128), 1)
    odd = di % 2 == 1
    plain = jnp.where(odd, jnp.where(lane < 64, ra, rb), qa).astype(bf)
    rotary = jnp.where(lane < 64, jnp.where(odd, rb, qb), 0.0).astype(bf)
    absorbed = lax.dot_general(plain, KC[...], nt, preferred_element_type=f32).astype(bf)
    E[:, :, 0:KVL] = absorbed.reshape(8, 32, KVL)
    E[:, :, KVL:WIDE] = rotary.reshape(8, 32, 128)
    heads = []
    for h in range(2):
        span = pl.ds(16 * h, 16)
        heads.append(net.group())
        for j in range(1, 8):
            net.send(E.at[j, span], QR.at[h, di], (di + j) % 8, "dp", heads[h])
        QR[h, di] = E[0, span]
    loads[3].wait()
    to_log2 = float(NOPE + ROPE) ** -0.5 * LOG2E

    def place(h):
        net.arrive(heads[h], QR.at[h, 0:7])
        span = pl.ds(4 * h, 4)
        rotary = QR[h, :, :, KVL:WIDE].reshape(128, 128).astype(f32)
        even = lax.broadcasted_iota(jnp.int32, (128, 128), 1) % 2 == 0
        other = jnp.where(even, pltpu.roll(rotary, 127, 1), pltpu.roll(rotary, 1, 1))
        cosine, sine = turns[h]
        rotary = rotary.reshape(8, 16, 128) * cosine[None] + other.reshape(8, 16, 128) * sine[None]
        move = MOVE[2, 0:128, 0:128]
        absorbed = jnp.dot(move, QR[h, :, :, 0:KVL].reshape(128, KVL), preferred_element_type=f32)
        rotary = jnp.dot(move, rotary.reshape(128, 128).astype(bf), preferred_element_type=f32)
        G[span, pl.ds(gi, 1), :, 0:KVL] = absorbed.astype(bf).reshape(4, 1, 32, KVL)
        G[span, pl.ds(gi, 1), :, KVL:WIDTH] = rotary[:, :ROPE].astype(bf).reshape(4, 1, 32, ROPE)

    def new_scores(h):
        query = lax.broadcasted_iota(jnp.int32, (128, 32), 0)
        key = lax.broadcasted_iota(jnp.int32, (128, 32), 1)
        live = (key % 8 == 4 * h + query // 32) & (key // 8 <= query % 4)
        score = lax.dot_general(
            G[pl.ds(4 * h, 4), pl.ds(gi, 1)].reshape(128, WIDTH), NEW[...], nt,
            preferred_element_type=f32,
        )
        SN[pl.ds(128 * h, 128)] = jnp.where(live, score * to_log2, -1e30)

    def gather(h):
        b = 4 * h
        A, B = (b, 2), (b + 2, 2)
        s_l, s_r, s_z = p_xm, p_xp, p_z
        s_lz, s_rz, s_f, s_fz = at(xm, zo, c), at(xp, zo, c), p_x2, at(x2, zo, c)

        def go(span, slot, peer, group=None):
            block = G.at[pl.ds(span[0], span[1]), slot]
            return net.send(block, block, peer, group=group)

        mate, far, far_a, far_b = net.group(), net.group(), net.group(), net.group()

        def share(span, slot):
            go(span, slot, p_c, mate)

        z_a = go(A, gi, p_z)
        l_b, r_b = go(B, gi, p_xp), go(B, gi, p_xm)
        l_a, r_a = go(A, gi, p_xp), go(A, gi, p_xm)
        share((b, 4), gi)
        z_b = go(B, gi, p_z)
        yield
        z_a.wait_recv()
        lz_a, rz_a = go(A, s_z, p_xp), go(A, s_z, p_xm)
        share(A, s_z)
        l_b.wait_recv()
        f0_b, lz_b = go((b + 2, 1), s_l, p_xp), go(B, s_l, p_z)
        share(B, s_l)
        r_b.wait_recv()
        f1_b, rz_b = go((b + 3, 1), s_r, p_xm), go(B, s_r, p_z)
        share(B, s_r)
        l_a.wait_recv()
        go((b, 1), s_l, p_xp, far)
        share(A, s_l)
        r_a.wait_recv()
        go((b + 1, 1), s_r, p_xm, far)
        share(A, s_r)
        yield
        lz_a.wait_recv()
        go((b, 1), s_lz, p_xp, far_a)
        share(A, s_lz)
        rz_a.wait_recv()
        go((b + 1, 1), s_rz, p_xm, far_a)
        share(A, s_rz)
        f0_b.wait_recv()
        go((b + 2, 1), s_f, p_z, far_b)
        f1_b.wait_recv()
        go((b + 3, 1), s_f, p_z, far_b)
        share(B, s_f)
        net.arrive(far, G.at[pl.ds(b, 2), 0])
        share(A, s_f)
        yield
        z_b.wait_recv()
        share(B, s_z)
        lz_b.wait_recv()
        share(B, s_lz)
        rz_b.wait_recv()
        share(B, s_rz)
        net.arrive(far_a, G.at[pl.ds(b, 2), 0])
        share(A, s_fz)
        net.arrive(far_b, G.at[pl.ds(b, 2), 0])
        share(B, s_fz)
        yield
        net.arrive(mate, G.at[pl.ds(b, 4), 0:8])
        yield

    lanes = lax.broadcasted_iota(jnp.int32, (512, 128), 1)
    key_at = lax.broadcasted_iota(jnp.int32, (1, 512), 1) + gi * 512
    own_rows = pl.ds(gi * 32, 32)

    def score_one(r, carry):
        s = jnp.dot(G[r].reshape(512, WIDTH), K[r], preferred_element_type=f32) * to_log2
        s = jnp.where(key_at < len_ref[r], s, -1e30)
        S[r % 4] = s
        peak = jnp.maximum(jnp.max(s, 1, keepdims=True), -1e29)
        M[r] = jnp.broadcast_to(peak, (512, 128))
        M[r, own_rows, :] = jnp.maximum(
            M[r, own_rows, :], jnp.max(SN[pl.ds(r * 32, 32), :], 1, keepdims=True)
        )
        ml_send[r // 4, 0, pl.ds(r % 4, 1), :] = jnp.transpose(M[r])[0:1]
        return carry

    def value_one(r, carry):
        p = jnp.exp2(S[r % 4] - M[r, :, 0:1])
        pn = jnp.exp2(SN[pl.ds(r * 32, 32), :] - M[r, own_rows, 0:1])
        L[...] = jnp.broadcast_to(jnp.sum(p, 1, keepdims=True), (512, 128))
        L[own_rows, :] = L[own_rows, :] + jnp.sum(pn, 1, keepdims=True)
        O[r] = lax.dot_general(p.astype(bf), K[r, 0:KVL], nt, preferred_element_type=f32)
        O[r, own_rows, :] = O[r, own_rows, :] + jnp.dot(
            pn.astype(bf), NEW[:, :KVL], preferred_element_type=f32
        )
        sums[pl.ds(r, 1), :] = jnp.transpose(L[...])[0:1]
        return carry

    def score(first, count):
        lax.fori_loop(first, first + count, score_one, 0)

    def value(first, count):
        lax.fori_loop(first, first + count, value_one, 0)

    def butterfly(n, join):
        total = ml_send[n, 0]
        for stage, peer in ((0, p_c), (1, p_z)):
            copy = net.send(ml_send.at[n, stage], ml_recv.at[n, stage], peer)
            yield
            copy.wait_recv()
            total = join(total, ml_recv[n, stage])
            ml_send[n, stage + 1] = total
        last = net.group()
        for j, p in enumerate((p_xp, p_xm, p_x2)):
            net.send(ml_send.at[n, 2], ml_recv.at[n, 2 + j], p, group=last)
        yield
        net.arrive(last, ml_recv.at[n, 2:5])
        for j in range(3):
            total = join(total, ml_recv[n, 2 + j])
        ml_send[n, 3] = total

    def peaks(h):
        yield from butterfly(h, jnp.maximum)
        factor = jnp.exp2(ml_send[h, 0] - ml_send[h, 3])
        sums[4 * h : 4 * h + 4] = sums[4 * h : 4 * h + 4] * factor[0:4]
        SC[0:8] = factor
        SCT[h] = jnp.transpose(SC[...])
        yield

    def totals():
        ml_send[2, 0] = sums[...]
        yield from butterfly(2, jnp.add)
        SC[0:8] = ml_send[2, 3]
        SCT[2] = jnp.transpose(SC[...])
        yield

    def total_of(*terms):
        total = terms[0].astype(f32)
        for term in terms[1:]:
            total = total + term.astype(f32)
        return total

    def add(*terms):
        return total_of(*terms).astype(bf)

    def reduce(h):
        b = 4 * h
        A, B = pl.ds(b, 2), pl.ds(b + 2, 2)
        near_a, near_b = net.group(), net.group()
        mate = {}
        for first in (b + 2, b):
            for r in (first, first + 1):
                part = (O[r] * SCT[h, :, r - b : r - b + 1]).astype(bf)
                NB[r] = part.reshape(4, 2, 2, 32, KVL)
            span = pl.ds(first, 2)
            mate[first] = net.send(NB.at[span, :, :, co], RD.at[span], p_c)
        yield
        mate[b + 2].wait_recv()
        for r in (b + 2, b + 3):
            T[r] = add(NB[r, :, :, c], RD[r])
        over = [net.send(T.at[B, xx, zo], RZB.at[h, :, xx], p_z) for xx in (x2, xp, xm, x)]
        mate[b].wait_recv()
        for r in (b, b + 1):
            T[r] = add(NB[r, :, :, c], RD[r])
        f0 = net.send(T.at[b, x2], RFA.at[h, 0], p_xp)
        f1 = net.send(T.at[b + 1, x2], RFA.at[h, 1], p_xm)
        net.send(T.at[b + 1, xp], RLA.at[h, 1], p_xp, group=near_a)
        net.send(T.at[b, xm], RRA.at[h, 0], p_xm, group=near_a)
        yield
        over[0].wait_recv()
        V[h, :, x2] = add(T[B, x2, zl], RZB[h, :, x2])
        g0 = net.send(V.at[h, 0, x2], RFB.at[h, 0], p_xp)
        g1 = net.send(V.at[h, 1, x2], RFB.at[h, 1], p_xm)
        f0.wait_recv()
        T[b, xp] = add(T[b, xp], RFA[h, 0])
        net.send(T.at[b, xp], RLA.at[h, 0], p_xp, group=near_a)
        f1.wait_recv()
        T[b + 1, xm] = add(T[b + 1, xm], RFA[h, 1])
        net.send(T.at[b + 1, xm], RRA.at[h, 1], p_xm, group=near_a)
        yield
        over[1].wait_recv()
        V[h, :, xp] = add(T[B, xp, zl], RZB[h, :, xp])
        net.send(V.at[h, 1, xp], RLB.at[h, 1], p_xp, group=near_b)
        over[2].wait_recv()
        V[h, :, xm] = add(T[B, xm, zl], RZB[h, :, xm])
        net.send(V.at[h, 0, xm], RRB.at[h, 0], p_xm, group=near_b)
        g0.wait_recv()
        V[h, 0, xp] = add(V[h, 0, xp], RFB[h, 0])
        net.send(V.at[h, 0, xp], RLB.at[h, 0], p_xp, group=near_b)
        g1.wait_recv()
        V[h, 1, xm] = add(V[h, 1, xm], RFB[h, 1])
        net.send(V.at[h, 1, xm], RRB.at[h, 1], p_xm, group=near_b)
        yield
        net.arrive(near_a, RLA)
        for n in range(2):
            U[h, n] = add(T[b + n, x], RLA[h, n], RRA[h, n])
        z_a = net.send(U.at[h, :, zo], RZA.at[h], p_z)
        over[3].wait_recv()
        V[h, :, x] = add(T[B, x, zl], RZB[h, :, x])
        yield
        z_a.wait_recv()
        F[A] = total_of(U[h, :, zl], RZA[h])
        net.arrive(near_b, RLB)
        F[B] = total_of(V[h, :, x], RLB[h], RRB[h])
        yield

    def values():
        partner = (di + 4) % 8
        around = [(di // 4) * 4 + (di + j) % 4 for j in range(1, 4)]
        mine = net.group()
        for p in around:
            net.send(WV.at[di], WV.at[di], p, "dp", mine)
        yield
        over = net.send(WV.at[di], WV.at[di], partner, "dp")
        yield
        over.wait_recv()
        for p in around:
            net.send(WV.at[partner], WV.at[partner], p, "dp", mine)
        yield
        net.arrive(mine, WV.at[0:6])
        yield

    gather0, gather1 = gather(0), gather(1)
    peaks0, peaks1 = peaks(0), peaks(1)
    reduce0, reduce1 = reduce(0), reduce(1)
    weights, sum_up = values(), totals()
    place(0)
    next(gather0)
    place(1)
    new_scores(0)
    new_scores(1)
    next(weights)
    next(gather0)
    next(gather0)
    next(gather1)
    next(weights)
    next(gather0)
    loads[4].wait()
    next(gather0)
    score(0, 4)
    next(peaks0)
    next(gather1)
    value(0, 2)
    next(peaks0)
    value(2, 2)
    next(gather1)
    next(peaks0)
    next(weights)
    next(gather1)
    next(peaks0)
    next(reduce0)
    next(gather1)
    score(4, 2)
    next(reduce0)
    score(6, 2)
    next(peaks1)
    value(4, 1)
    next(peaks1)
    value(5, 1)
    next(reduce0)
    value(6, 1)
    next(peaks1)
    value(7, 1)
    next(reduce0)
    next(peaks1)
    next(reduce1)
    next(sum_up)
    next(reduce0)
    next(reduce1)
    next(sum_up)
    next(reduce0)
    next(reduce1)
    next(sum_up)
    next(reduce1)
    next(sum_up)
    next(reduce1)
    next(weights)
    next(reduce1)

    for r in range(8):
        F[r] = F[r] / SCT[2, own_rows, r : r + 1]
    latent = jnp.dot(
        MOVE[3], F[...].astype(bf).reshape(256, KVL), preferred_element_type=f32
    ).astype(bf)
    for i in range(8):
        out_ref[:, i * VDIM : (i + 1) * VDIM] = jnp.dot(
            latent[i * 32 : (i + 1) * 32], WV[i], preferred_element_type=f32
        ).astype(bf)
    net.finish()
    pltpu.make_async_copy(X.at[0:127], X.at[0:127], all_send).wait()


def per_device(query_latent, q_up, kv_up, latent_cache, new_latent, lengths):
    bf, f32 = jnp.bfloat16, jnp.float32
    pair = np.arange(128) // 2
    freq = np.where(pair < ROPE // 2, 10000.0 ** (-(2.0 * pair) / ROPE), 0.0).astype(np.float32)
    vmem = pl.BlockSpec(memory_space=pltpu.VMEM)
    out = pl.pallas_call(
        kernel,
        out_shape=jax.ShapeDtypeStruct((32, 8 * VDIM), bf),
        in_specs=[pl.BlockSpec(memory_space=pltpu.SMEM), vmem] + [pl.BlockSpec(memory_space=pl.ANY)] * 5,
        out_specs=vmem,
        scratch_shapes=[
            pltpu.VMEM((12, H * (NOPE + ROPE)), bf),
            pltpu.VMEM((4, H * (NOPE + VDIM)), bf),
            pltpu.VMEM((32, WIDTH), bf),
            pltpu.VMEM((4, 256, 256), bf),
            pltpu.VMEM((256, 32), f32),
            pltpu.VMEM((128, 32, 128), bf),
            pltpu.VMEM((128, 32, 128), bf),
            pltpu.VMEM((8, 32, QL), bf),
            pltpu.VMEM((2, QL, 128), bf),
            pltpu.VMEM((KVL, NOPE), bf),
            pltpu.VMEM((8, 32, WIDE), bf),
            pltpu.VMEM((2, 8, 16, WIDE), bf),
            pltpu.VMEM((8, KVL, VDIM), bf),
            pltpu.VMEM((8, 16, 32, WIDTH), bf),
            pltpu.VMEM((8, WIDTH, 512), bf),
            pltpu.VMEM((8, 512, KVL), f32),
            pltpu.VMEM((8, 4, 2, 2, 32, KVL), bf),
            pltpu.VMEM((8, 4, 2, 32, KVL), bf),
            pltpu.VMEM((8, 4, 2, 32, KVL), bf),
            pltpu.VMEM((2, 2, 4, 32, KVL), bf),
            pltpu.VMEM((2, 2, 2, 32, KVL), bf),
            pltpu.VMEM((2, 2, 2, 32, KVL), bf),
            pltpu.VMEM((2, 2, 2, 32, KVL), bf),
            pltpu.VMEM((2, 2, 2, 32, KVL), bf),
            pltpu.VMEM((2, 2, 32, KVL), bf),
            pltpu.VMEM((2, 2, 32, KVL), bf),
            pltpu.VMEM((2, 2, 32, KVL), bf),
            pltpu.VMEM((2, 2, 32, KVL), bf),
            pltpu.VMEM((2, 2, 4, 32, KVL), bf),
            pltpu.VMEM((4, 512, 512), f32),
            pltpu.VMEM((8, 512, 128), f32),
            pltpu.VMEM((512, 128), f32),
            pltpu.VMEM((8, 512), f32),
            pltpu.VMEM((3, 4, 8, 512), f32),
            pltpu.VMEM((3, 5, 8, 512), f32),
            pltpu.VMEM((128, 512), f32),
            pltpu.VMEM((3, 512, 128), f32),
            pltpu.VMEM((8, 32, KVL), f32),
            pltpu.SemaphoreType.DMA((POOL,)),
            pltpu.SemaphoreType.DMA((GROUPS,)),
            pltpu.SemaphoreType.DMA((5,)),
            pltpu.SemaphoreType.DMA,
            pltpu.SemaphoreType.DMA,
        ],
        compiler_params=pltpu.CompilerParams(
            collective_id=1, has_side_effects=True, vmem_limit_bytes=60 * 1024 * 1024
        ),
    )(
        lengths, jnp.asarray(freq)[None], query_latent.reshape(32, QL), q_up, kv_up,
        latent_cache.transpose(0, 2, 1), new_latent.reshape(32, WIDTH),
    )
    return out.reshape(STEPS, 8, 8 * VDIM)


def solution(mesh):
    return jax.shard_map(
        per_device,
        mesh=mesh,
        in_specs=(
            P(None, "dp", None),
            P(("dp", "grp"), None),
            P(("dp", "grp"), None),
            P("dp", "grp", None),
            P(None, "dp", None),
            P("dp"),
        ),
        out_specs=P(None, "dp", "grp"),
        check_vma=False,
    )
```

```python
import jax
import jax.numpy as jnp
import numpy as np
from jax import lax
from jax.experimental import pallas as pl
from jax.experimental.pallas import tpu as pltpu
from jax.sharding import PartitionSpec as P

MESH = pl.DeviceIdType.MESH

H = 128
QL = 1536
KVL = 512
NOPE = 128
ROPE = 64
VDIM = 128
STEPS = 4
WIDTH = KVL + ROPE
WIDE = KVL + 128
LOG2E = 1.4426950408889634
POOL = 40
GROUPS = 70


class Copies:
    def __init__(self, send_sem, recv_sem):
        self.send_sem, self.recv_sem, self.sent, self.groups = send_sem, recv_sem, [], 0

    def group(self):
        self.groups += 1
        assert self.groups <= GROUPS
        return self.groups - 1

    def send(self, src, dst, peer, axis="grp", group=None):
        k = len(self.sent)
        if k >= POOL:
            self.sent[k - POOL].wait_send()
        copy = pltpu.make_async_remote_copy(
            src_ref=src,
            dst_ref=dst,
            send_sem=self.send_sem.at[k % POOL],
            recv_sem=self.recv_sem.at[self.group() if group is None else group],
            device_id={axis: peer},
            device_id_type=MESH,
        )
        copy.start()
        self.sent.append(copy)
        return copy

    def arrive(self, group, like):
        pltpu.make_async_copy(like, like, self.recv_sem.at[group]).wait()

    def finish(self):
        for copy in self.sent[-POOL:]:
            copy.wait_send()


def kernel(
    len_ref, freq_ref, ql_ref, q_ref, kv_ref, cache_ref, new_ref, out_ref,
    QIN, KVIN, NEW, MOVE, SN, X, LAND, QLS, W, KC, E, QR, WV,
    G, K, KR, O, NB, RD, T, V, U, RFA, RLA, RRA, RZA, RFB, RLB, RRB, RZB, S, M, L, sums, ml_send, ml_recv, SC, SCT, F,
    send_sem, recv_sem, load_sem, all_send, all_recv,
):
    di, gi = lax.axis_index("dp"), lax.axis_index("grp")
    me = di * 16 + gi
    x, zl, c = gi // 4, (gi // 2) % 2, gi % 2
    xp, xm, x2 = (x + 1) % 4, (x + 3) % 4, (x + 2) % 4
    zo, co = 1 - zl, 1 - c

    def at(xx, zz, cc):
        return xx * 4 + zz * 2 + cc

    p_xp, p_xm, p_x2 = at(xp, zl, c), at(xm, zl, c), at(x2, zl, c)
    p_z, p_c = at(x, zo, c), at(x, zl, co)

    loads = [
        pltpu.make_async_copy(src, dst, load_sem.at[n])
        for n, (src, dst) in enumerate(
            ((q_ref, QIN), (kv_ref, KVIN), (ql_ref, QLS.at[0]), (new_ref, NEW), (cache_ref, K))
        )
    ]
    for load in loads:
        load.start()
    barrier = pltpu.get_barrier_semaphore()

    def there(j):
        d = (me + 37 * j) % 128
        return d // 16, d % 16

    def greet(j, carry):
        dd, gg = there(j)
        pl.semaphore_signal(
            barrier, inc=1, device_id={"dp": dd, "grp": gg}, device_id_type=MESH
        )
        return carry

    lax.fori_loop(1, 128, greet, 0)
    bf, f32 = jnp.bfloat16, jnp.float32
    nt = (((1,), (1,)), ((), ()))

    loads[0].wait()
    loads[1].wait()

    def pack(p, carry):
        def tiles(upper, lower):
            a = QIN[:, pl.ds(pl.multiple_of(upper * 128, 128), 128)]
            b = KVIN[:, pl.ds(pl.multiple_of(lower * 128, 128), 128)]
            return jnp.concatenate([a, b], 0)

        X[2 * p, 0:16] = tiles(3 * p, 4 * p)
        X[2 * p, 16:32] = tiles(3 * p + 1, 4 * p + 1)
        X[2 * p + 1, 0:16] = tiles(3 * p + 1, 4 * p + 2)
        X[2 * p + 1, 16:32] = tiles(3 * p + 2, 4 * p + 3)
        return carry

    lax.fori_loop(0, 64, pack, 0)
    LAND[me] = X[8 * gi + di]
    loads[2].wait()
    pl.semaphore_wait(barrier, 127)

    net = Copies(send_sem, recv_sem)
    rows = pl.ds(pl.multiple_of(c * 16, 16), 16)
    first = net.group()
    for j in range(1, 8):
        net.send(QLS.at[0, rows], QLS.at[8 - j, rows], (di + j) % 8, "dp", first)

    def deal(j, carry):
        dd, gg = there(j)
        pltpu.make_async_remote_copy(
            src_ref=X.at[8 * gg + dd],
            dst_ref=LAND.at[me],
            send_sem=all_send,
            recv_sem=all_recv,
            device_id={"dp": dd, "grp": gg},
            device_id_type=MESH,
        ).start()
        return carry

    lax.fori_loop(1, 128, deal, 0)

    to = lax.broadcasted_iota(jnp.int32, (256, 256), 0)
    was = lax.broadcasted_iota(jnp.int32, (256, 256), 1)
    within = jnp.where(to < 96, to, to - 96)
    twelve = jnp.where(to < 96, to, to - 80)
    for n in range(1, 8):
        twelve = twelve + jnp.where(within >= 12 * n, 20, 0)
    four = 32 * ((to % 32) // 4) + to % 4 + jnp.where(to < 224, 12, 28)
    half = to - to % 32 + ((to % 16) // 4) * 8 + ((to % 32) // 16) * 4 + to % 4
    MOVE[0] = (was == jnp.where(to < 192, twelve, four)).astype(f32).astype(bf)
    MOVE[1] = (was == half).astype(f32).astype(bf)
    MOVE[2] = (was == ((to // 4) % 8) * 16 + (to % 4) * 4 + to // 32).astype(f32).astype(bf)
    MOVE[3] = (was == (to % 8) * 32 + to // 8).astype(f32).astype(bf)
    loads[4].wait()
    for r in range(8):
        KR[r, ROPE * (r % 2) : ROPE * (r % 2) + ROPE] = K[r, KVL:WIDTH]
        KR[r, ROPE * (1 - r % 2) : ROPE * (1 - r % 2) + ROPE] = jnp.zeros((ROPE, 512), bf)
    SC[...] = jnp.zeros_like(SC)
    ml_send[...] = jnp.zeros_like(ml_send)

    row = lax.broadcasted_iota(jnp.int32, (16, 128), 0)
    sign = jnp.where(lax.broadcasted_iota(jnp.int32, (16, 128), 1) % 2 == 0, -1.0, 1.0)
    turns = []
    for h in range(2):
        position = row // 4
        for r in range(4):
            position = position + jnp.where(row % 4 == r, len_ref[4 * h + r], 0)
        angle = position.astype(f32) * freq_ref[...]
        turns.append((jnp.cos(angle), sign * jnp.sin(angle)))

    net.arrive(first, QLS.at[1:8, rows])
    net.send(QLS.at[1:8, rows], QLS.at[1:8, rows], p_c).wait_recv()
    pltpu.make_async_copy(LAND.at[0:127], LAND.at[0:127], all_recv).wait()

    for b in range(16):
        block = jnp.dot(
            MOVE[0], LAND[8 * b : 8 * b + 8].reshape(256, 128), preferred_element_type=f32
        ).astype(bf)
        W[0, 96 * b : 96 * b + 96] = block[0:96]
        W[1, 96 * b : 96 * b + 96] = block[96:192]
        KC[32 * b : 32 * b + 32] = block[192:224]
        WV[di, 32 * b : 32 * b + 32] = block[224:256]
    latent_in = QLS[...].reshape(256, QL)
    qa = jnp.dot(latent_in, W[0], preferred_element_type=f32).astype(bf)
    qb = jnp.dot(latent_in, W[1], preferred_element_type=f32).astype(bf)
    qa = jnp.dot(MOVE[1], qa, preferred_element_type=f32)
    qb = jnp.dot(MOVE[1], qb, preferred_element_type=f32)
    ra, rb = pltpu.roll(qa, 64, 1), pltpu.roll(qb, 64, 1)
    lane = lax.broadcasted_iota(jnp.int32, (256, 128), 1)
    odd = di % 2 == 1
    plain = jnp.where(odd, jnp.where(lane < 64, ra, rb), qa).astype(bf)
    rotary = jnp.where(lane < 64, jnp.where(odd, rb, qb), 0.0).astype(bf)
    absorbed = lax.dot_general(plain, KC[...], nt, preferred_element_type=f32).astype(bf)
    E[:, :, 0:KVL] = absorbed.reshape(8, 32, KVL)
    E[:, :, KVL:WIDE] = rotary.reshape(8, 32, 128)
    heads = []
    for h in range(2):
        span = pl.ds(16 * h, 16)
        heads.append(net.group())
        for j in range(1, 8):
            net.send(E.at[j, span], QR.at[h, di], (di + j) % 8, "dp", heads[h])
        QR[h, di] = E[0, span]
    loads[3].wait()
    to_log2 = float(NOPE + ROPE) ** -0.5 * LOG2E

    def place(h):
        net.arrive(heads[h], QR.at[h, 0:7])
        span = pl.ds(4 * h, 4)
        rotary = QR[h, :, :, KVL:WIDE].reshape(128, 128).astype(f32)
        even = lax.broadcasted_iota(jnp.int32, (128, 128), 1) % 2 == 0
        other = jnp.where(even, pltpu.roll(rotary, 127, 1), pltpu.roll(rotary, 1, 1))
        cosine, sine = turns[h]
        rotary = rotary.reshape(8, 16, 128) * cosine[None] + other.reshape(8, 16, 128) * sine[None]
        move = MOVE[2, 0:128, 0:128]
        absorbed = jnp.dot(move, QR[h, :, :, 0:KVL].reshape(128, KVL), preferred_element_type=f32)
        rotary = jnp.dot(move, rotary.reshape(128, 128).astype(bf), preferred_element_type=f32)
        for n in range(2):
            one, two = slice(64 * n, 64 * n + 32), slice(64 * n + 32, 64 * n + 64)
            G[2 * h + n, gi, :, 0:KVL] = absorbed[one].astype(bf)
            G[2 * h + n, gi, :, KVL : 2 * KVL] = absorbed[two].astype(bf)
            both = jnp.where(lane[0:32] < ROPE, rotary[one], pltpu.roll(rotary[two], ROPE, 1))
            G[2 * h + n, gi, :, 2 * KVL :] = both.astype(bf)
        return absorbed.astype(bf), rotary.astype(bf)

    def new_scores(h, absorbed, rotary):
        query = lax.broadcasted_iota(jnp.int32, (128, 32), 0)
        key = lax.broadcasted_iota(jnp.int32, (128, 32), 1)
        live = (key % 8 == 4 * h + query // 32) & (key // 8 <= query % 4)
        score = lax.dot_general(absorbed, NEW[:, 0:KVL], nt, preferred_element_type=f32)
        score = score + lax.dot_general(
            rotary[:, 0:ROPE], NEW[:, KVL:WIDTH], nt, preferred_element_type=f32
        )
        SN[pl.ds(128 * h, 128)] = jnp.where(live, score * to_log2, -1e30)

    def gather(h):
        A, B, every, upper, lower = 2 * h, 2 * h + 1, slice(0, 32), slice(0, 16), slice(16, 32)
        s_l, s_r, s_z = p_xm, p_xp, p_z
        s_lz, s_rz, s_f, s_fz = at(xm, zo, c), at(xp, zo, c), p_x2, at(x2, zo, c)

        def go(pair, slot, peer, group=None, part=every):
            block = G.at[pair, slot, part]
            return net.send(block, block, peer, group=group)

        mate, far, far_a, far_b = net.group(), net.group(), net.group(), net.group()

        def share(span, slot):
            go(span, slot, p_c, mate)

        z_a = go(A, gi, p_z)
        l_b, r_b = go(B, gi, p_xp), go(B, gi, p_xm)
        l_a, r_a = go(A, gi, p_xp), go(A, gi, p_xm)
        share(pl.ds(2 * h, 2), gi)
        z_b = go(B, gi, p_z)
        yield
        z_a.wait_recv()
        lz_a, rz_a = go(A, s_z, p_xp), go(A, s_z, p_xm)
        share(A, s_z)
        l_b.wait_recv()
        f0_b, lz_b = go(B, s_l, p_xp, part=upper), go(B, s_l, p_z)
        share(B, s_l)
        r_b.wait_recv()
        f1_b, rz_b = go(B, s_r, p_xm, part=lower), go(B, s_r, p_z)
        share(B, s_r)
        l_a.wait_recv()
        go(A, s_l, p_xp, far, upper)
        share(A, s_l)
        r_a.wait_recv()
        go(A, s_r, p_xm, far, lower)
        share(A, s_r)
        yield
        lz_a.wait_recv()
        go(A, s_lz, p_xp, far_a, upper)
        share(A, s_lz)
        rz_a.wait_recv()
        go(A, s_rz, p_xm, far_a, lower)
        share(A, s_rz)
        f0_b.wait_recv()
        go(B, s_f, p_z, far_b, upper)
        f1_b.wait_recv()
        go(B, s_f, p_z, far_b, lower)
        share(B, s_f)
        net.arrive(far, G.at[0, 0])
        share(A, s_f)
        yield
        z_b.wait_recv()
        share(B, s_z)
        lz_b.wait_recv()
        share(B, s_lz)
        rz_b.wait_recv()
        share(B, s_rz)
        net.arrive(far_a, G.at[0, 0])
        share(A, s_fz)
        net.arrive(far_b, G.at[0, 0])
        share(B, s_fz)
        yield
        net.arrive(mate, G.at[pl.ds(2 * h, 2), 0:8])
        yield

    lanes = lax.broadcasted_iota(jnp.int32, (512, 128), 1)
    key_at = lax.broadcasted_iota(jnp.int32, (1, 512), 1) + gi * 512
    own_rows = pl.ds(gi * 32, 32)

    def score_pair(pair, carry):
        turned = G[pair, :, :, 2 * KVL :].reshape(512, 2 * ROPE)
        for n in range(2):
            r = 2 * pair + n
            plain = G[pair, :, :, KVL * n : KVL * (n + 1)].reshape(512, KVL)
            s = jnp.dot(plain, K[r, 0:KVL], preferred_element_type=f32)
            s = (s + jnp.dot(turned, KR[r], preferred_element_type=f32)) * to_log2
            s = jnp.where(key_at < len_ref[r], s, -1e30)
            S[r % 4] = s
            peak = jnp.maximum(jnp.max(s, 1, keepdims=True), -1e29)
            M[r] = jnp.broadcast_to(peak, (512, 128))
            M[r, own_rows, :] = jnp.maximum(
                M[r, own_rows, :], jnp.max(SN[pl.ds(r * 32, 32), :], 1, keepdims=True)
            )
            ml_send[r // 4, 0, pl.ds(r % 4, 1), :] = jnp.transpose(M[r])[0:1]
        return carry

    def value_one(r, carry):
        p = jnp.exp2(S[r % 4] - M[r, :, 0:1])
        pn = jnp.exp2(SN[pl.ds(r * 32, 32), :] - M[r, own_rows, 0:1])
        L[...] = jnp.broadcast_to(jnp.sum(p, 1, keepdims=True), (512, 128))
        L[own_rows, :] = L[own_rows, :] + jnp.sum(pn, 1, keepdims=True)
        O[r] = lax.dot_general(p.astype(bf), K[r, 0:KVL], nt, preferred_element_type=f32)
        O[r, own_rows, :] = O[r, own_rows, :] + jnp.dot(
            pn.astype(bf), NEW[:, :KVL], preferred_element_type=f32
        )
        sums[pl.ds(r, 1), :] = jnp.transpose(L[...])[0:1]
        return carry

    def score(first, count):
        lax.fori_loop(first // 2, (first + count) // 2, score_pair, 0)

    def value(first, count):
        lax.fori_loop(first, first + count, value_one, 0)

    def butterfly(n, join):
        copy = net.send(ml_send.at[n, 0], ml_recv.at[n, 0], p_c)
        yield
        copy.wait_recv()
        total = join(ml_send[n, 0], ml_recv[n, 0])
        ml_send[n, 1] = total
        others = net.group()
        for j in range(1, 8):
            peer = (gi + 2 * j) % 16
            net.send(ml_send.at[n, 1], ml_recv.at[n, j], peer, group=others)
        yield
        net.arrive(others, ml_recv.at[n, 1:8])
        for j in range(1, 8):
            total = join(total, ml_recv[n, j])
        ml_send[n, 2] = total

    def peaks(h):
        yield from butterfly(h, jnp.maximum)
        factor = jnp.exp2(ml_send[h, 0] - ml_send[h, 2])
        sums[4 * h : 4 * h + 4] = sums[4 * h : 4 * h + 4] * factor[0:4]
        SC[0:8] = factor
        SCT[h] = jnp.transpose(SC[...])
        yield

    def totals():
        ml_send[2, 0] = sums[...]
        yield from butterfly(2, jnp.add)
        SC[0:8] = ml_send[2, 2]
        SCT[2] = jnp.transpose(SC[...])
        yield

    def total_of(*terms):
        total = terms[0].astype(f32)
        for term in terms[1:]:
            total = total + term.astype(f32)
        return total

    def add(*terms):
        return total_of(*terms).astype(bf)

    def reduce(h):
        b = 4 * h
        A, B = pl.ds(b, 2), pl.ds(b + 2, 2)
        near_a, near_b = net.group(), net.group()
        mate = {}
        for first in (b + 2, b):
            for r in (first, first + 1):
                part = (O[r] * SCT[h, :, r - b : r - b + 1]).astype(bf)
                NB[r] = part.reshape(4, 2, 2, 32, KVL)
            span = pl.ds(first, 2)
            mate[first] = net.send(NB.at[span, :, :, co], RD.at[span], p_c)
        yield
        mate[b + 2].wait_recv()
        for r in (b + 2, b + 3):
            T[r] = add(NB[r, :, :, c], RD[r])
        over = [net.send(T.at[B, xx, zo], RZB.at[h, :, xx], p_z) for xx in (x2, xp, xm, x)]
        mate[b].wait_recv()
        for r in (b, b + 1):
            T[r] = add(NB[r, :, :, c], RD[r])
        f0 = net.send(T.at[b, x2], RFA.at[h, 0], p_xp)
        f1 = net.send(T.at[b + 1, x2], RFA.at[h, 1], p_xm)
        net.send(T.at[b + 1, xp], RLA.at[h, 1], p_xp, group=near_a)
        net.send(T.at[b, xm], RRA.at[h, 0], p_xm, group=near_a)
        yield
        over[0].wait_recv()
        V[h, :, x2] = add(T[B, x2, zl], RZB[h, :, x2])
        g0 = net.send(V.at[h, 0, x2], RFB.at[h, 0], p_xp)
        g1 = net.send(V.at[h, 1, x2], RFB.at[h, 1], p_xm)
        f0.wait_recv()
        T[b, xp] = add(T[b, xp], RFA[h, 0])
        net.send(T.at[b, xp], RLA.at[h, 0], p_xp, group=near_a)
        f1.wait_recv()
        T[b + 1, xm] = add(T[b + 1, xm], RFA[h, 1])
        net.send(T.at[b + 1, xm], RRA.at[h, 1], p_xm, group=near_a)
        yield
        over[1].wait_recv()
        V[h, :, xp] = add(T[B, xp, zl], RZB[h, :, xp])
        net.send(V.at[h, 1, xp], RLB.at[h, 1], p_xp, group=near_b)
        over[2].wait_recv()
        V[h, :, xm] = add(T[B, xm, zl], RZB[h, :, xm])
        net.send(V.at[h, 0, xm], RRB.at[h, 0], p_xm, group=near_b)
        g0.wait_recv()
        V[h, 0, xp] = add(V[h, 0, xp], RFB[h, 0])
        net.send(V.at[h, 0, xp], RLB.at[h, 0], p_xp, group=near_b)
        g1.wait_recv()
        V[h, 1, xm] = add(V[h, 1, xm], RFB[h, 1])
        net.send(V.at[h, 1, xm], RRB.at[h, 1], p_xm, group=near_b)
        yield
        net.arrive(near_a, RLA)
        for n in range(2):
            U[h, n] = add(T[b + n, x], RLA[h, n], RRA[h, n])
        z_a = net.send(U.at[h, :, zo], RZA.at[h], p_z)
        over[3].wait_recv()
        V[h, :, x] = add(T[B, x, zl], RZB[h, :, x])
        yield
        z_a.wait_recv()
        F[A] = total_of(U[h, :, zl], RZA[h])
        net.arrive(near_b, RLB)
        F[B] = total_of(V[h, :, x], RLB[h], RRB[h])
        yield

    def values():
        partner = (di + 4) % 8
        around = [(di // 4) * 4 + (di + j) % 4 for j in range(1, 4)]
        mine = net.group()
        for p in around:
            net.send(WV.at[di], WV.at[di], p, "dp", mine)
        yield
        over = net.send(WV.at[di], WV.at[di], partner, "dp")
        yield
        over.wait_recv()
        for p in around:
            net.send(WV.at[partner], WV.at[partner], p, "dp", mine)
        yield
        net.arrive(mine, WV.at[0:6])
        yield

    gather0, gather1 = gather(0), gather(1)
    peaks0, peaks1 = peaks(0), peaks(1)
    reduce0, reduce1 = reduce(0), reduce(1)
    weights, sum_up = values(), totals()
    queries0 = place(0)
    next(gather0)
    queries1 = place(1)
    new_scores(0, *queries0)
    new_scores(1, *queries1)
    next(weights)
    next(gather0)
    next(gather0)
    next(gather1)
    next(weights)
    next(gather0)
    next(gather0)
    score(0, 4)
    next(peaks0)
    next(gather1)
    value(0, 2)
    next(peaks0)
    value(2, 2)
    next(gather1)
    next(weights)
    next(peaks0)
    next(reduce0)
    next(gather1)
    next(reduce0)
    next(gather1)
    score(4, 4)
    next(peaks1)
    value(4, 2)
    next(peaks1)
    next(reduce0)
    value(6, 2)
    next(reduce0)
    next(peaks1)
    next(reduce1)
    next(sum_up)
    next(reduce0)
    next(sum_up)
    next(reduce1)
    next(reduce0)
    next(reduce1)
    next(sum_up)
    next(reduce1)
    next(reduce1)
    next(weights)
    next(reduce1)

    for r in range(8):
        F[r] = F[r] / SCT[2, own_rows, r : r + 1]
    latent = jnp.dot(
        MOVE[3], F[...].astype(bf).reshape(256, KVL), preferred_element_type=f32
    ).astype(bf)
    for i in range(8):
        out_ref[:, i * VDIM : (i + 1) * VDIM] = jnp.dot(
            latent[i * 32 : (i + 1) * 32], WV[i], preferred_element_type=f32
        ).astype(bf)
    net.finish()
    pltpu.make_async_copy(X.at[0:127], X.at[0:127], all_send).wait()


def per_device(query_latent, q_up, kv_up, latent_cache, new_latent, lengths):
    bf, f32 = jnp.bfloat16, jnp.float32
    pair = np.arange(128) // 2
    freq = np.where(pair < ROPE // 2, 10000.0 ** (-(2.0 * pair) / ROPE), 0.0).astype(np.float32)
    vmem = pl.BlockSpec(memory_space=pltpu.VMEM)
    out = pl.pallas_call(
        kernel,
        out_shape=jax.ShapeDtypeStruct((32, 8 * VDIM), bf),
        in_specs=[pl.BlockSpec(memory_space=pltpu.SMEM), vmem] + [pl.BlockSpec(memory_space=pl.ANY)] * 5,
        out_specs=vmem,
        scratch_shapes=[
            pltpu.VMEM((12, H * (NOPE + ROPE)), bf),
            pltpu.VMEM((4, H * (NOPE + VDIM)), bf),
            pltpu.VMEM((32, WIDTH), bf),
            pltpu.VMEM((4, 256, 256), bf),
            pltpu.VMEM((256, 32), f32),
            pltpu.VMEM((128, 32, 128), bf),
            pltpu.VMEM((128, 32, 128), bf),
            pltpu.VMEM((8, 32, QL), bf),
            pltpu.VMEM((2, QL, 128), bf),
            pltpu.VMEM((KVL, NOPE), bf),
            pltpu.VMEM((8, 32, WIDE), bf),
            pltpu.VMEM((2, 8, 16, WIDE), bf),
            pltpu.VMEM((8, KVL, VDIM), bf),
            pltpu.VMEM((4, 16, 32, 2 * WIDTH), bf),
            pltpu.VMEM((8, WIDTH, 512), bf),
            pltpu.VMEM((8, 2 * ROPE, 512), bf),
            pltpu.VMEM((8, 512, KVL), f32),
            pltpu.VMEM((8, 4, 2, 2, 32, KVL), bf),
            pltpu.VMEM((8, 4, 2, 32, KVL), bf),
            pltpu.VMEM((8, 4, 2, 32, KVL), bf),
            pltpu.VMEM((2, 2, 4, 32, KVL), bf),
            pltpu.VMEM((2, 2, 2, 32, KVL), bf),
            pltpu.VMEM((2, 2, 2, 32, KVL), bf),
            pltpu.VMEM((2, 2, 2, 32, KVL), bf),
            pltpu.VMEM((2, 2, 2, 32, KVL), bf),
            pltpu.VMEM((2, 2, 32, KVL), bf),
            pltpu.VMEM((2, 2, 32, KVL), bf),
            pltpu.VMEM((2, 2, 32, KVL), bf),
            pltpu.VMEM((2, 2, 32, KVL), bf),
            pltpu.VMEM((2, 2, 4, 32, KVL), bf),
            pltpu.VMEM((4, 512, 512), f32),
            pltpu.VMEM((8, 512, 128), f32),
            pltpu.VMEM((512, 128), f32),
            pltpu.VMEM((8, 512), f32),
            pltpu.VMEM((3, 3, 8, 512), f32),
            pltpu.VMEM((3, 8, 8, 512), f32),
            pltpu.VMEM((128, 512), f32),
            pltpu.VMEM((3, 512, 128), f32),
            pltpu.VMEM((8, 32, KVL), f32),
            pltpu.SemaphoreType.DMA((POOL,)),
            pltpu.SemaphoreType.DMA((GROUPS,)),
            pltpu.SemaphoreType.DMA((5,)),
            pltpu.SemaphoreType.DMA,
            pltpu.SemaphoreType.DMA,
        ],
        compiler_params=pltpu.CompilerParams(
            collective_id=1, has_side_effects=True, vmem_limit_bytes=60 * 1024 * 1024
        ),
    )(
        lengths, jnp.asarray(freq)[None], query_latent.reshape(32, QL), q_up, kv_up,
        latent_cache.transpose(0, 2, 1), new_latent.reshape(32, WIDTH),
    )
    return out.reshape(STEPS, 8, 8 * VDIM)


def solution(mesh):
    return jax.shard_map(
        per_device,
        mesh=mesh,
        in_specs=(
            P(None, "dp", None),
            P(("dp", "grp"), None),
            P(("dp", "grp"), None),
            P("dp", "grp", None),
            P(None, "dp", None),
            P("dp"),
        ),
        out_specs=P(None, "dp", "grp"),
        check_vma=False,
    )
```

```python
import jax
import jax.numpy as jnp
import numpy as np
from jax import lax
from jax.experimental import pallas as pl
from jax.experimental.pallas import tpu as pltpu
from jax.sharding import PartitionSpec as P

MESH = pl.DeviceIdType.MESH

H = 128
QL = 1536
KVL = 512
NOPE = 128
ROPE = 64
VDIM = 128
STEPS = 4
WIDTH = KVL + ROPE
WIDE = KVL + 128
LOG2E = 1.4426950408889634
POOL = 40
GROUPS = 70


class Copies:
    def __init__(self, send_sem, recv_sem):
        self.send_sem, self.recv_sem, self.sent, self.groups = send_sem, recv_sem, [], 0

    def group(self):
        self.groups += 1
        assert self.groups <= GROUPS
        return self.groups - 1

    def send(self, src, dst, peer, axis="grp", group=None):
        k = len(self.sent)
        if k >= POOL:
            self.sent[k - POOL].wait_send()
        copy = pltpu.make_async_remote_copy(
            src_ref=src,
            dst_ref=dst,
            send_sem=self.send_sem.at[k % POOL],
            recv_sem=self.recv_sem.at[self.group() if group is None else group],
            device_id={axis: peer},
            device_id_type=MESH,
        )
        copy.start()
        self.sent.append(copy)
        return copy

    def arrive(self, group, like):
        pltpu.make_async_copy(like, like, self.recv_sem.at[group]).wait()

    def finish(self):
        for copy in self.sent[-POOL:]:
            copy.wait_send()


def kernel(
    len_ref, freq_ref, ql_ref, q_ref, kv_ref, cache_ref, new_ref, out_ref,
    QIN, KVIN, NEW, MOVE, SN, X, LAND, QLS, W, KC, E, QR, WV,
    G, K, KR, O, NB, RD, T, V, U, RFA, RLA, RRA, RZA, RFB, RLB, RRB, RZB, S, M, L, sums, ml_send, ml_recv, SC, SCT, F,
    send_sem, recv_sem, load_sem, all_send, all_recv,
):
    di, gi = lax.axis_index("dp"), lax.axis_index("grp")
    me = di * 16 + gi
    x, zl, c = gi // 4, (gi // 2) % 2, gi % 2
    xp, xm, x2 = (x + 1) % 4, (x + 3) % 4, (x + 2) % 4
    zo, co = 1 - zl, 1 - c

    def at(xx, zz, cc):
        return xx * 4 + zz * 2 + cc

    p_xp, p_xm, p_x2 = at(xp, zl, c), at(xm, zl, c), at(x2, zl, c)
    p_z, p_c = at(x, zo, c), at(x, zl, co)

    loads = [
        pltpu.make_async_copy(src, dst, load_sem.at[n])
        for n, (src, dst) in enumerate(
            ((q_ref, QIN), (kv_ref, KVIN), (ql_ref, QLS.at[0]), (new_ref, NEW), (cache_ref, K))
        )
    ]
    for load in loads:
        load.start()
    barrier = pltpu.get_barrier_semaphore()

    def there(j):
        d = (me + 37 * j) % 128
        return d // 16, d % 16

    def six(one):
        def body(n, carry):
            for j in range(6):
                one(6 * n + j + 1)
            return carry

        lax.fori_loop(0, 21, body, 0)
        one(127)

    def greet(j):
        dd, gg = there(j)
        pl.semaphore_signal(
            barrier, inc=1, device_id={"dp": dd, "grp": gg}, device_id_type=MESH
        )

    six(greet)
    bf, f32 = jnp.bfloat16, jnp.float32
    nt = (((1,), (1,)), ((), ()))

    loads[0].wait()
    loads[1].wait()

    def pack(p, carry):
        def tiles(upper, lower):
            a = QIN[:, pl.ds(pl.multiple_of(upper * 128, 128), 128)]
            b = KVIN[:, pl.ds(pl.multiple_of(lower * 128, 128), 128)]
            return jnp.concatenate([a, b], 0)

        X[2 * p, 0:16] = tiles(3 * p, 4 * p)
        X[2 * p, 16:32] = tiles(3 * p + 1, 4 * p + 1)
        X[2 * p + 1, 0:16] = tiles(3 * p + 1, 4 * p + 2)
        X[2 * p + 1, 16:32] = tiles(3 * p + 2, 4 * p + 3)
        return carry

    lax.fori_loop(0, 64, pack, 0)
    LAND[me] = X[8 * gi + di]
    loads[2].wait()
    pl.semaphore_wait(barrier, 127)

    net = Copies(send_sem, recv_sem)
    rows = pl.ds(pl.multiple_of(c * 16, 16), 16)
    first = net.group()
    for j in range(1, 8):
        net.send(QLS.at[0, rows], QLS.at[8 - j, rows], (di + j) % 8, "dp", first)

    def deal(j):
        dd, gg = there(j)
        pltpu.make_async_remote_copy(
            src_ref=X.at[8 * gg + dd],
            dst_ref=LAND.at[me],
            send_sem=all_send,
            recv_sem=all_recv,
            device_id={"dp": dd, "grp": gg},
            device_id_type=MESH,
        ).start()

    six(deal)

    to = lax.broadcasted_iota(jnp.int32, (256, 256), 0)
    was = lax.broadcasted_iota(jnp.int32, (256, 256), 1)
    within = jnp.where(to < 96, to, to - 96)
    twelve = jnp.where(to < 96, to, to - 80)
    for n in range(1, 8):
        twelve = twelve + jnp.where(within >= 12 * n, 20, 0)
    four = 32 * ((to % 32) // 4) + to % 4 + jnp.where(to < 224, 12, 28)
    half = to - to % 32 + ((to % 16) // 4) * 8 + ((to % 32) // 16) * 4 + to % 4
    MOVE[0] = (was == jnp.where(to < 192, twelve, four)).astype(f32).astype(bf)
    MOVE[1] = (was == half).astype(f32).astype(bf)
    MOVE[2] = (was == ((to // 4) % 8) * 16 + (to % 4) * 4 + to // 32).astype(f32).astype(bf)
    MOVE[3] = (was == (to % 8) * 32 + to // 8).astype(f32).astype(bf)
    loads[4].wait()
    for r in range(8):
        KR[r, ROPE * (r % 2) : ROPE * (r % 2) + ROPE] = K[r, KVL:WIDTH]
        KR[r, ROPE * (1 - r % 2) : ROPE * (1 - r % 2) + ROPE] = jnp.zeros((ROPE, 512), bf)
    SC[...] = jnp.zeros_like(SC)
    ml_send[...] = jnp.zeros_like(ml_send)

    row = lax.broadcasted_iota(jnp.int32, (16, 128), 0)
    sign = jnp.where(lax.broadcasted_iota(jnp.int32, (16, 128), 1) % 2 == 0, -1.0, 1.0)
    turns = []
    for h in range(2):
        position = row // 4
        for r in range(4):
            position = position + jnp.where(row % 4 == r, len_ref[4 * h + r], 0)
        angle = position.astype(f32) * freq_ref[...]
        turns.append((jnp.cos(angle), sign * jnp.sin(angle)))

    net.arrive(first, QLS.at[1:8, rows])
    net.send(QLS.at[1:8, rows], QLS.at[1:8, rows], p_c).wait_recv()
    pltpu.make_async_copy(LAND.at[0:127], LAND.at[0:127], all_recv).wait()

    for b in range(16):
        block = jnp.dot(
            MOVE[0], LAND[8 * b : 8 * b + 8].reshape(256, 128), preferred_element_type=f32
        ).astype(bf)
        W[0, 96 * b : 96 * b + 96] = block[0:96]
        W[1, 96 * b : 96 * b + 96] = block[96:192]
        KC[32 * b : 32 * b + 32] = block[192:224]
        WV[di, 32 * b : 32 * b + 32] = block[224:256]
    latent_in = QLS[...].reshape(256, QL)
    qa = jnp.dot(latent_in, W[0], preferred_element_type=f32).astype(bf)
    qb = jnp.dot(latent_in, W[1], preferred_element_type=f32).astype(bf)
    qa = jnp.dot(MOVE[1], qa, preferred_element_type=f32)
    qb = jnp.dot(MOVE[1], qb, preferred_element_type=f32)
    ra, rb = pltpu.roll(qa, 64, 1), pltpu.roll(qb, 64, 1)
    lane = lax.broadcasted_iota(jnp.int32, (256, 128), 1)
    odd = di % 2 == 1
    plain = jnp.where(odd, jnp.where(lane < 64, ra, rb), qa).astype(bf)
    rotary = jnp.where(lane < 64, jnp.where(odd, rb, qb), 0.0).astype(bf)
    absorbed = lax.dot_general(plain, KC[...], nt, preferred_element_type=f32).astype(bf)
    E[:, :, 0:KVL] = absorbed.reshape(8, 32, KVL)
    E[:, :, KVL:WIDE] = rotary.reshape(8, 32, 128)
    heads = []
    for h in range(2):
        span = pl.ds(16 * h, 16)
        heads.append(net.group())
        for j in range(1, 8):
            net.send(E.at[j, span], QR.at[h, di], (di + j) % 8, "dp", heads[h])
        QR[h, di] = E[0, span]
    loads[3].wait()
    to_log2 = float(NOPE + ROPE) ** -0.5 * LOG2E

    def place(h):
        net.arrive(heads[h], QR.at[h, 0:7])
        span = pl.ds(4 * h, 4)
        rotary = QR[h, :, :, KVL:WIDE].reshape(128, 128).astype(f32)
        even = lax.broadcasted_iota(jnp.int32, (128, 128), 1) % 2 == 0
        other = jnp.where(even, pltpu.roll(rotary, 127, 1), pltpu.roll(rotary, 1, 1))
        cosine, sine = turns[h]
        rotary = rotary.reshape(8, 16, 128) * cosine[None] + other.reshape(8, 16, 128) * sine[None]
        move = MOVE[2, 0:128, 0:128]
        absorbed = jnp.dot(move, QR[h, :, :, 0:KVL].reshape(128, KVL), preferred_element_type=f32)
        rotary = jnp.dot(move, rotary.reshape(128, 128).astype(bf), preferred_element_type=f32)
        for n in range(2):
            one, two = slice(64 * n, 64 * n + 32), slice(64 * n + 32, 64 * n + 64)
            G[2 * h + n, gi, :, 0:KVL] = absorbed[one].astype(bf)
            G[2 * h + n, gi, :, KVL : 2 * KVL] = absorbed[two].astype(bf)
            both = jnp.where(lane[0:32] < ROPE, rotary[one], pltpu.roll(rotary[two], ROPE, 1))
            G[2 * h + n, gi, :, 2 * KVL :] = both.astype(bf)
        return absorbed.astype(bf), rotary.astype(bf)

    def new_scores(h, absorbed, rotary):
        query = lax.broadcasted_iota(jnp.int32, (128, 32), 0)
        key = lax.broadcasted_iota(jnp.int32, (128, 32), 1)
        live = (key % 8 == 4 * h + query // 32) & (key // 8 <= query % 4)
        score = lax.dot_general(absorbed, NEW[:, 0:KVL], nt, preferred_element_type=f32)
        score = score + lax.dot_general(
            rotary[:, 0:ROPE], NEW[:, KVL:WIDTH], nt, preferred_element_type=f32
        )
        SN[pl.ds(128 * h, 128)] = jnp.where(live, score * to_log2, -1e30)

    def gather(h):
        A, B, every, upper, lower = 2 * h, 2 * h + 1, slice(0, 32), slice(0, 16), slice(16, 32)
        s_l, s_r, s_z = p_xm, p_xp, p_z
        s_lz, s_rz, s_f, s_fz = at(xm, zo, c), at(xp, zo, c), p_x2, at(x2, zo, c)

        def go(pair, slot, peer, group=None, part=every):
            block = G.at[pair, slot, part]
            return net.send(block, block, peer, group=group)

        mate, far, far_a, far_b = net.group(), net.group(), net.group(), net.group()

        def share(span, slot):
            go(span, slot, p_c, mate)

        z_a = go(A, gi, p_z)
        l_b, r_b = go(B, gi, p_xp), go(B, gi, p_xm)
        l_a, r_a = go(A, gi, p_xp), go(A, gi, p_xm)
        share(pl.ds(2 * h, 2), gi)
        z_b = go(B, gi, p_z)
        yield
        z_a.wait_recv()
        lz_a, rz_a = go(A, s_z, p_xp), go(A, s_z, p_xm)
        share(A, s_z)
        l_b.wait_recv()
        f0_b, lz_b = go(B, s_l, p_xp, part=upper), go(B, s_l, p_z)
        share(B, s_l)
        r_b.wait_recv()
        f1_b, rz_b = go(B, s_r, p_xm, part=lower), go(B, s_r, p_z)
        share(B, s_r)
        l_a.wait_recv()
        go(A, s_l, p_xp, far, upper)
        share(A, s_l)
        r_a.wait_recv()
        go(A, s_r, p_xm, far, lower)
        share(A, s_r)
        yield
        lz_a.wait_recv()
        go(A, s_lz, p_xp, far_a, upper)
        share(A, s_lz)
        rz_a.wait_recv()
        go(A, s_rz, p_xm, far_a, lower)
        share(A, s_rz)
        f0_b.wait_recv()
        go(B, s_f, p_z, far_b, upper)
        f1_b.wait_recv()
        go(B, s_f, p_z, far_b, lower)
        share(B, s_f)
        net.arrive(far, G.at[0, 0])
        share(A, s_f)
        yield
        z_b.wait_recv()
        share(B, s_z)
        lz_b.wait_recv()
        share(B, s_lz)
        rz_b.wait_recv()
        share(B, s_rz)
        net.arrive(far_a, G.at[0, 0])
        share(A, s_fz)
        net.arrive(far_b, G.at[0, 0])
        share(B, s_fz)
        yield
        net.arrive(mate, G.at[pl.ds(2 * h, 2), 0:8])
        yield

    lanes = lax.broadcasted_iota(jnp.int32, (512, 128), 1)
    key_at = lax.broadcasted_iota(jnp.int32, (1, 512), 1) + gi * 512
    own_rows = pl.ds(gi * 32, 32)

    def score_pair(pair, carry):
        turned = G[pair, :, :, 2 * KVL :].reshape(512, 2 * ROPE)
        for n in range(2):
            r = 2 * pair + n
            plain = G[pair, :, :, KVL * n : KVL * (n + 1)].reshape(512, KVL)
            s = jnp.dot(plain, K[r, 0:KVL], preferred_element_type=f32)
            s = (s + jnp.dot(turned, KR[r], preferred_element_type=f32)) * to_log2
            s = jnp.where(key_at < len_ref[r], s, -1e30)
            S[r % 4] = s
            peak = jnp.maximum(jnp.max(s, 1, keepdims=True), -1e29)
            M[r] = jnp.broadcast_to(peak, (512, 128))
            M[r, own_rows, :] = jnp.maximum(
                M[r, own_rows, :], jnp.max(SN[pl.ds(r * 32, 32), :], 1, keepdims=True)
            )
            ml_send[r // 4, 0, pl.ds(r % 4, 1), :] = jnp.transpose(M[r])[0:1]
        return carry

    def value_one(r, carry):
        p = jnp.exp2(S[r % 4] - M[r, :, 0:1])
        pn = jnp.exp2(SN[pl.ds(r * 32, 32), :] - M[r, own_rows, 0:1])
        L[...] = jnp.broadcast_to(jnp.sum(p, 1, keepdims=True), (512, 128))
        L[own_rows, :] = L[own_rows, :] + jnp.sum(pn, 1, keepdims=True)
        O[r] = lax.dot_general(p.astype(bf), K[r, 0:KVL], nt, preferred_element_type=f32)
        O[r, own_rows, :] = O[r, own_rows, :] + jnp.dot(
            pn.astype(bf), NEW[:, :KVL], preferred_element_type=f32
        )
        sums[pl.ds(r, 1), :] = jnp.transpose(L[...])[0:1]
        return carry

    def score(first, count):
        lax.fori_loop(first // 2, (first + count) // 2, score_pair, 0)

    def value(first, count):
        lax.fori_loop(first, first + count, value_one, 0)

    def butterfly(n, join):
        copy = net.send(ml_send.at[n, 0], ml_recv.at[n, 0], p_c)
        yield
        copy.wait_recv()
        total = join(ml_send[n, 0], ml_recv[n, 0])
        ml_send[n, 1] = total
        others = net.group()
        for j in range(1, 8):
            peer = (gi + 2 * j) % 16
            net.send(ml_send.at[n, 1], ml_recv.at[n, j], peer, group=others)
        yield
        net.arrive(others, ml_recv.at[n, 1:8])
        for j in range(1, 8):
            total = join(total, ml_recv[n, j])
        ml_send[n, 2] = total

    def peaks(h):
        yield from butterfly(h, jnp.maximum)
        factor = jnp.exp2(ml_send[h, 0] - ml_send[h, 2])
        sums[4 * h : 4 * h + 4] = sums[4 * h : 4 * h + 4] * factor[0:4]
        SC[0:8] = factor
        SCT[h] = jnp.transpose(SC[...])
        yield

    def totals():
        ml_send[2, 0] = sums[...]
        yield from butterfly(2, jnp.add)
        SC[0:8] = ml_send[2, 2]
        SCT[2] = jnp.transpose(SC[...])
        yield

    def total_of(*terms):
        total = terms[0].astype(f32)
        for term in terms[1:]:
            total = total + term.astype(f32)
        return total

    def add(*terms):
        return total_of(*terms).astype(bf)

    def reduce(h):
        b = 4 * h
        A, B = pl.ds(b, 2), pl.ds(b + 2, 2)
        near_a, near_b = net.group(), net.group()
        mate = {}
        for first in (b + 2, b):
            for r in (first, first + 1):
                part = (O[r] * SCT[h, :, r - b : r - b + 1]).astype(bf)
                NB[r] = part.reshape(4, 2, 2, 32, KVL)
            span = pl.ds(first, 2)
            mate[first] = net.send(NB.at[span, :, :, co], RD.at[span], p_c)
        yield
        mate[b + 2].wait_recv()
        for r in (b + 2, b + 3):
            T[r] = add(NB[r, :, :, c], RD[r])
        over = [net.send(T.at[B, xx, zo], RZB.at[h, :, xx], p_z) for xx in (x2, xp, xm, x)]
        mate[b].wait_recv()
        for r in (b, b + 1):
            T[r] = add(NB[r, :, :, c], RD[r])
        f0 = net.send(T.at[b, x2], RFA.at[h, 0], p_xp)
        f1 = net.send(T.at[b + 1, x2], RFA.at[h, 1], p_xm)
        net.send(T.at[b + 1, xp], RLA.at[h, 1], p_xp, group=near_a)
        net.send(T.at[b, xm], RRA.at[h, 0], p_xm, group=near_a)
        yield
        over[0].wait_recv()
        V[h, :, x2] = add(T[B, x2, zl], RZB[h, :, x2])
        g0 = net.send(V.at[h, 0, x2], RFB.at[h, 0], p_xp)
        g1 = net.send(V.at[h, 1, x2], RFB.at[h, 1], p_xm)
        f0.wait_recv()
        T[b, xp] = add(T[b, xp], RFA[h, 0])
        net.send(T.at[b, xp], RLA.at[h, 0], p_xp, group=near_a)
        f1.wait_recv()
        T[b + 1, xm] = add(T[b + 1, xm], RFA[h, 1])
        net.send(T.at[b + 1, xm], RRA.at[h, 1], p_xm, group=near_a)
        yield
        over[1].wait_recv()
        V[h, :, xp] = add(T[B, xp, zl], RZB[h, :, xp])
        net.send(V.at[h, 1, xp], RLB.at[h, 1], p_xp, group=near_b)
        over[2].wait_recv()
        V[h, :, xm] = add(T[B, xm, zl], RZB[h, :, xm])
        net.send(V.at[h, 0, xm], RRB.at[h, 0], p_xm, group=near_b)
        g0.wait_recv()
        V[h, 0, xp] = add(V[h, 0, xp], RFB[h, 0])
        net.send(V.at[h, 0, xp], RLB.at[h, 0], p_xp, group=near_b)
        g1.wait_recv()
        V[h, 1, xm] = add(V[h, 1, xm], RFB[h, 1])
        net.send(V.at[h, 1, xm], RRB.at[h, 1], p_xm, group=near_b)
        yield
        net.arrive(near_a, RLA)
        for n in range(2):
            U[h, n] = add(T[b + n, x], RLA[h, n], RRA[h, n])
        z_a = net.send(U.at[h, :, zo], RZA.at[h], p_z)
        over[3].wait_recv()
        V[h, :, x] = add(T[B, x, zl], RZB[h, :, x])
        yield
        z_a.wait_recv()
        F[A] = total_of(U[h, :, zl], RZA[h])
        net.arrive(near_b, RLB)
        F[B] = total_of(V[h, :, x], RLB[h], RRB[h])
        yield

    def values():
        partner = (di + 4) % 8
        around = [(di // 4) * 4 + (di + j) % 4 for j in range(1, 4)]
        mine = net.group()
        for p in around:
            net.send(WV.at[di], WV.at[di], p, "dp", mine)
        yield
        over = net.send(WV.at[di], WV.at[di], partner, "dp")
        yield
        over.wait_recv()
        for p in around:
            net.send(WV.at[partner], WV.at[partner], p, "dp", mine)
        yield
        net.arrive(mine, WV.at[0:6])
        yield

    gather0, gather1 = gather(0), gather(1)
    peaks0, peaks1 = peaks(0), peaks(1)
    reduce0, reduce1 = reduce(0), reduce(1)
    weights, sum_up = values(), totals()
    queries0 = place(0)
    next(gather0)
    queries1 = place(1)
    new_scores(0, *queries0)
    new_scores(1, *queries1)
    next(weights)
    next(gather0)
    next(gather0)
    next(gather1)
    next(weights)
    next(gather0)
    next(gather0)
    score(0, 4)
    next(peaks0)
    next(gather1)
    value(0, 2)
    next(peaks0)
    value(2, 2)
    next(gather1)
    next(weights)
    next(peaks0)
    next(reduce0)
    next(gather1)
    next(reduce0)
    next(gather1)
    score(4, 4)
    next(peaks1)
    value(4, 2)
    next(peaks1)
    next(reduce0)
    value(6, 2)
    next(reduce0)
    next(peaks1)
    next(reduce1)
    next(sum_up)
    next(reduce0)
    next(sum_up)
    next(reduce1)
    next(reduce0)
    next(reduce1)
    next(sum_up)
    next(reduce1)
    next(reduce1)
    next(weights)
    next(reduce1)

    for r in range(8):
        F[r] = F[r] / SCT[2, own_rows, r : r + 1]
    latent = jnp.dot(
        MOVE[3], F[...].astype(bf).reshape(256, KVL), preferred_element_type=f32
    ).astype(bf)
    for i in range(8):
        out_ref[:, i * VDIM : (i + 1) * VDIM] = jnp.dot(
            latent[i * 32 : (i + 1) * 32], WV[i], preferred_element_type=f32
        ).astype(bf)
    net.finish()
    pltpu.make_async_copy(X.at[0:127], X.at[0:127], all_send).wait()


def per_device(query_latent, q_up, kv_up, latent_cache, new_latent, lengths):
    bf, f32 = jnp.bfloat16, jnp.float32
    pair = np.arange(128) // 2
    freq = np.where(pair < ROPE // 2, 10000.0 ** (-(2.0 * pair) / ROPE), 0.0).astype(np.float32)
    vmem = pl.BlockSpec(memory_space=pltpu.VMEM)
    out = pl.pallas_call(
        kernel,
        out_shape=jax.ShapeDtypeStruct((32, 8 * VDIM), bf),
        in_specs=[pl.BlockSpec(memory_space=pltpu.SMEM), vmem] + [pl.BlockSpec(memory_space=pl.ANY)] * 5,
        out_specs=vmem,
        scratch_shapes=[
            pltpu.VMEM((12, H * (NOPE + ROPE)), bf),
            pltpu.VMEM((4, H * (NOPE + VDIM)), bf),
            pltpu.VMEM((32, WIDTH), bf),
            pltpu.VMEM((4, 256, 256), bf),
            pltpu.VMEM((256, 32), f32),
            pltpu.VMEM((128, 32, 128), bf),
            pltpu.VMEM((128, 32, 128), bf),
            pltpu.VMEM((8, 32, QL), bf),
            pltpu.VMEM((2, QL, 128), bf),
            pltpu.VMEM((KVL, NOPE), bf),
            pltpu.VMEM((8, 32, WIDE), bf),
            pltpu.VMEM((2, 8, 16, WIDE), bf),
            pltpu.VMEM((8, KVL, VDIM), bf),
            pltpu.VMEM((4, 16, 32, 2 * WIDTH), bf),
            pltpu.VMEM((8, WIDTH, 512), bf),
            pltpu.VMEM((8, 2 * ROPE, 512), bf),
            pltpu.VMEM((8, 512, KVL), f32),
            pltpu.VMEM((8, 4, 2, 2, 32, KVL), bf),
            pltpu.VMEM((8, 4, 2, 32, KVL), bf),
            pltpu.VMEM((8, 4, 2, 32, KVL), bf),
            pltpu.VMEM((2, 2, 4, 32, KVL), bf),
            pltpu.VMEM((2, 2, 2, 32, KVL), bf),
            pltpu.VMEM((2, 2, 2, 32, KVL), bf),
            pltpu.VMEM((2, 2, 2, 32, KVL), bf),
            pltpu.VMEM((2, 2, 2, 32, KVL), bf),
            pltpu.VMEM((2, 2, 32, KVL), bf),
            pltpu.VMEM((2, 2, 32, KVL), bf),
            pltpu.VMEM((2, 2, 32, KVL), bf),
            pltpu.VMEM((2, 2, 32, KVL), bf),
            pltpu.VMEM((2, 2, 4, 32, KVL), bf),
            pltpu.VMEM((4, 512, 512), f32),
            pltpu.VMEM((8, 512, 128), f32),
            pltpu.VMEM((512, 128), f32),
            pltpu.VMEM((8, 512), f32),
            pltpu.VMEM((3, 3, 8, 512), f32),
            pltpu.VMEM((3, 8, 8, 512), f32),
            pltpu.VMEM((128, 512), f32),
            pltpu.VMEM((3, 512, 128), f32),
            pltpu.VMEM((8, 32, KVL), f32),
            pltpu.SemaphoreType.DMA((POOL,)),
            pltpu.SemaphoreType.DMA((GROUPS,)),
            pltpu.SemaphoreType.DMA((5,)),
            pltpu.SemaphoreType.DMA,
            pltpu.SemaphoreType.DMA,
        ],
        compiler_params=pltpu.CompilerParams(
            collective_id=1, has_side_effects=True, vmem_limit_bytes=60 * 1024 * 1024
        ),
    )(
        lengths, jnp.asarray(freq)[None], query_latent.reshape(32, QL), q_up, kv_up,
        latent_cache.transpose(0, 2, 1), new_latent.reshape(32, WIDTH),
    )
    return out.reshape(STEPS, 8, 8 * VDIM)


def solution(mesh):
    return jax.shard_map(
        per_device,
        mesh=mesh,
        in_specs=(
            P(None, "dp", None),
            P(("dp", "grp"), None),
            P(("dp", "grp"), None),
            P("dp", "grp", None),
            P(None, "dp", None),
            P("dp"),
        ),
        out_specs=P(None, "dp", "grp"),
        check_vma=False,
    )
```

```python
import jax
import jax.numpy as jnp
import numpy as np
from jax import lax
from jax.experimental import pallas as pl
from jax.experimental.pallas import tpu as pltpu
from jax.sharding import PartitionSpec as P

MESH = pl.DeviceIdType.MESH

H = 128
QL = 1536
KVL = 512
NOPE = 128
ROPE = 64
VDIM = 128
STEPS = 4
WIDTH = KVL + ROPE
WIDE = KVL + 128
LOG2E = 1.4426950408889634
POOL = 40
FAR_FIRST = (2, 6, 1, 3, 5, 7, 4)
GROUPS = 72


class Copies:
    def __init__(self, send_sem, recv_sem):
        self.send_sem, self.recv_sem, self.sent, self.groups = send_sem, recv_sem, [], 0

    def group(self):
        self.groups += 1
        assert self.groups <= GROUPS
        return self.groups - 1

    def send(self, src, dst, peer, axis="grp", group=None):
        k = len(self.sent)
        if k >= POOL:
            self.sent[k - POOL].wait_send()
        copy = pltpu.make_async_remote_copy(
            src_ref=src,
            dst_ref=dst,
            send_sem=self.send_sem.at[k % POOL],
            recv_sem=self.recv_sem.at[self.group() if group is None else group],
            device_id={axis: peer},
            device_id_type=MESH,
        )
        copy.start()
        self.sent.append(copy)
        return copy

    def arrive(self, group, like):
        pltpu.make_async_copy(like, like, self.recv_sem.at[group]).wait()

    def finish(self):
        for copy in self.sent[-POOL:]:
            copy.wait_send()


def kernel(
    len_ref, freq_ref, ql_ref, q_ref, kv_ref, cache_ref, new_ref, out_ref,
    QIN, KVIN, NEW, MOVE, SN, X, LAND, QLS, W, KC, E, QR, WV,
    G, K, KR, O, NB, RD, T, V, U, RFA, RLA, RRA, RZA, RFB, RLB, RRB, RZB, S, M, L, sums, ml_send, ml_recv, SC, SCT, F,
    send_sem, recv_sem, load_sem, all_send, all_recv,
):
    di, gi = lax.axis_index("dp"), lax.axis_index("grp")
    me = di * 16 + gi
    x, zl, c = gi // 4, (gi // 2) % 2, gi % 2
    xp, xm, x2 = (x + 1) % 4, (x + 3) % 4, (x + 2) % 4
    zo, co = 1 - zl, 1 - c

    def at(xx, zz, cc):
        return xx * 4 + zz * 2 + cc

    p_xp, p_xm, p_x2 = at(xp, zl, c), at(xm, zl, c), at(x2, zl, c)
    p_z, p_c = at(x, zo, c), at(x, zl, co)

    loads = [
        pltpu.make_async_copy(src, dst, load_sem.at[n])
        for n, (src, dst) in enumerate(
            ((q_ref, QIN), (kv_ref, KVIN), (ql_ref, QLS.at[0]), (new_ref, NEW), (cache_ref, K))
        )
    ]
    for load in loads:
        load.start()
    barrier = pltpu.get_barrier_semaphore()

    def there(j):
        d = (me + 37 * j) % 128
        return d // 16, d % 16

    def six(one):
        def body(n, carry):
            for j in range(6):
                one(6 * n + j + 1)
            return carry

        lax.fori_loop(0, 21, body, 0)
        one(127)

    def greet(j):
        dd, gg = there(j)
        pl.semaphore_signal(
            barrier, inc=1, device_id={"dp": dd, "grp": gg}, device_id_type=MESH
        )

    six(greet)
    bf, f32 = jnp.bfloat16, jnp.float32
    nt = (((1,), (1,)), ((), ()))

    loads[0].wait()
    loads[1].wait()

    def pack(p, carry):
        def tiles(upper, lower):
            a = QIN[:, pl.ds(pl.multiple_of(upper * 128, 128), 128)]
            b = KVIN[:, pl.ds(pl.multiple_of(lower * 128, 128), 128)]
            return jnp.concatenate([a, b], 0)

        X[2 * p, 0:16] = tiles(3 * p, 4 * p)
        X[2 * p, 16:32] = tiles(3 * p + 1, 4 * p + 1)
        X[2 * p + 1, 0:16] = tiles(3 * p + 1, 4 * p + 2)
        X[2 * p + 1, 16:32] = tiles(3 * p + 2, 4 * p + 3)
        return carry

    lax.fori_loop(0, 64, pack, 0)
    LAND[me] = X[8 * gi + di]
    loads[2].wait()
    pl.semaphore_wait(barrier, 127)

    net = Copies(send_sem, recv_sem)
    rows = pl.ds(pl.multiple_of(c * 16, 16), 16)
    first = net.group()
    for j in FAR_FIRST:
        net.send(QLS.at[0, rows], QLS.at[8 - j, rows], (di + j) % 8, "dp", first)

    def deal(j):
        dd, gg = there(j)
        pltpu.make_async_remote_copy(
            src_ref=X.at[8 * gg + dd],
            dst_ref=LAND.at[me],
            send_sem=all_send,
            recv_sem=all_recv,
            device_id={"dp": dd, "grp": gg},
            device_id_type=MESH,
        ).start()

    six(deal)

    to = lax.broadcasted_iota(jnp.int32, (256, 256), 0)
    was = lax.broadcasted_iota(jnp.int32, (256, 256), 1)
    within = jnp.where(to < 96, to, to - 96)
    twelve = jnp.where(to < 96, to, to - 80)
    for n in range(1, 8):
        twelve = twelve + jnp.where(within >= 12 * n, 20, 0)
    four = 32 * ((to % 32) // 4) + to % 4 + jnp.where(to < 224, 12, 28)
    half = to - to % 32 + ((to % 16) // 4) * 8 + ((to % 32) // 16) * 4 + to % 4
    MOVE[0] = (was == jnp.where(to < 192, twelve, four)).astype(f32).astype(bf)
    MOVE[1] = (was == half).astype(f32).astype(bf)
    MOVE[2] = (was == ((to // 4) % 8) * 16 + (to % 4) * 4 + to // 32).astype(f32).astype(bf)
    MOVE[3] = (was == (to % 8) * 32 + to // 8).astype(f32).astype(bf)
    loads[4].wait()
    for r in range(8):
        KR[r, ROPE * (r % 2) : ROPE * (r % 2) + ROPE] = K[r, KVL:WIDTH]
        KR[r, ROPE * (1 - r % 2) : ROPE * (1 - r % 2) + ROPE] = jnp.zeros((ROPE, 512), bf)
    SC[...] = jnp.zeros_like(SC)
    ml_send[...] = jnp.zeros_like(ml_send)

    row = lax.broadcasted_iota(jnp.int32, (16, 128), 0)
    sign = jnp.where(lax.broadcasted_iota(jnp.int32, (16, 128), 1) % 2 == 0, -1.0, 1.0)
    turns = []
    for h in range(2):
        position = row // 4
        for r in range(4):
            position = position + jnp.where(row % 4 == r, len_ref[4 * h + r], 0)
        angle = position.astype(f32) * freq_ref[...]
        turns.append((jnp.cos(angle), sign * jnp.sin(angle)))

    net.arrive(first, QLS.at[1:8, rows])
    net.send(QLS.at[1:8, rows], QLS.at[1:8, rows], p_c).wait_recv()
    pltpu.make_async_copy(LAND.at[0:127], LAND.at[0:127], all_recv).wait()

    for b in range(16):
        block = jnp.dot(
            MOVE[0], LAND[8 * b : 8 * b + 8].reshape(256, 128), preferred_element_type=f32
        ).astype(bf)
        W[0, 96 * b : 96 * b + 96] = block[0:96]
        W[1, 96 * b : 96 * b + 96] = block[96:192]
        KC[32 * b : 32 * b + 32] = block[192:224]
        WV[di, 32 * b : 32 * b + 32] = block[224:256]
    latent_in = QLS[...].reshape(256, QL)
    qa = jnp.dot(latent_in, W[0], preferred_element_type=f32).astype(bf)
    qb = jnp.dot(latent_in, W[1], preferred_element_type=f32).astype(bf)
    qa = jnp.dot(MOVE[1], qa, preferred_element_type=f32)
    qb = jnp.dot(MOVE[1], qb, preferred_element_type=f32)
    ra, rb = pltpu.roll(qa, 64, 1), pltpu.roll(qb, 64, 1)
    lane = lax.broadcasted_iota(jnp.int32, (256, 128), 1)
    odd = di % 2 == 1
    plain = jnp.where(odd, jnp.where(lane < 64, ra, rb), qa).astype(bf)
    rotary = jnp.where(lane < 64, jnp.where(odd, rb, qb), 0.0).astype(bf)
    absorbed = lax.dot_general(plain, KC[...], nt, preferred_element_type=f32).astype(bf)
    E[:, :, 0:KVL] = absorbed.reshape(8, 32, KVL)
    E[:, :, KVL:WIDE] = rotary.reshape(8, 32, 128)
    heads = []
    for h in range(2):
        span = pl.ds(16 * h, 16)
        heads.append(net.group())
        for j in FAR_FIRST:
            net.send(E.at[j, span], QR.at[h, di], (di + j) % 8, "dp", heads[h])
        QR[h, di] = E[0, span]
    loads[3].wait()
    to_log2 = float(NOPE + ROPE) ** -0.5 * LOG2E

    def place(h):
        net.arrive(heads[h], QR.at[h, 0:7])
        span = pl.ds(4 * h, 4)
        rotary = QR[h, :, :, KVL:WIDE].reshape(128, 128).astype(f32)
        even = lax.broadcasted_iota(jnp.int32, (128, 128), 1) % 2 == 0
        other = jnp.where(even, pltpu.roll(rotary, 127, 1), pltpu.roll(rotary, 1, 1))
        cosine, sine = turns[h]
        rotary = rotary.reshape(8, 16, 128) * cosine[None] + other.reshape(8, 16, 128) * sine[None]
        move = MOVE[2, 0:128, 0:128]
        absorbed = jnp.dot(move, QR[h, :, :, 0:KVL].reshape(128, KVL), preferred_element_type=f32)
        rotary = jnp.dot(move, rotary.reshape(128, 128).astype(bf), preferred_element_type=f32)
        for n in range(2):
            one, two = slice(64 * n, 64 * n + 32), slice(64 * n + 32, 64 * n + 64)
            G[2 * h + n, gi, :, 0:KVL] = absorbed[one].astype(bf)
            G[2 * h + n, gi, :, KVL : 2 * KVL] = absorbed[two].astype(bf)
            both = jnp.where(lane[0:32] < ROPE, rotary[one], pltpu.roll(rotary[two], ROPE, 1))
            G[2 * h + n, gi, :, 2 * KVL :] = both.astype(bf)
        return absorbed.astype(bf), rotary.astype(bf)

    def new_scores(h, absorbed, rotary):
        query = lax.broadcasted_iota(jnp.int32, (128, 32), 0)
        key = lax.broadcasted_iota(jnp.int32, (128, 32), 1)
        live = (key % 8 == 4 * h + query // 32) & (key // 8 <= query % 4)
        score = lax.dot_general(absorbed, NEW[:, 0:KVL], nt, preferred_element_type=f32)
        score = score + lax.dot_general(
            rotary[:, 0:ROPE], NEW[:, KVL:WIDTH], nt, preferred_element_type=f32
        )
        SN[pl.ds(128 * h, 128)] = jnp.where(live, score * to_log2, -1e30)

    def gather(h):
        A, B, every, upper, lower = 2 * h, 2 * h + 1, slice(0, 32), slice(0, 16), slice(16, 32)
        s_l, s_r, s_z = p_xm, p_xp, p_z
        s_lz, s_rz, s_f, s_fz = at(xm, zo, c), at(xp, zo, c), p_x2, at(x2, zo, c)

        def go(pair, slot, peer, group=None, part=every):
            block = G.at[pair, slot, part]
            return net.send(block, block, peer, group=group)

        mate, far, far_a, far_b = {}, net.group(), net.group(), net.group()
        for pair in (A, B):
            mate[pair] = net.group()

        def share(span, slot):
            go(span, slot, p_c, mate[span])

        z_a = go(A, gi, p_z)
        l_b, r_b = go(B, gi, p_xp), go(B, gi, p_xm)
        l_a, r_a = go(A, gi, p_xp), go(A, gi, p_xm)
        share(A, gi)
        share(B, gi)
        z_b = go(B, gi, p_z)
        yield
        z_a.wait_recv()
        lz_a, rz_a = go(A, s_z, p_xp), go(A, s_z, p_xm)
        share(A, s_z)
        l_b.wait_recv()
        f0_b, lz_b = go(B, s_l, p_xp, part=upper), go(B, s_l, p_z)
        share(B, s_l)
        r_b.wait_recv()
        f1_b, rz_b = go(B, s_r, p_xm, part=lower), go(B, s_r, p_z)
        share(B, s_r)
        l_a.wait_recv()
        go(A, s_l, p_xp, far, upper)
        share(A, s_l)
        r_a.wait_recv()
        go(A, s_r, p_xm, far, lower)
        share(A, s_r)
        yield
        lz_a.wait_recv()
        go(A, s_lz, p_xp, far_a, upper)
        share(A, s_lz)
        rz_a.wait_recv()
        go(A, s_rz, p_xm, far_a, lower)
        share(A, s_rz)
        f0_b.wait_recv()
        go(B, s_f, p_z, far_b, upper)
        f1_b.wait_recv()
        go(B, s_f, p_z, far_b, lower)
        share(B, s_f)
        net.arrive(far, G.at[0, 0])
        share(A, s_f)
        yield
        net.arrive(far_a, G.at[0, 0])
        share(A, s_fz)
        z_b.wait_recv()
        share(B, s_z)
        yield
        net.arrive(mate[A], G.at[A, 0:8])
        yield
        lz_b.wait_recv()
        share(B, s_lz)
        rz_b.wait_recv()
        share(B, s_rz)
        net.arrive(far_b, G.at[0, 0])
        share(B, s_fz)
        yield
        net.arrive(mate[B], G.at[B, 0:8])
        yield

    lanes = lax.broadcasted_iota(jnp.int32, (512, 128), 1)
    key_at = lax.broadcasted_iota(jnp.int32, (1, 512), 1) + gi * 512
    own_rows = pl.ds(gi * 32, 32)

    def score_pair(pair, carry):
        turned = G[pair, :, :, 2 * KVL :].reshape(512, 2 * ROPE)
        for n in range(2):
            r = 2 * pair + n
            plain = G[pair, :, :, KVL * n : KVL * (n + 1)].reshape(512, KVL)
            s = jnp.dot(plain, K[r, 0:KVL], preferred_element_type=f32)
            s = (s + jnp.dot(turned, KR[r], preferred_element_type=f32)) * to_log2
            s = jnp.where(key_at < len_ref[r], s, -1e30)
            S[r % 4] = s
            peak = jnp.maximum(jnp.max(s, 1, keepdims=True), -1e29)
            M[r] = jnp.broadcast_to(peak, (512, 128))
            M[r, own_rows, :] = jnp.maximum(
                M[r, own_rows, :], jnp.max(SN[pl.ds(r * 32, 32), :], 1, keepdims=True)
            )
            ml_send[r // 4, 0, pl.ds(r % 4, 1), :] = jnp.transpose(M[r])[0:1]
        return carry

    def value_one(r, carry):
        p = jnp.exp2(S[r % 4] - M[r, :, 0:1])
        pn = jnp.exp2(SN[pl.ds(r * 32, 32), :] - M[r, own_rows, 0:1])
        L[...] = jnp.broadcast_to(jnp.sum(p, 1, keepdims=True), (512, 128))
        L[own_rows, :] = L[own_rows, :] + jnp.sum(pn, 1, keepdims=True)
        O[r] = lax.dot_general(p.astype(bf), K[r, 0:KVL], nt, preferred_element_type=f32)
        O[r, own_rows, :] = O[r, own_rows, :] + jnp.dot(
            pn.astype(bf), NEW[:, :KVL], preferred_element_type=f32
        )
        sums[pl.ds(r, 1), :] = jnp.transpose(L[...])[0:1]
        return carry

    def score(first, count):
        lax.fori_loop(first // 2, (first + count) // 2, score_pair, 0)

    def value(first, count):
        lax.fori_loop(first, first + count, value_one, 0)

    def butterfly(n, join):
        copy = net.send(ml_send.at[n, 0], ml_recv.at[n, 0], p_c)
        yield
        copy.wait_recv()
        total = join(ml_send[n, 0], ml_recv[n, 0])
        ml_send[n, 1] = total
        others = net.group()
        for j in range(1, 8):
            peer = (gi + 2 * j) % 16
            net.send(ml_send.at[n, 1], ml_recv.at[n, j], peer, group=others)
        yield
        net.arrive(others, ml_recv.at[n, 1:8])
        for j in range(1, 8):
            total = join(total, ml_recv[n, j])
        ml_send[n, 2] = total

    def peaks(h):
        yield from butterfly(h, jnp.maximum)
        factor = jnp.exp2(ml_send[h, 0] - ml_send[h, 2])
        sums[4 * h : 4 * h + 4] = sums[4 * h : 4 * h + 4] * factor[0:4]
        SC[0:8] = factor
        SCT[h] = jnp.transpose(SC[...])
        yield

    def totals():
        ml_send[2, 0] = sums[...]
        yield from butterfly(2, jnp.add)
        SC[0:8] = ml_send[2, 2]
        SCT[2] = jnp.transpose(SC[...])
        yield

    def total_of(*terms):
        total = terms[0].astype(f32)
        for term in terms[1:]:
            total = total + term.astype(f32)
        return total

    def add(*terms):
        if len(terms) == 2:
            return terms[0] + terms[1]
        return total_of(*terms).astype(bf)

    def reduce(h):
        b = 4 * h
        A, B = pl.ds(b, 2), pl.ds(b + 2, 2)
        near_a, near_b = net.group(), net.group()
        mate = {}
        for first in (b + 2, b):
            for r in (first, first + 1):
                part = (O[r] * SCT[h, :, r - b : r - b + 1]).astype(bf)
                NB[r] = part.reshape(4, 2, 2, 32, KVL)
            span = pl.ds(first, 2)
            mate[first] = net.send(NB.at[span, :, :, co], RD.at[span], p_c)
        yield
        mate[b + 2].wait_recv()
        for r in (b + 2, b + 3):
            T[r] = add(NB[r, :, :, c], RD[r])
        over = [net.send(T.at[B, xx, zo], RZB.at[h, :, xx], p_z) for xx in (x2, xp, xm, x)]
        mate[b].wait_recv()
        for r in (b, b + 1):
            T[r] = add(NB[r, :, :, c], RD[r])
        f0 = net.send(T.at[b, x2], RFA.at[h, 0], p_xp)
        f1 = net.send(T.at[b + 1, x2], RFA.at[h, 1], p_xm)
        net.send(T.at[b + 1, xp], RLA.at[h, 1], p_xp, group=near_a)
        net.send(T.at[b, xm], RRA.at[h, 0], p_xm, group=near_a)
        yield
        over[0].wait_recv()
        V[h, :, x2] = add(T[B, x2, zl], RZB[h, :, x2])
        g0 = net.send(V.at[h, 0, x2], RFB.at[h, 0], p_xp)
        g1 = net.send(V.at[h, 1, x2], RFB.at[h, 1], p_xm)
        f0.wait_recv()
        T[b, xp] = add(T[b, xp], RFA[h, 0])
        net.send(T.at[b, xp], RLA.at[h, 0], p_xp, group=near_a)
        f1.wait_recv()
        T[b + 1, xm] = add(T[b + 1, xm], RFA[h, 1])
        net.send(T.at[b + 1, xm], RRA.at[h, 1], p_xm, group=near_a)
        yield
        over[1].wait_recv()
        V[h, :, xp] = add(T[B, xp, zl], RZB[h, :, xp])
        net.send(V.at[h, 1, xp], RLB.at[h, 1], p_xp, group=near_b)
        over[2].wait_recv()
        V[h, :, xm] = add(T[B, xm, zl], RZB[h, :, xm])
        net.send(V.at[h, 0, xm], RRB.at[h, 0], p_xm, group=near_b)
        g0.wait_recv()
        V[h, 0, xp] = add(V[h, 0, xp], RFB[h, 0])
        net.send(V.at[h, 0, xp], RLB.at[h, 0], p_xp, group=near_b)
        g1.wait_recv()
        V[h, 1, xm] = add(V[h, 1, xm], RFB[h, 1])
        net.send(V.at[h, 1, xm], RRB.at[h, 1], p_xm, group=near_b)
        yield
        net.arrive(near_a, RLA)
        for n in range(2):
            U[h, n] = add(T[b + n, x], RLA[h, n], RRA[h, n])
        z_a = net.send(U.at[h, :, zo], RZA.at[h], p_z)
        over[3].wait_recv()
        V[h, :, x] = add(T[B, x, zl], RZB[h, :, x])
        yield
        z_a.wait_recv()
        F[A] = total_of(U[h, :, zl], RZA[h])
        net.arrive(near_b, RLB)
        F[B] = total_of(V[h, :, x], RLB[h], RRB[h])
        yield

    def values():
        partner = (di + 4) % 8
        around = [(di // 4) * 4 + (di + j) % 4 for j in range(1, 4)]
        mine = net.group()
        for p in around:
            net.send(WV.at[di], WV.at[di], p, "dp", mine)
        yield
        over = net.send(WV.at[di], WV.at[di], partner, "dp")
        yield
        over.wait_recv()
        for p in around:
            net.send(WV.at[partner], WV.at[partner], p, "dp", mine)
        yield
        net.arrive(mine, WV.at[0:6])
        yield

    gather0, gather1 = gather(0), gather(1)
    peaks0, peaks1 = peaks(0), peaks(1)
    reduce0, reduce1 = reduce(0), reduce(1)
    weights, sum_up = values(), totals()
    queries0 = place(0)
    next(gather0)
    queries1 = place(1)
    new_scores(0, *queries0)
    new_scores(1, *queries1)
    next(weights)
    next(gather0)
    next(gather0)
    next(gather1)
    next(weights)
    next(gather0)
    next(gather0)
    next(gather0)
    score(0, 2)
    next(gather0)
    score(2, 2)
    next(peaks0)
    next(gather1)
    value(0, 2)
    next(peaks0)
    value(2, 2)
    next(gather1)
    next(weights)
    next(peaks0)
    next(reduce0)
    next(gather1)
    next(reduce0)
    next(gather1)
    next(gather1)
    score(4, 2)
    next(gather1)
    score(6, 2)
    next(peaks1)
    value(4, 2)
    next(peaks1)
    next(reduce0)
    value(6, 2)
    next(reduce0)
    next(peaks1)
    next(reduce1)
    next(sum_up)
    next(reduce0)
    next(sum_up)
    next(reduce1)
    next(reduce0)
    next(reduce1)
    next(sum_up)
    next(reduce1)
    next(reduce1)
    next(weights)
    next(reduce1)

    for r in range(8):
        F[r] = F[r] / SCT[2, own_rows, r : r + 1]
    latent = jnp.dot(
        MOVE[3], F[...].astype(bf).reshape(256, KVL), preferred_element_type=f32
    ).astype(bf)
    for i in range(8):
        out_ref[:, i * VDIM : (i + 1) * VDIM] = jnp.dot(
            latent[i * 32 : (i + 1) * 32], WV[i], preferred_element_type=f32
        ).astype(bf)
    net.finish()
    pltpu.make_async_copy(X.at[0:127], X.at[0:127], all_send).wait()


def per_device(query_latent, q_up, kv_up, latent_cache, new_latent, lengths):
    bf, f32 = jnp.bfloat16, jnp.float32
    pair = np.arange(128) // 2
    freq = np.where(pair < ROPE // 2, 10000.0 ** (-(2.0 * pair) / ROPE), 0.0).astype(np.float32)
    vmem = pl.BlockSpec(memory_space=pltpu.VMEM)
    out = pl.pallas_call(
        kernel,
        out_shape=jax.ShapeDtypeStruct((32, 8 * VDIM), bf),
        in_specs=[pl.BlockSpec(memory_space=pltpu.SMEM), vmem] + [pl.BlockSpec(memory_space=pl.ANY)] * 5,
        out_specs=vmem,
        scratch_shapes=[
            pltpu.VMEM((12, H * (NOPE + ROPE)), bf),
            pltpu.VMEM((4, H * (NOPE + VDIM)), bf),
            pltpu.VMEM((32, WIDTH), bf),
            pltpu.VMEM((4, 256, 256), bf),
            pltpu.VMEM((256, 32), f32),
            pltpu.VMEM((128, 32, 128), bf),
            pltpu.VMEM((128, 32, 128), bf),
            pltpu.VMEM((8, 32, QL), bf),
            pltpu.VMEM((2, QL, 128), bf),
            pltpu.VMEM((KVL, NOPE), bf),
            pltpu.VMEM((8, 32, WIDE), bf),
            pltpu.VMEM((2, 8, 16, WIDE), bf),
            pltpu.VMEM((8, KVL, VDIM), bf),
            pltpu.VMEM((4, 16, 32, 2 * WIDTH), bf),
            pltpu.VMEM((8, WIDTH, 512), bf),
            pltpu.VMEM((8, 2 * ROPE, 512), bf),
            pltpu.VMEM((8, 512, KVL), f32),
            pltpu.VMEM((8, 4, 2, 2, 32, KVL), bf),
            pltpu.VMEM((8, 4, 2, 32, KVL), bf),
            pltpu.VMEM((8, 4, 2, 32, KVL), bf),
            pltpu.VMEM((2, 2, 4, 32, KVL), bf),
            pltpu.VMEM((2, 2, 2, 32, KVL), bf),
            pltpu.VMEM((2, 2, 2, 32, KVL), bf),
            pltpu.VMEM((2, 2, 2, 32, KVL), bf),
            pltpu.VMEM((2, 2, 2, 32, KVL), bf),
            pltpu.VMEM((2, 2, 32, KVL), bf),
            pltpu.VMEM((2, 2, 32, KVL), bf),
            pltpu.VMEM((2, 2, 32, KVL), bf),
            pltpu.VMEM((2, 2, 32, KVL), bf),
            pltpu.VMEM((2, 2, 4, 32, KVL), bf),
            pltpu.VMEM((4, 512, 512), f32),
            pltpu.VMEM((8, 512, 128), f32),
            pltpu.VMEM((512, 128), f32),
            pltpu.VMEM((8, 512), f32),
            pltpu.VMEM((3, 3, 8, 512), f32),
            pltpu.VMEM((3, 8, 8, 512), f32),
            pltpu.VMEM((128, 512), f32),
            pltpu.VMEM((3, 512, 128), f32),
            pltpu.VMEM((8, 32, KVL), f32),
            pltpu.SemaphoreType.DMA((POOL,)),
            pltpu.SemaphoreType.DMA((GROUPS,)),
            pltpu.SemaphoreType.DMA((5,)),
            pltpu.SemaphoreType.DMA,
            pltpu.SemaphoreType.DMA,
        ],
        compiler_params=pltpu.CompilerParams(
            collective_id=1, has_side_effects=True, vmem_limit_bytes=60 * 1024 * 1024
        ),
    )(
        lengths, jnp.asarray(freq)[None], query_latent.reshape(32, QL), q_up, kv_up,
        latent_cache.transpose(0, 2, 1), new_latent.reshape(32, WIDTH),
    )
    return out.reshape(STEPS, 8, 8 * VDIM)


def solution(mesh):
    return jax.shard_map(
        per_device,
        mesh=mesh,
        in_specs=(
            P(None, "dp", None),
            P(("dp", "grp"), None),
            P(("dp", "grp"), None),
            P("dp", "grp", None),
            P(None, "dp", None),
            P("dp"),
        ),
        out_specs=P(None, "dp", "grp"),
        check_vma=False,
    )
```
